32 devices in a mesh: dp: 16 (over z, y, core), fsdp: 2 (over x).
Axes of the slice: x: 2, y: 2, z: 4, core: 2. Of those that a mesh axis runs over, the one named last changes fastest.
Arguments:
- inputs: bfloat16 [16, 1024, 2048], P('dp', 'fsdp'), may hold values from -6 to 6
- cotangent: bfloat16 [16, 1024, 2048], P('dp', 'fsdp'), may hold values from -30 to 30
- segments: int32 [16, 1024], P('dp'), may hold values from 0 to 2, as said below
- w_query: float32 [2048, 2048], P(None, ('dp', 'fsdp')), may hold values from -0.125 to 0.125
- key_weight_master: float32 [2048, 1024], P(('dp', 'fsdp')), may hold values from -0.125 to 0.125
- value_weight_master: float32 [2048, 1024], P(('dp', 'fsdp')), may hold values from -0.125 to 0.125
- w_output: float32 [2048, 2048], P(('dp', 'fsdp')), may hold values from -0.75 to 0.75
- w_gate: float32 [2048, 6144], P(None, ('dp', 'fsdp')), may hold values from -0.125 to 0.125
- w_up: float32 [2048, 6144], P(None, ('dp', 'fsdp')), may hold values from -0.125 to 0.125
- w_down: float32 [6144, 2048], P(('dp', 'fsdp')), may hold values from -0.078125 to 0.078125
- moment_query: float32 [2048, 2048], P(None, ('dp', 'fsdp')), may hold values from -491520 to 491520
- moment_key: float32 [2048, 1024], P(('dp', 'fsdp')), may hold values from -491520 to 491520
- moment_value: float32 [2048, 1024], P(('dp', 'fsdp')), may hold values from -491520 to 491520
- moment_output: float32 [2048, 2048], P(('dp', 'fsdp')), may hold values from -491520 to 491520
- moment_gate: float32 [2048, 6144], P(None, ('dp', 'fsdp')), may hold values from -491520 to 491520
- moment_up: float32 [2048, 6144], P(None, ('dp', 'fsdp')), may hold values from -491520 to 491520
- moment_down: float32 [6144, 2048], P(('dp', 'fsdp')), may hold values from -491520 to 491520
- norm_gains: float32 [4352], replicated, may hold values from 0.5 to 1.5
- gain_first: float32 [4352], replicated, may hold values from -262144 to 262144
- gain_second: float32 [4352], replicated, may hold values from 0 to 262144
Outputs:
- block_out: bfloat16 [16, 1024, 2048], P('dp', 'fsdp')
- input_grad: float32 [16, 1024, 2048], P('dp', 'fsdp')
- grad_query: float32 [2048, 2048], P(None, ('dp', 'fsdp'))
- grad_key: float32 [2048, 1024], P(('dp', 'fsdp'))
- grad_value: float32 [2048, 1024], P(('dp', 'fsdp'))
- grad_output: float32 [2048, 2048], P(('dp', 'fsdp'))
- grad_gate: float32 [2048, 6144], P(None, ('dp', 'fsdp'))
- grad_up: float32 [2048, 6144], P(None, ('dp', 'fsdp'))
- grad_down: float32 [6144, 2048], P(('dp', 'fsdp'))
- moment_query_new: float32 [2048, 2048], P(None, ('dp', 'fsdp'))
- moment_key_new: float32 [2048, 1024], P(('dp', 'fsdp'))
- moment_value_new: float32 [2048, 1024], P(('dp', 'fsdp'))
- moment_output_new: float32 [2048, 2048], P(('dp', 'fsdp'))
- moment_gate_new: float32 [2048, 6144], P(None, ('dp', 'fsdp'))
- moment_up_new: float32 [2048, 6144], P(None, ('dp', 'fsdp'))
- moment_down_new: float32 [6144, 2048], P(('dp', 'fsdp'))
- weight_query_new: float32 [2048, 2048], P(None, ('dp', 'fsdp'))
- weight_key_new: float32 [2048, 1024], P(('dp', 'fsdp'))
- weight_value_new: float32 [2048, 1024], P(('dp', 'fsdp'))
- weight_output_new: float32 [2048, 2048], P(('dp', 'fsdp'))
- weight_gate_new: float32 [2048, 6144], P(None, ('dp', 'fsdp'))
- weight_up_new: float32 [2048, 6144], P(None, ('dp', 'fsdp'))
- weight_down_new: float32 [6144, 2048], P(('dp', 'fsdp'))
- gain_first_new: float32 [4352], replicated
- gain_second_new: float32 [4352], replicated
- gains_new: float32 [4352], replicated
The draws below stay inside these ranges and needn't reach their ends.
Inputs may be any that keep to these rules, and one draw needn't show every extreme that they name: `segments`: along each row segment numbers never fall; every row holds three documents numbered 0, 1, 2; document 1 has exactly 800 tokens and reaches from the tokens of the first device of fsdp to those of the last; documents 0 and 2 have 60 tokens or more, and in every draw some row's document 0 and some row's document 2 have exactly 60.
All inputs are finite; a program needn't handle non-finite values.
Results may differ from the reference program's by a relative error of at most 0.019.
Values may be sent and summed in bfloat16 or wider, within the bound.
No kernel may reach another device: no remote copies, remote signals or barrier semaphores. Data moves between devices by JAX's collectives and lax.ppermute only.
A program may use at most 512 MiB of HBM per device.

```python
import math
import jax
import jax.numpy as jnp
from jax import lax

MODEL_WIDTH = 2048
QUERY_HEADS = 16
KEY_VALUE_HEADS = 8
HEAD_SIZE = 128
FF = 6144
SEQ_LEN = 1024
DOC_MAX = 800
NS_STEPS = 2
ADAM_STEP = 10
DOC_MIN = 60
BATCH = 16
N_DP = 16
N_FSDP = 2


BETA_ONE = 0.9


BETA_TWO = 0.95


def clipped_normal(key, shape):
    return jnp.clip(jax.random.normal(key, shape, jnp.float32), -5.0, 5.0)


def rising(sequence_length, steepness):
    position_idx = jnp.arange(sequence_length)
    outer_rank = (position_idx // (sequence_length // N_DP)).astype(jnp.float32)
    inner_rank = (position_idx // (sequence_length // (N_DP * N_FSDP)) % N_FSDP).astype(jnp.float32)
    outer_factor = 1.0 + (steepness - 1.0) * outer_rank / max(N_DP - 1, 1)
    inner_factor = 1.0 + (steepness - 1.0) * inner_rank / max(N_FSDP - 1, 1)
    return outer_factor * inner_factor / ((1.0 + steepness) / 2.0) ** 2


def momentum_sample(key, rows, cols, along, factor, steepness):
    normal_draw = clipped_normal(key, (rows, cols))
    if along == 1:
        rise_factor = rising(cols, steepness)[None, :]
    else:
        rise_factor = rising(rows, steepness)[:, None]
    return normal_draw * rise_factor * (factor * math.sqrt(BATCH * SEQ_LEN))


def draw_cotangent(key, part):
    key = jax.random.fold_in(key, 5)
    steepness = 3.0
    normal_draw = clipped_normal(key, (BATCH, SEQ_LEN, MODEL_WIDTH))
    along_batch = 1.0 + (steepness - 1.0) * jnp.arange(BATCH, dtype=jnp.float32) / max(BATCH - 1, 1)
    along_seq = 1.0 + (steepness - 1.0) * jnp.arange(SEQ_LEN, dtype=jnp.float32) / max(SEQ_LEN - 1, 1)
    scaled = normal_draw * along_batch[:, None, None] * along_seq[None, :, None]
    return (scaled * (2.0 / ((1.0 + steepness) / 2.0) ** 2)).astype(jnp.bfloat16)


def draw_segments(key, part):
    key = jax.random.fold_in(key, 3)
    block_rows = SEQ_LEN // N_FSDP
    lowest = DOC_MIN
    highest = min(block_rows - 1, SEQ_LEN - DOC_MAX - DOC_MIN)
    offset_key, pick_key, other_key = jax.random.split(key, 3)
    offset = jax.random.randint(offset_key, (BATCH,), lowest, highest + 1)
    low_row = jax.random.randint(pick_key, (), 0, BATCH)
    high_row = (low_row + jax.random.randint(other_key, (), 1, BATCH)) % BATCH
    row_idx = jnp.arange(BATCH, dtype=jnp.int32)
    offset = jnp.where(row_idx == low_row, lowest, jnp.where(row_idx == high_row, highest, offset))
    position_idx = jnp.arange(SEQ_LEN, dtype=jnp.int32)[None, :]
    first_cut = (position_idx >= offset[:, None]).astype(jnp.int32)
    second_cut = (position_idx >= offset[:, None] + DOC_MAX).astype(jnp.int32)
    return first_cut + second_cut


def draw_moment_query(key, part):
    key = jax.random.fold_in(key, 11)
    return momentum_sample(key, MODEL_WIDTH, QUERY_HEADS * HEAD_SIZE, 1, 1.4, 3.0)


def draw_moment_key(key, part):
    key = jax.random.fold_in(key, 12)
    return momentum_sample(key, MODEL_WIDTH, KEY_VALUE_HEADS * HEAD_SIZE, 0, 1.4, 3.0)


def draw_moment_value(key, part):
    key = jax.random.fold_in(key, 13)
    return momentum_sample(key, MODEL_WIDTH, KEY_VALUE_HEADS * HEAD_SIZE, 0, 1.6, 3.0)


def draw_moment_output(key, part):
    key = jax.random.fold_in(key, 14)
    return momentum_sample(key, QUERY_HEADS * HEAD_SIZE, MODEL_WIDTH, 0, 0.25, 3.0)


def draw_moment_gate(key, part):
    key = jax.random.fold_in(key, 15)
    return momentum_sample(key, MODEL_WIDTH, FF, 1, 1.2, 3.0)


def draw_moment_up(key, part):
    key = jax.random.fold_in(key, 16)
    return momentum_sample(key, MODEL_WIDTH, FF, 1, 1.2, 3.0)


def draw_moment_down(key, part):
    key = jax.random.fold_in(key, 17)
    return momentum_sample(key, FF, MODEL_WIDTH, 0, 2.0, 3.0)


def gain_scale():
    gathered_tokens = BATCH * SEQ_LEN
    return jnp.concatenate([jnp.full((MODEL_WIDTH,), 1.2 * math.sqrt(gathered_tokens), jnp.float32), jnp.full((MODEL_WIDTH,), 1.5 * math.sqrt(gathered_tokens), jnp.float32), jnp.full((HEAD_SIZE,), 0.7 * math.sqrt(gathered_tokens * QUERY_HEADS), jnp.float32), jnp.full((HEAD_SIZE,), 0.7 * math.sqrt(gathered_tokens * KEY_VALUE_HEADS), jnp.float32)])


def draw_gain_first(key, part):
    key = jax.random.fold_in(key, 21)
    return clipped_normal(key, (2 * MODEL_WIDTH + 2 * HEAD_SIZE,)) * gain_scale() * ((1.0 - BETA_ONE) / BETA_ONE)


def draw_gain_second(key, part):
    key = jax.random.fold_in(key, 22)
    spread = jnp.exp(jax.random.uniform(key, (2 * MODEL_WIDTH + 2 * HEAD_SIZE,), jnp.float32, 0.0, math.log(4.0)))
    scale_now = gain_scale()
    return spread * scale_now * scale_now * ((1.0 - BETA_TWO) / BETA_TWO)


def block_levels(rng, extent, cuts, least, largest):
    loudness, own = 1.0, jax.random.fold_in(rng, 6)
    for dim, parts in cuts:
        steps = jnp.exp(jax.random.uniform(jax.random.fold_in(own, dim), (parts,), jnp.float32, least / len(cuts), largest / len(cuts)))
        loudness = loudness * jnp.repeat(steps, extent[dim] // parts).reshape([-1 if axis == dim else 1 for axis in range(len(extent))])
    return loudness


def gaussian(own_key, dims, deviation, limit, cuts=(), held_as=jnp.bfloat16):
    level = block_levels(own_key, dims, cuts, -0.22, 0.18) if cuts else 1.0
    values = jax.random.normal(own_key, dims, jnp.float32) * deviation * level
    return jnp.minimum(jnp.maximum(values, -limit), limit).astype(held_as)


def setup_inputs(seed: int = 0) -> dict:
    key_of = jax.random.split(jax.random.key(seed), 21)
    return {
        "inputs": gaussian(key_of[0], (BATCH, SEQ_LEN, MODEL_WIDTH), 1.0, 6.0, ((0, 16), (1, 2))),
        "cotangent": draw_cotangent(jax.random.fold_in(key_of[20], 71), 0),
        "segments": draw_segments(jax.random.fold_in(key_of[20], 71), 0),
        "w_query": gaussian(key_of[3], (MODEL_WIDTH, QUERY_HEADS * HEAD_SIZE), MODEL_WIDTH ** -0.5, 0.125, ((1, 32),), jnp.float32),
        "key_weight_master": gaussian(key_of[4], (MODEL_WIDTH, KEY_VALUE_HEADS * HEAD_SIZE), MODEL_WIDTH ** -0.5, 0.125, ((0, 32),), jnp.float32),
        "value_weight_master": gaussian(key_of[5], (MODEL_WIDTH, KEY_VALUE_HEADS * HEAD_SIZE), MODEL_WIDTH ** -0.5, 0.125, ((0, 32),), jnp.float32),
        "w_output": gaussian(key_of[6], (QUERY_HEADS * HEAD_SIZE, MODEL_WIDTH), (QUERY_HEADS * HEAD_SIZE // 32) ** -0.5, 0.75, ((0, 32),), jnp.float32),
        "w_gate": gaussian(key_of[7], (MODEL_WIDTH, FF), MODEL_WIDTH ** -0.5, 0.125, ((1, 32),), jnp.float32),
        "w_up": gaussian(key_of[8], (MODEL_WIDTH, FF), MODEL_WIDTH ** -0.5, 0.125, ((1, 32),), jnp.float32),
        "w_down": gaussian(key_of[9], (FF, MODEL_WIDTH), FF ** -0.5, 0.078125, ((0, 32),), jnp.float32),
        "moment_query": draw_moment_query(jax.random.fold_in(key_of[20], 71), 0),
        "moment_key": draw_moment_key(jax.random.fold_in(key_of[20], 71), 0),
        "moment_value": draw_moment_value(jax.random.fold_in(key_of[20], 71), 0),
        "moment_output": draw_moment_output(jax.random.fold_in(key_of[20], 71), 0),
        "moment_gate": draw_moment_gate(jax.random.fold_in(key_of[20], 71), 0),
        "moment_up": draw_moment_up(jax.random.fold_in(key_of[20], 71), 0),
        "moment_down": draw_moment_down(jax.random.fold_in(key_of[20], 71), 0),
        "norm_gains": jnp.clip(1.0 + 0.1 * jax.random.normal(key_of[17], (2 * MODEL_WIDTH + 2 * HEAD_SIZE,), jnp.float32), 0.5, 1.5),
        "gain_first": draw_gain_first(jax.random.fold_in(key_of[20], 71), 0),
        "gain_second": draw_gain_second(jax.random.fold_in(key_of[20], 71), 0),
    }


EPS_NORM = 1e-06
THETA = 1000000.0
NEG_FILL = -1e+30
MOMENTUM = 0.95
NS_A = 3.4445
NS_B = -4.775
NS_C = 2.0315
NS_EPS = 1e-07
LR_MUON = 0.2
DECAY_MUON = 0.01
LR_GAIN = 0.5
BETA_ONE = 0.9
BETA_TWO = 0.95
EPS_ADAM = 1e-08
HIGH_PRECISION = lax.Precision.HIGHEST
SIDEWAYS = (True, False, False, False, True, True, False)

@jax.custom_vjp
def low(v):
    return lax.optimization_barrier(v.astype(jnp.bfloat16)).astype(jnp.float32)

@jax.custom_vjp
def low_back(v):
    return v

def low_keep(v):
    return (low(v), None)

def low_pass(kept, grad):
    return (grad,)

def back_keep(v):
    return (v, None)

def back_low(kept, grad):
    return (low(grad),)
low.defvjp(low_keep, low_pass)
low_back.defvjp(back_keep, back_low)

def rms_scale(values, gain):
    return values * lax.rsqrt(lax.optimization_barrier(jnp.mean(values * values, axis=-1, keepdims=True)) + EPS_NORM) * gain

def rope_tables(positions, head_width):
    half_width = head_width // 2
    freq = jnp.exp(-(2.0 * jnp.arange(half_width, dtype=jnp.float32) / head_width) * math.log(THETA))
    angle = positions.astype(jnp.float32)[:, None] * freq[None, :]
    angle = jnp.concatenate([angle, angle], axis=-1)
    return (jnp.cos(angle)[:, None, :], jnp.sin(angle)[:, None, :])

def rotate(values, cosine_table, sine_table):
    half_width = values.shape[-1] // 2
    turned = jnp.concatenate([-values[..., half_width:], values[..., :half_width]], axis=-1)
    return values * cosine_table + turned * sine_table

def head_chain(projected, gain, cosine_table, sine_table):
    shaped = projected.reshape(projected.shape[0], -1, gain.shape[0])
    return rotate(rms_scale(shaped, gain), cosine_table, sine_table)

def doc_positions(segment_row):
    position_idx = jnp.arange(segment_row.shape[0], dtype=jnp.int32)
    boundary = jnp.concatenate([jnp.ones((1,), dtype=bool), segment_row[1:] != segment_row[:-1]])
    doc_start = lax.cummax(jnp.where(boundary, position_idx, 0), axis=0)
    return position_idx - doc_start

def sequence_layer(weight_set, gain_set, tokens_row, segment_row):
    full_query, full_key, full_value, full_output, full_gate, full_up, full_down = weight_set
    gain_attn = gain_set[:MODEL_WIDTH]
    gain_mlp = gain_set[MODEL_WIDTH:2 * MODEL_WIDTH]
    gain_query = gain_set[2 * MODEL_WIDTH:2 * MODEL_WIDTH + HEAD_SIZE]
    gain_key = gain_set[2 * MODEL_WIDTH + HEAD_SIZE:]
    sequence_length = tokens_row.shape[0]
    query_group_count = QUERY_HEADS // KEY_VALUE_HEADS
    cosine_table, sine_table = rope_tables(doc_positions(segment_row), HEAD_SIZE)
    normed = low(rms_scale(tokens_row, gain_attn))
    q_proj = low_back(jnp.dot(normed, full_query, precision=HIGH_PRECISION))
    k_proj = low_back(jnp.dot(normed, full_key, precision=HIGH_PRECISION))
    value_reduced = low(low_back(jnp.dot(normed, full_value, precision=HIGH_PRECISION)))
    rotated_queries = low(head_chain(q_proj, gain_query, cosine_table, sine_table))
    rotated_keys = low(head_chain(k_proj, gain_key, cosine_table, sine_table))
    grouped_queries = rotated_queries.reshape(sequence_length, KEY_VALUE_HEADS, query_group_count, HEAD_SIZE)
    scores = low_back(jnp.einsum('qhgd,khd->hgqk', grouped_queries, rotated_keys, precision=HIGH_PRECISION) * HEAD_SIZE ** (-0.5))
    position_idx = jnp.arange(sequence_length)
    allowed = (position_idx[None, :] <= position_idx[:, None]) & (segment_row[None, :] == segment_row[:, None])
    scores = jnp.where(allowed[None, None, :, :], scores, NEG_FILL)
    attention_probability = jax.nn.softmax(scores, axis=-1)
    head_output_rows = jnp.einsum('bwvz,zbu->vbwu', attention_probability, value_reduced.reshape(sequence_length, KEY_VALUE_HEADS, HEAD_SIZE), precision=HIGH_PRECISION)
    att_low = low(low_back(head_output_rows.reshape(sequence_length, QUERY_HEADS * HEAD_SIZE)))
    branch = low_back(jnp.dot(att_low, full_output, precision=HIGH_PRECISION))
    middle = tokens_row + branch
    normed_two = low(rms_scale(middle, gain_mlp))
    gate_pre = low_back(jnp.dot(normed_two, full_gate, precision=HIGH_PRECISION))
    up_pre = low_back(jnp.dot(normed_two, full_up, precision=HIGH_PRECISION))
    hidden = low(jax.nn.silu(gate_pre) * up_pre)
    return middle + low_back(jnp.dot(hidden, full_down, precision=HIGH_PRECISION))

def newton_schulz(current):
    for ns_turn in range(NS_STEPS):
        gram = lax.dot_general(current, current, (((0,), (0,)), ((), ())), preferred_element_type=jnp.float32).astype(jnp.bfloat16)
        product = jnp.dot(current, gram, preferred_element_type=jnp.float32)
        again = jnp.dot(product.astype(jnp.bfloat16), gram, preferred_element_type=jnp.float32)
        current = (NS_A * current.astype(jnp.float32) + NS_B * product + NS_C * again).astype(jnp.bfloat16)
    return current

def reference(inputs, cotangent, segments, w_query, key_weight_master, value_weight_master, w_output, w_gate, w_up, w_down, moment_query, moment_key, moment_value, moment_output, moment_gate, moment_up, moment_down, norm_gains, gain_first, gain_second):
    masters = (w_query, key_weight_master, value_weight_master, w_output, w_gate, w_up, w_down)
    moments = (moment_query, moment_key, moment_value, moment_output, moment_gate, moment_up, moment_down)

    def forward(weight_set, gain_set, token_set):
        rounded = tuple((low(weight) for weight in weight_set))

        def one_sequence(pair):
            return sequence_layer(rounded, gain_set, pair[0], pair[1])
        return lax.map(jax.checkpoint(one_sequence), (token_set, segments))
    outputs, pullback = jax.vjp(forward, masters, norm_gains, inputs.astype(jnp.float32))
    weight_grads, gain_grad, input_grad = pullback(cotangent.astype(jnp.float32))
    new_moments = []
    new_weights = []
    for matrix_idx in range(7):
        grad_now = weight_grads[matrix_idx]
        moment_new = MOMENTUM * moments[matrix_idx] + grad_now
        update = grad_now + MOMENTUM * moment_new
        norm_value = jnp.sqrt(jnp.sum(update * update))
        form = update.T if SIDEWAYS[matrix_idx] else update
        ortho = newton_schulz((form / (norm_value + NS_EPS)).astype(jnp.bfloat16)).astype(jnp.float32)
        ortho = ortho.T if SIDEWAYS[matrix_idx] else ortho
        stride = LR_MUON * math.sqrt(max(update.shape))
        new_weights.append(masters[matrix_idx] * (1.0 - LR_MUON * DECAY_MUON) - stride * ortho)
        new_moments.append(moment_new)
    first_new = BETA_ONE * gain_first + (1.0 - BETA_ONE) * gain_grad
    second_new = BETA_TWO * gain_second + (1.0 - BETA_TWO) * gain_grad * gain_grad
    corr_one = 1.0 - BETA_ONE ** ADAM_STEP
    corr_two = 1.0 - BETA_TWO ** ADAM_STEP
    gains_new = norm_gains - LR_GAIN * (first_new / corr_one) / (jnp.sqrt(second_new / corr_two) + EPS_ADAM)
    return (outputs.astype(jnp.bfloat16), input_grad, weight_grads[0], weight_grads[1], weight_grads[2], weight_grads[3], weight_grads[4], weight_grads[5], weight_grads[6], new_moments[0], new_moments[1], new_moments[2], new_moments[3], new_moments[4], new_moments[5], new_moments[6], new_weights[0], new_weights[1], new_weights[2], new_weights[3], new_weights[4], new_weights[5], new_weights[6], first_new, second_new, gains_new)
```

```python
import functools
import math

import jax
import jax.numpy as jnp
from jax import lax
from jax.experimental import pallas as pl
from jax.experimental.pallas import tpu as pltpu
from jax.sharding import Mesh
from jax.sharding import PartitionSpec as P

MODEL_WIDTH = 2048
QUERY_HEADS = 16
KEY_VALUE_HEADS = 8
HEAD_SIZE = 128
FF = 6144
ADAM_STEP = 10

EPS_NORM = 1e-06
THETA = 1000000.0
NEG_FILL = -1e30
MOMENTUM = 0.95
NS_A = 3.4445
NS_B = -4.775
NS_C = 2.0315
NS_EPS = 1e-07
LR_MUON = 0.2
DECAY_MUON = 0.01
LR_GAIN = 0.5
BETA_ONE = 0.9
BETA_TWO = 0.95
EPS_ADAM = 1e-08

CORES = 2
PLANES = 4
KV_WIDTH = KEY_VALUE_HEADS * HEAD_SIZE
BF16 = jnp.bfloat16
F32 = jnp.float32
SHARDS = ("z", "y", "fsdp")
PLANE_ROWS = ("z", "y")
EVERYWHERE = ("z", "y", "core", "fsdp")


def rms_scale(values, gain):
    return values * lax.rsqrt(jnp.mean(values * values, axis=-1, keepdims=True) + EPS_NORM) * gain


def rope_tables(positions, head_width):
    half_width = head_width // 2
    freq = jnp.exp(
        -(2.0 * jnp.arange(half_width, dtype=jnp.float32) / head_width) * math.log(THETA)
    )
    angle = positions.astype(jnp.float32)[..., None] * freq
    cosine = jnp.cos(angle)
    sine = jnp.sin(angle)
    return jnp.concatenate([cosine, cosine], -1), jnp.concatenate([-sine, sine], -1)


def dot_nn(left, right):
    return lax.dot_general(left, right, (((1,), (0,)), ((), ())), preferred_element_type=F32)


def dot_nt(left, right):
    return lax.dot_general(left, right, (((1,), (1,)), ((), ())), preferred_element_type=F32)


def dot_tn(left, right):
    return lax.dot_general(left, right, (((0,), (0,)), ((), ())), preferred_element_type=F32)


def head_chain(head, gain, cosine, sine):
    scaled = head * lax.rsqrt(jnp.mean(head * head, axis=-1, keepdims=True) + EPS_NORM) * gain
    return scaled * cosine + pltpu.roll(scaled, HEAD_SIZE // 2, 1) * sine


def head_chain_back(head, gain, cosine, sine, grad):
    grad = grad * cosine + pltpu.roll(grad * sine, HEAD_SIZE // 2, 1)
    scale = lax.rsqrt(jnp.mean(head * head, axis=-1, keepdims=True) + EPS_NORM)
    unit = head * scale
    d_gain = jnp.sum(grad * unit, axis=0, keepdims=True)
    grad = grad * gain
    return scale * (grad - unit * jnp.mean(grad * unit, axis=-1, keepdims=True)), d_gain


def key_value_kernel(near_ref, far_ref, gain_ref, cos_ref, sin_ref, proj_ref, low_ref):
    proj = near_ref[...] + far_ref[...].astype(F32)
    proj_ref[...] = proj
    is_key = pl.program_id(0) < KEY_VALUE_HEADS

    @pl.when(is_key)
    def _():
        low_ref[...] = head_chain(proj, gain_ref[...], cos_ref[...], sin_ref[...]).astype(BF16)

    @pl.when(jnp.logical_not(is_key))
    def _():
        low_ref[...] = proj.astype(BF16)


def key_value_back_kernel(grad_ref, proj_ref, gain_ref, cos_ref, sin_ref, low_ref, d_gain_ref):
    head = pl.program_id(0)

    @pl.when(head == 0)
    def _():
        d_gain_ref[...] = jnp.zeros_like(d_gain_ref)

    @pl.when(head < KEY_VALUE_HEADS)
    def _():
        d_proj, d_gain = head_chain_back(
            proj_ref[...], gain_ref[...], cos_ref[...], sin_ref[...], grad_ref[0]
        )
        low_ref[...] = d_proj.astype(BF16)
        d_gain_ref[...] += d_gain

    @pl.when(head >= KEY_VALUE_HEADS)
    def _():
        low_ref[...] = grad_ref[0].astype(BF16)


def attention_weights(q_ref, k_ref, mask_ref, gain_ref, cos_ref, sin_ref):
    query = head_chain(q_ref[...], gain_ref[...], cos_ref[0], sin_ref[0]).astype(BF16)
    scores = dot_nt(k_ref[0], query)
    weights = jnp.exp2(scores * (HEAD_SIZE ** (-0.5) * math.log2(math.e)))
    return query, weights * mask_ref[0].astype(F32)


def attention_kernel(
    q_ref, k_ref, v_ref, mask_ref, gain_ref, cos_ref, sin_ref, out_ref, out_turned_ref
):
    _, weights = attention_weights(q_ref, k_ref, mask_ref, gain_ref, cos_ref, sin_ref)
    total = jnp.sum(weights, axis=0, keepdims=True)
    out = dot_tn(v_ref[0], weights.astype(BF16)) * (1.0 / total)
    out_turned_ref[...] = out.astype(BF16)
    out_ref[...] = out.T.astype(BF16)


def attention_back_kernel(
    q_ref, k_ref, v_ref, mask_ref, gain_ref, cos_ref, sin_ref, grad_ref,
    *refs,
):
    q_low_ref, q_low_turned_ref, d_kv_ref, d_gain_ref = refs[-4:]

    @pl.when(pl.program_id(0) == 0)
    def _():
        d_gain_ref[...] = jnp.zeros_like(d_gain_ref)

    query, weights = attention_weights(q_ref, k_ref, mask_ref, gain_ref, cos_ref, sin_ref)
    grad = grad_ref[...]
    probs = weights * (1.0 / jnp.sum(weights, axis=0, keepdims=True))
    d_probs = dot_nt(v_ref[0], grad)
    delta = jnp.sum(probs * d_probs, axis=0, keepdims=True)
    d_scores = (probs * (d_probs - delta)).astype(BF16)
    d_value = dot_nn(probs.astype(BF16), grad).astype(BF16)
    d_key = (dot_nn(d_scores, query) * HEAD_SIZE ** (-0.5)).astype(BF16)

    d_kv_ref[0] = d_key
    d_kv_ref[1] = d_value
    d_query = dot_tn(k_ref[0], d_scores).T * HEAD_SIZE ** (-0.5)
    d_proj, d_gain = head_chain_back(
        q_ref[...], gain_ref[...], cos_ref[0], sin_ref[0], d_query
    )
    q_low_ref[...] = d_proj.astype(BF16)
    q_low_turned_ref[...] = d_proj.T.astype(BF16)
    d_gain_ref[...] += d_gain


def swiglu_kernel(two_ref, cot_ref, gate_ref, up_ref, down_ref, *out_refs):
    width = two_ref.shape[1]
    two = two_ref[...]
    gate = dot_nt(two, gate_ref[...].reshape(-1, width))
    up = dot_nt(two, up_ref[...].reshape(-1, width))
    d_hidden = dot_nt(cot_ref[...], down_ref[...].reshape(-1, width))
    sig = 1.0 / (1.0 + jnp.exp(-gate))
    silu = gate * sig
    results = (silu * up, d_hidden * up * sig * (1.0 + gate * (1.0 - sig)), d_hidden * silu)
    for result, out_ref, turned_ref in zip(results, out_refs[:3], out_refs[3:]):
        low = result.astype(BF16)
        out_ref[...] = low
        turned_ref[...] = low.T


def back_to_width_kernel(count, *refs):
    lefts, rights, out_ref = refs[:count], refs[count : 2 * count], refs[-1]
    width = out_ref.shape[1]
    total = 0.0
    for left, right in zip(lefts, rights):
        if split_by_y(right.shape[2]):
            half = left.shape[1] // CORES
            for y in range(CORES):
                rows = right[:, y].reshape(-1, width)
                total = total + dot_nn(left[:, y * half : (y + 1) * half], rows)
        else:
            total = total + dot_nn(left[...], right[...].reshape(-1, width))
    out_ref[...] = total.astype(BF16)


def weight_grad_kernel(place_ref, left_ref, right_ref, out_ref):
    out_ref[...] = dot_nn(left_ref[...], right_ref[...]).astype(BF16)


def chain_kernel(start_ref, gram_ref, bend_ref, out_ref, first_ref, product_ref, one_ref, two_ref):
    width = start_ref.shape[1]
    tile = 512

    def columns(body):
        @pl.loop(0, width // tile)
        def _(step):
            body(pl.ds(pl.multiple_of(step * tile, tile), tile))

    def times_p(rows_ref, cols):
        return NS_A * rows_ref[:, cols].astype(F32) + dot_nn(rows_ref[...], bend_ref[:, cols])

    def to_first(cols):
        first_ref[:, cols] = times_p(start_ref, cols).astype(BF16)

    def bent_first(cols):
        one_ref[:, cols] = times_p(first_ref, cols).astype(BF16)

    def by_gram(cols):
        two_ref[:, cols] = dot_nn(one_ref[...], gram_ref[:, cols]).astype(BF16)

    def to_product(cols):
        product_ref[:, cols] = times_p(two_ref, cols).astype(BF16)

    def bent_product(cols):
        one_ref[:, cols] = times_p(product_ref, cols).astype(BF16)

    def finish(cols):
        again = times_p(two_ref, cols)
        out_ref[:, cols] = (
            NS_A * first_ref[:, cols].astype(F32)
            + NS_B * product_ref[:, cols].astype(F32)
            + NS_C * again
        ).astype(BF16)

    for body in (to_first, bent_first, by_gram, to_product, bent_product, by_gram, finish):
        columns(body)


def shaped(shape, dtype):
    return jax.ShapeDtypeStruct(shape, dtype)


SMALL = pl.CostEstimate(flops=1, bytes_accessed=1, transcendentals=0)


def limits(mebibytes):
    return pltpu.CompilerParams(vmem_limit_bytes=mebibytes * 1024 * 1024)


def key_value_chain(near, far, gain, cosine, sine):
    rows = near.shape[0]
    block = pl.BlockSpec((rows, HEAD_SIZE), lambda head: (0, head))
    fixed = pl.BlockSpec((rows, HEAD_SIZE), lambda head: (0, 0))
    one = pl.BlockSpec((1, HEAD_SIZE), lambda head: (0, 0))
    return pl.pallas_call(
        key_value_kernel,
        grid=(2 * KEY_VALUE_HEADS,),
        in_specs=[block, block, one, fixed, fixed],
        out_specs=[block, block],
        out_shape=[shaped(near.shape, F32), shaped(near.shape, BF16)],
        compiler_params=limits(16),
        cost_estimate=SMALL,
        name="key_value_chain",
    )(near, far, gain, cosine, sine)


def key_value_back(grad, proj, gain, cosine, sine):
    rows = proj.shape[0]
    heads = KEY_VALUE_HEADS
    block = pl.BlockSpec((rows, HEAD_SIZE), lambda head: (0, head))
    split = pl.BlockSpec((1, rows, HEAD_SIZE), lambda head: (head // heads, 0, head % heads))
    fixed = pl.BlockSpec((rows, HEAD_SIZE), lambda head: (0, 0))
    one = pl.BlockSpec((1, HEAD_SIZE), lambda head: (0, 0))
    return pl.pallas_call(
        key_value_back_kernel,
        grid=(2 * heads,),
        in_specs=[split, block, one, fixed, fixed],
        out_specs=[block, one],
        out_shape=[shaped(proj.shape, BF16), shaped((1, HEAD_SIZE), F32)],
        compiler_params=limits(16),
        cost_estimate=SMALL,
        name="key_value_back",
    )(grad, proj, gain, cosine, sine)


def attention_specs(rows, keys, heads):
    return [
        pl.BlockSpec((rows, HEAD_SIZE), lambda seq, head: (seq, head)),
        pl.BlockSpec((1, keys, HEAD_SIZE), lambda seq, head: (seq, 0, head)),
        pl.BlockSpec((1, keys, HEAD_SIZE), lambda seq, head: (seq, 0, heads + head)),
        pl.BlockSpec((1, keys, rows), lambda seq, head: (seq, 0, 0)),
        pl.BlockSpec((1, HEAD_SIZE), lambda seq, head: (0, 0)),
        pl.BlockSpec((1, rows, HEAD_SIZE), lambda seq, head: (seq, 0, 0)),
        pl.BlockSpec((1, rows, HEAD_SIZE), lambda seq, head: (seq, 0, 0)),
    ]


def attention(q_proj, kv, mask, gain, cosine, sine):
    sequences, keys, rows = mask.shape
    heads = q_proj.shape[1] // HEAD_SIZE
    specs = attention_specs(rows, keys, heads)
    return pl.pallas_call(
        attention_kernel,
        grid=(sequences, heads),
        in_specs=specs,
        out_specs=[specs[0], pl.BlockSpec((HEAD_SIZE, rows), lambda seq, head: (head, seq))],
        out_shape=[shaped(q_proj.shape, BF16), shaped(q_proj.shape[::-1], BF16)],
        compiler_params=limits(40),
        cost_estimate=SMALL,
        name="attention",
    )(q_proj, kv, kv, mask, gain, cosine, sine)


def attention_back(q_proj, kv, mask, gain, cosine, sine, grad, seq, others):
    _, keys, rows = mask.shape
    heads = q_proj.shape[1] // HEAD_SIZE
    specs = [
        pl.BlockSpec((rows, HEAD_SIZE), lambda head: (seq, head)),
        pl.BlockSpec((1, keys, HEAD_SIZE), lambda head: (seq, 0, head)),
        pl.BlockSpec((1, keys, HEAD_SIZE), lambda head: (seq, 0, heads + head)),
        pl.BlockSpec((1, keys, rows), lambda head: (seq, 0, 0)),
        pl.BlockSpec((1, HEAD_SIZE), lambda head: (0, 0)),
        pl.BlockSpec((1, rows, HEAD_SIZE), lambda head: (seq, 0, 0)),
        pl.BlockSpec((1, rows, HEAD_SIZE), lambda head: (seq, 0, 0)),
    ]
    return pl.pallas_call(
        attention_back_kernel,
        grid=(heads,),
        in_specs=[*specs, specs[0]] + [pl.BlockSpec(memory_space=pl.ANY)] * len(others),
        out_specs=[
            specs[0],
            pl.BlockSpec((HEAD_SIZE, rows), lambda head: (head, seq)),
            pl.BlockSpec((2, keys, HEAD_SIZE), lambda head: (0, 0, head)),
            specs[4],
        ],
        out_shape=[
            shaped(q_proj.shape, BF16),
            shaped(q_proj.shape[::-1], BF16),
            shaped((2, keys, heads * HEAD_SIZE), BF16),
            shaped((1, HEAD_SIZE), F32),
        ],
        input_output_aliases={8 + place: place for place in range(len(others))},
        compiler_params=limits(48),
        cost_estimate=SMALL,
        name="attention_back",
    )(q_proj, kv, kv, mask, gain, cosine, sine, grad, *others)


def split_by_y(block_rows):
    return (PLANES * block_rows) % 128 == 0


def swiglu_both_ways(two, cot, ff):
    tokens, width = two.shape
    _, _, block_rows, _ = ff[0].shape
    ys = 1 if split_by_y(block_rows) else CORES
    tile = min(512, tokens)
    ff_tile = PLANES * ys * block_rows
    row_block = pl.BlockSpec((tile, width), lambda col, row: (row, 0))
    out_block = pl.BlockSpec((tile, ff_tile), lambda col, row: (row, col))
    turned_block = pl.BlockSpec((ff_tile, tile), lambda col, row: (col, row))
    weights = pl.BlockSpec((PLANES, ys, block_rows, width), lambda col, row: (0, col, 0, 0))
    columns = PLANES * CORES * block_rows
    return pl.pallas_call(
        swiglu_kernel,
        grid=(CORES // ys, tokens // tile),
        in_specs=[row_block, row_block] + [weights] * 3,
        out_specs=[out_block] * 3 + [turned_block] * 3,
        out_shape=[shaped((tokens, columns), BF16)] * 3 + [shaped((columns, tokens), BF16)] * 3,
        compiler_params=limits(60),
        cost_estimate=SMALL,
        name="swiglu_both_ways",
    )(two, cot, *ff)


def back_to_width(lefts, ff, first_row, rows):
    _, _, block_rows, width = ff[0].shape
    columns = PLANES * CORES * block_rows
    tile = min(256, rows)
    first = first_row // tile
    left_block = pl.BlockSpec((tile, columns), lambda row: (first + row, 0))
    weights = pl.BlockSpec(ff[0].shape, lambda row: (0, 0, 0, 0))
    return pl.pallas_call(
        functools.partial(back_to_width_kernel, len(lefts)),
        grid=(rows // tile,),
        in_specs=[left_block] * len(lefts) + [weights] * len(lefts),
        out_specs=pl.BlockSpec((tile, width), lambda row: (row, 0)),
        out_shape=shaped((rows, width), BF16),
        compiler_params=limits(56),
        cost_estimate=SMALL,
        name="back_to_width",
    )(*lefts, *ff)


def weight_grad(left_turned, right, place, parts):
    rows = left_turned.shape[0] // parts
    tokens, width = right.shape
    tile = min(512, width)
    return pl.pallas_call(
        weight_grad_kernel,
        grid_spec=pltpu.PrefetchScalarGridSpec(
            num_scalar_prefetch=1,
            grid=(width // tile,),
            in_specs=[
                pl.BlockSpec((rows, tokens), lambda col, place_ref: (place_ref[0], 0)),
                pl.BlockSpec((tokens, tile), lambda col, place_ref: (0, col)),
            ],
            out_specs=pl.BlockSpec((rows, tile), lambda col, place_ref: (0, col)),
        ),
        out_shape=shaped((rows, width), BF16),
        compiler_params=limits(40),
        cost_estimate=SMALL,
        name="weight_grad",
    )(jnp.asarray(place, jnp.int32).reshape(1), left_turned, right)


def times_columns_kernel(left_ref, right_ref, out_ref):
    out_ref[...] = dot_nn(left_ref[...], right_ref[...]).astype(BF16)


def times_columns(left, right, first_column, width):
    rows, depth = left.shape
    tile = min(512, width)
    first = first_column // tile
    return pl.pallas_call(
        times_columns_kernel,
        grid=(width // tile,),
        in_specs=[
            pl.BlockSpec((rows, depth), lambda col: (0, 0)),
            pl.BlockSpec((depth, tile), lambda col: (0, first + col)),
        ],
        out_specs=pl.BlockSpec((rows, tile), lambda col: (0, col)),
        out_shape=shaped((rows, width), BF16),
        compiler_params=limits(40),
        cost_estimate=SMALL,
        name="times_columns",
    )(left, right)


def bend_kernel(gram_ref, tile_ref, out_ref):
    square = dot_nn(gram_ref[...], tile_ref[...])
    out_ref[...] = (NS_B * tile_ref[...].astype(F32) + NS_C * square).astype(BF16)


def bend_of(gram):
    width = gram.shape[0]
    tile = 512
    return pl.pallas_call(
        bend_kernel,
        grid=(width // tile,),
        in_specs=[
            pl.BlockSpec((width, width), lambda col: (0, 0)),
            pl.BlockSpec((width, tile), lambda col: (0, col)),
        ],
        out_specs=pl.BlockSpec((width, tile), lambda col: (0, col)),
        out_shape=shaped(gram.shape, BF16),
        compiler_params=limits(48),
        cost_estimate=SMALL,
        name="bend_of",
    )(gram, gram)


def times_rows_kernel(left_ref, right_ref, out_ref):
    out_ref[...] = dot_nt(left_ref[...], right_ref[...]).astype(BF16)


def times_rows(left, right, place):
    rows, depth = left.shape
    columns = right.shape[0]
    tile = min(256, columns)
    return pl.pallas_call(
        times_rows_kernel,
        grid=(columns // tile,),
        in_specs=[
            pl.BlockSpec((rows, depth), lambda col: (0, 0)),
            pl.BlockSpec((tile, depth), lambda col: (col, place)),
        ],
        out_specs=pl.BlockSpec((rows, tile), lambda col: (0, col)),
        out_shape=shaped((rows, columns), BF16),
        compiler_params=limits(40),
        cost_estimate=SMALL,
        name="times_rows",
    )(left, right)


def chain(start, gram, bend):
    rows, width = start.shape
    whole = pl.BlockSpec((width, width), lambda: (0, 0), pipeline_mode=pl.Buffered(1))
    block = pl.BlockSpec((rows, width), lambda: (0, 0), pipeline_mode=pl.Buffered(1))
    return pl.pallas_call(
        chain_kernel,
        grid=(),
        in_specs=[block, whole, whole],
        out_specs=pl.BlockSpec((rows, width), lambda: (0, 0)),
        out_shape=shaped(start.shape, BF16),
        scratch_shapes=[pltpu.VMEM(start.shape, BF16)] * 4,
        compiler_params=limits(56),
        cost_estimate=SMALL,
        name="chain",
    )(start, gram, bend)


def after(value, *earlier):
    return lax.optimization_barrier((value, earlier))[0]


def shifted(step, count):
    return [(src, (src + step) % count) for src in range(count)]


def swap(value, axis_name="core"):
    return lax.ppermute(value, axis_name, shifted(1, CORES))


def with_partner(value):
    return jnp.concatenate([value, swap(value)], axis=0)


def ring_blocks(value, axis_name, count):
    return [value] + [
        lax.ppermute(value, axis_name, shifted(step, count)) for step in range(1, count)
    ]


def ring_send(blocks, axis_name, count):
    return [
        lax.ppermute(blocks[step].astype(BF16), axis_name, shifted(-step, count))
        for step in range(1, count)
    ]


def add_all(own, arrived):
    for term in arrived:
        own = own + term.astype(F32)
    return own


def pick(blocks, index, axis=0):
    return lax.dynamic_index_in_dim(blocks, index, axis, keepdims=False)


def gather_rows(shard, axes):
    return lax.all_gather(shard, axes, axis=0, tiled=True)


def scatter_blocks(blocks, axis_name):
    count = blocks.shape[0]
    here = lax.axis_index(axis_name)
    arrived = [
        lax.ppermute(pick(blocks, (here + step) % count), axis_name, shifted(step, count))
        for step in range(1, count)
    ]
    return add_all(pick(blocks, here).astype(F32), arrived)


def ordered_blocks(value, axis_name):
    count = lax.axis_size(axis_name)
    here = lax.axis_index(axis_name)
    blocks = ring_blocks(value, axis_name, count)
    if count == 2:
        first = jnp.where(here == 0, blocks[0], blocks[1])
        second = jnp.where(here == 0, blocks[1], blocks[0])
        return jnp.concatenate([first, second], axis=0)
    rows = value.shape[0]
    whole = jnp.zeros((count * rows, *value.shape[1:]), value.dtype)
    for step, block in enumerate(blocks):
        whole = lax.dynamic_update_slice_in_dim(whole, block, (here - step) % count * rows, 0)
    return whole


def sum_over_plane(partial, gain, beside):
    width = partial.shape[1]
    ring = lax.axis_size("fsdp")
    mine = scatter_blocks(partial.astype(BF16).reshape(CORES, -1, width), "core").astype(BF16)
    mine, gain = lax.optimization_barrier((mine, butterfly(gain, "core")))
    half = mine.shape[0] // 2
    one, two = mine[:half], mine[half:]
    one = scatter_blocks(one.reshape(ring, -1, width), "fsdp").astype(BF16)
    two = scatter_blocks(two.reshape(CORES, -1, width), "y").astype(BF16)
    one, two, gain, beside = lax.optimization_barrier(
        (one, two, butterfly(gain, "fsdp"), beside)
    )
    one = scatter_blocks(one.reshape(CORES, -1, width), "y").astype(BF16)
    two = scatter_blocks(two.reshape(ring, -1, width), "fsdp").astype(BF16)
    one, two, gain = lax.optimization_barrier((one, two, butterfly(gain, "y")))
    one = ordered_blocks(one, "y")
    two = ordered_blocks(two, "fsdp")
    one, two, gain = lax.optimization_barrier((one, two, butterfly(gain, "z")))
    one = ordered_blocks(one, "fsdp")
    two = ordered_blocks(two, "y")
    return ordered_blocks(jnp.concatenate([one, two], axis=0), "core"), gain, beside


def ff_grad_half(left_turned, right, block_rows, y):
    shape = (PLANES, block_rows, right.shape[1])
    if split_by_y(block_rows):
        return weight_grad(left_turned, right, y, CORES).reshape(shape)
    full = weight_grad(left_turned, right, 0, 1)
    return pick(full.reshape(PLANES, CORES, block_rows, -1), y, 1)


def halves_over_y(partials):
    here = lax.axis_index("y")
    split = [value.reshape(PLANES, CORES, -1, value.shape[-1]) for value in partials]
    sent = jnp.concatenate([pick(value, 1 - here, 1) for value in split], axis=-1)
    kept = [pick(value, here, 1) for value in split]
    return kept, swap(sent, "y"), sent


def chunks_over_z(kept, arrived):
    here = lax.axis_index("z")

    def chunk(step):
        plane = (here + step) % PLANES
        near = jnp.concatenate([pick(value, plane) for value in kept], axis=-1)
        return near.astype(F32) + pick(arrived, plane).astype(F32)

    own = chunk(0)
    sent = [chunk(step).astype(BF16) for step in range(1, PLANES)]
    return own, [
        lax.ppermute(value, "z", shifted(step + 1, PLANES)) for step, value in enumerate(sent)
    ], sent


def butterfly(value, axis_name):
    count = lax.axis_size(axis_name)
    step = 1
    while step < count:
        value = value + lax.ppermute(value, axis_name, [(src, src ^ step) for src in range(count)])
        step *= 2
    return value


def to_planes(chunks):
    here = lax.axis_index("z")
    arrived = [pick(chunks, here)]
    for step in range(1, PLANES):
        arrived.append(
            lax.ppermute(pick(chunks, (here + step) % PLANES), "z", shifted(step, PLANES))
        )
    return jnp.stack(arrived)


def from_planes(arrived):
    here = lax.axis_index("z")
    back = [arrived[0]]
    for step in range(1, PLANES):
        back.append(lax.ppermute(arrived[step], "z", shifted(-step, PLANES)))
    back = jnp.stack(back)
    return [pick(back, (chunk - here) % PLANES) for chunk in range(PLANES)]


def orthogonal_rows(update, update_gram, halves, earlier):
    width = update.shape[1]
    side = jnp.arange(width) < width // 2
    index = jnp.arange(width)
    diagonal = jnp.sum(
        jnp.where(index[:, None] == index[None, :], update_gram.astype(F32), 0.0), axis=0
    )
    low_half = jnp.sum(diagonal[: width // 2])
    high_half = jnp.sum(diagonal[width // 2 :])
    both = low_half + high_half
    squares = jnp.stack([jnp.where(halves, low_half, both), jnp.where(halves, high_half, both)])
    inverse = jnp.repeat(1.0 / (jnp.sqrt(squares) + NS_EPS), width // 2)
    kept = jnp.logical_not(halves) | (side[:, None] == side[None, :])
    start = (update.astype(F32) * inverse).astype(BF16)
    gram = jnp.where(kept, update_gram.astype(F32) * inverse[:, None] * inverse[None, :], 0.0).astype(BF16)
    return chain(start, after(gram, earlier), bend_of(gram))


def per_device(
    inputs,
    cotangent,
    segments,
    w_query,
    key_weight_master,
    value_weight_master,
    w_output,
    w_gate,
    w_up,
    w_down,
    moment_query,
    moment_key,
    moment_value,
    moment_output,
    moment_gate,
    moment_up,
    moment_down,
    norm_gains,
    gain_first,
    gain_second,
):
    rows = inputs.shape[1]
    complete_rows = segments.shape[1]
    ring = lax.axis_size("fsdp")
    place = lax.axis_index("fsdp")
    core = lax.axis_index("core")
    gain_attn = norm_gains[:MODEL_WIDTH]
    gain_mlp = norm_gains[MODEL_WIDTH : 2 * MODEL_WIDTH]
    gain_query = norm_gains[2 * MODEL_WIDTH : 2 * MODEL_WIDTH + HEAD_SIZE]
    gain_key = norm_gains[2 * MODEL_WIDTH + HEAD_SIZE :]

    attention_rows = gather_rows(
        jnp.concatenate(
            [
                key_weight_master.astype(BF16),
                value_weight_master.astype(BF16),
                w_query.astype(BF16).T,
                w_output.astype(BF16),
            ],
            axis=1,
        ),
        SHARDS,
    )
    key_value_rows = attention_rows[:, :MODEL_WIDTH]
    query_rows = attention_rows[:, MODEL_WIDTH : 2 * MODEL_WIDTH]
    output_rows = attention_rows[:, 2 * MODEL_WIDTH :]
    gate_ff, up_ff, down_ff = (
        gather_rows(shard[None], PLANE_ROWS).reshape(PLANES, CORES, *shard.shape)
        for shard in (w_gate.astype(BF16).T, w_up.astype(BF16).T, w_down.astype(BF16))
    )

    both_segments = with_partner(segments)
    row_idx = jnp.arange(complete_rows, dtype=jnp.int32)
    boundary = jnp.concatenate(
        [
            jnp.ones((CORES, 1), dtype=bool),
            both_segments[:, 1:] != both_segments[:, :-1],
        ],
        axis=1,
    )
    doc_start = lax.cummax(jnp.where(boundary, row_idx[None, :], 0), axis=1)
    first_row = place * rows
    positions = lax.dynamic_slice_in_dim(row_idx[None, :] - doc_start, first_row, rows, 1)
    cosine_table, sine_table = rope_tables(positions, HEAD_SIZE)
    query_segments = lax.dynamic_slice_in_dim(both_segments, first_row, rows, 1)
    query_pos = first_row + jnp.arange(rows, dtype=jnp.int32)
    key_starts = [((place - step) % ring) * rows for step in range(ring)]
    key_pos = jnp.concatenate([at + jnp.arange(rows, dtype=jnp.int32) for at in key_starts])
    key_segments = jnp.concatenate(
        [lax.dynamic_slice_in_dim(both_segments, at, rows, 1) for at in key_starts], axis=1
    )
    mask = (
        (key_pos[None, :, None] <= query_pos[None, None, :])
        & (key_segments[:, :, None] == query_segments[:, None, :])
    ).astype(BF16)

    residual = inputs.astype(F32).reshape(rows, MODEL_WIDTH)
    normed = rms_scale(residual, gain_attn).astype(BF16)
    both_normed = with_partner(normed)
    cotangent_rows = cotangent.reshape(rows, MODEL_WIDTH)
    pair_rows = CORES * rows

    def own_columns(values):
        split = values.reshape(values.shape[0], -1, CORES, HEAD_SIZE)
        return pick(split, core, 2).reshape(values.shape[0], MODEL_WIDTH // CORES)

    own_normed = own_columns(both_normed)
    kv_sent = dot_nn(own_normed[rows:], key_value_rows).astype(BF16)
    kv_near = dot_nn(own_normed[:rows], key_value_rows)
    q_proj = dot_nt(both_normed, query_rows)
    kv_proj, kv_low = key_value_chain(
        kv_near, swap(kv_sent), gain_key[None], cosine_table[0], sine_table[0]
    )
    own_kv = after(jnp.concatenate(ring_blocks(kv_low, "fsdp", ring), axis=0), q_proj)
    both_kv = with_partner(own_kv).reshape(CORES, complete_rows, 2 * KV_WIDTH)
    attention_inputs = (q_proj, both_kv, mask, gain_query[None], cosine_table, sine_table)
    att_low, att_turned = attention(*attention_inputs)
    team_cotangent = with_partner(
        jnp.concatenate(ring_blocks(after(cotangent_rows, own_kv), "fsdp", ring), axis=0)
    )
    out_sent = dot_nn(att_low[rows:], output_rows).astype(BF16)
    out_near = dot_nn(att_low[:rows], output_rows)
    middle = residual + out_near + swap(out_sent).astype(F32)

    normed_two = rms_scale(middle, gain_mlp).astype(BF16)
    team_two = with_partner(jnp.concatenate(ring_blocks(normed_two, "fsdp", ring), axis=0))
    hidden, d_gate, d_up, hidden_turned, d_gate_turned, d_up_turned = swiglu_both_ways(
        team_two, team_cotangent, (gate_ff, up_ff, down_ff)
    )
    block_rows = gate_ff.shape[2]
    own_rows = ring * rows
    other_y = 1 - lax.axis_index("y")
    own_y = lax.axis_index("y")
    down_sent = ff_grad_half(hidden_turned, team_cotangent, block_rows, other_y)
    down_passed = swap(down_sent, "y")
    down_kept = ff_grad_half(
        after(hidden_turned, down_sent), team_cotangent, block_rows, own_y
    )
    back_grads = after((d_gate, d_up), down_kept)
    back_far = back_to_width(back_grads, (gate_ff, up_ff), own_rows, own_rows)
    back_near = back_to_width(after(back_grads, back_far), (gate_ff, up_ff), 0, own_rows)
    gate_turned = after(d_gate_turned, back_near)
    gate_sent = ff_grad_half(gate_turned, team_two, block_rows, other_y)
    gate_passed = swap(gate_sent, "y")
    down_own, down_chunks, down_chunks_sent = chunks_over_z(
        [down_kept], after(down_passed, gate_sent)
    )
    back_half = back_near.astype(F32) + swap(after(back_far, down_chunks_sent)).astype(F32)
    back_half = back_half.reshape(ring, rows, MODEL_WIDTH)
    back_arrived = ring_send([back_half[step] for step in range(ring)], "fsdp", ring)
    gate_kept = ff_grad_half(after(gate_turned, back_half), team_two, block_rows, own_y)
    up_turned = after(d_up_turned, gate_kept)
    up_sent = ff_grad_half(up_turned, team_two, block_rows, other_y)
    up_passed = swap(up_sent, "y")
    up_kept = ff_grad_half(after(up_turned, up_sent), team_two, block_rows, own_y)
    back_arrived, down_chunks, gate_passed = after(
        (back_arrived, down_chunks, gate_passed), up_kept
    )
    gate_own, gate_chunks, gate_chunks_sent = chunks_over_z([gate_kept], gate_passed)
    d_normed_two = add_all(after(back_half[0], gate_chunks_sent), back_arrived)
    second_back = jax.vjp(rms_scale, middle, gain_mlp)[1]
    d_mid_norm, d_gain_mlp = second_back(d_normed_two)
    d_middle = cotangent_rows.astype(F32) + d_mid_norm

    both_mid = with_partner(d_middle.astype(BF16))
    d_head = times_rows(both_mid, attention_rows, 2)
    output_grad = weight_grad(att_turned, after(both_mid, d_head), 0, 1)
    output_blocks = jnp.moveaxis(output_grad.reshape(PLANES * CORES, ring, -1, MODEL_WIDTH), 1, 0)
    output_half = scatter_blocks(output_blocks, "fsdp").astype(BF16)
    d_head = after(d_head, output_grad)
    *far_parts, d_kv_far, far_gain = attention_back(*attention_inputs, d_head, 1, ())
    q_low, q_low_turned, d_kv_near, near_gain = attention_back(
        *attention_inputs, d_head, 0, far_parts
    )
    d_gain_query = (far_gain + near_gain)[0]
    query_grad = weight_grad(q_low_turned, both_normed, 0, 1)
    from_query = times_columns(after(q_low, query_grad), attention_rows, MODEL_WIDTH, MODEL_WIDTH)
    up_passed, gate_chunks = after((up_passed, gate_chunks), from_query)
    up_own, up_chunks, up_chunks_sent = chunks_over_z([up_kept], up_passed)
    d_kv_half = d_kv_near.astype(F32) + swap(after(d_kv_far, up_chunks_sent)).astype(F32)
    d_kv_half = d_kv_half.reshape(2, ring, rows, KV_WIDTH)
    d_kv_arrived = ring_send([d_kv_half[:, step] for step in range(ring)], "fsdp", ring)
    hidden = after(hidden, d_kv_half)
    down_far = back_to_width((hidden,), (down_ff,), own_rows, own_rows)
    down_near = back_to_width((after(hidden, down_far),), (down_ff,), 0, own_rows)
    up_chunks, d_kv_arrived, output_half = after(
        (up_chunks, d_kv_arrived, output_half), down_near
    )
    query_blocks = jnp.moveaxis(
        after(query_grad, *d_kv_arrived).reshape(PLANES * CORES, ring, -1, MODEL_WIDTH), 1, 0
    )
    query_half = scatter_blocks(query_blocks, "fsdp").astype(BF16)
    d_kv_total = add_all(d_kv_half[:, 0], d_kv_arrived)
    kv_low_grad, d_gain_key = key_value_back(
        d_kv_total, kv_proj, gain_key[None], cosine_table[0], sine_table[0]
    )
    d_gain_key = d_gain_key[0]
    both_kv_low = with_partner(kv_low_grad)
    key_value_grad = dot_tn(own_normed, both_kv_low).astype(BF16)
    key_value_blocks = jnp.moveaxis(
        key_value_grad.reshape(PLANES * CORES, ring, -1, MODEL_WIDTH), 1, 0
    )
    key_value_half = scatter_blocks(key_value_blocks, "fsdp").astype(BF16)
    from_kv = times_rows(after(both_kv_low, key_value_blocks), attention_rows, 0)
    down_shard = add_all(down_own, down_chunks)
    gate_shard = add_all(gate_own, gate_chunks)
    up_shard = add_all(up_own, up_chunks)
    masters = (w_query, key_weight_master, value_weight_master, w_output, w_gate, w_up, w_down)
    moments = (
        moment_query,
        moment_key,
        moment_value,
        moment_output,
        moment_gate,
        moment_up,
        moment_down,
    )
    full_sides = (MODEL_WIDTH,) * 4 + (FF,) * 3
    sideways = (True, False, False, False, True, True, False)

    def updated(shard, idx):
        grad = shard.T if sideways[idx] else shard
        moment = MOMENTUM * moments[idx] + grad
        update = grad + MOMENTUM * moment
        return grad, moment, (update.T if sideways[idx] else update).astype(BF16)

    plane = lax.axis_index("z")
    in_plane = ("y", "core", "fsdp")
    big = [updated(gate_shard, 4), updated(up_shard, 5), updated(down_shard, 6)]
    slots = jnp.stack([form for _, _, form in big] + [jnp.zeros_like(big[0][2])])
    big_mine = to_planes(slots).reshape(-1, MODEL_WIDTH)
    big_mine, query_half, key_value_half = after(
        (big_mine, query_half, key_value_half), from_kv
    )
    kept, arrived, attention_passed = halves_over_y([output_half, query_half, key_value_half])
    big_gram = dot_tn(after(big_mine, attention_passed), big_mine)

    from_query = from_query[:rows].astype(F32) + swap(from_query[rows:]).astype(F32)
    kv_here = from_kv[:rows].reshape(rows, -1, HEAD_SIZE)
    kv_there = swap(from_kv[rows:]).reshape(rows, -1, HEAD_SIZE)
    from_kv_full = jnp.stack(
        [jnp.where(core == 0, kv_here, kv_there), jnp.where(core == 0, kv_there, kv_here)], axis=2
    ).reshape(rows, MODEL_WIDTH)
    d_normed = from_query + from_kv_full.astype(F32)
    first_back = jax.vjp(rms_scale, residual, gain_attn)[1]
    d_residual, d_gain_attn = first_back(d_normed)
    input_grad = (d_middle + d_residual).reshape(inputs.shape)
    down_half = (down_near.astype(F32) + swap(after(down_far, big_gram)).astype(F32)).reshape(
        ring, rows, MODEL_WIDTH
    )
    down_arrived = ring_send([down_half[step] for step in range(ring)], "fsdp", ring)
    block_out = (middle + add_all(down_half[0], down_arrived)).astype(BF16).reshape(inputs.shape)
    gain_grad = jnp.concatenate([d_gain_attn, d_gain_mlp, d_gain_query, d_gain_key])

    big_gram, gain_grad, arrived = sum_over_plane(big_gram, gain_grad, arrived)
    attention_own, attention_chunks, _ = chunks_over_z(kept, arrived)
    attention_total = add_all(attention_own, attention_chunks)
    output_shard = attention_total[:, :MODEL_WIDTH]
    query_shard = attention_total[:, MODEL_WIDTH : 2 * MODEL_WIDTH]
    key_value_shard = attention_total[:, 2 * MODEL_WIDTH :]
    small = [
        updated(query_shard, 0),
        updated(key_value_shard[:, :KV_WIDTH], 1),
        updated(key_value_shard[:, KV_WIDTH:], 2),
        updated(output_shard, 3),
    ]
    small_slots = jnp.stack(
        [
            small[0][2],
            jnp.concatenate([small[1][2], small[2][2]], axis=1),
            small[3][2],
            jnp.zeros_like(small[3][2]),
        ]
    )
    small_mine = to_planes(small_slots).reshape(-1, MODEL_WIDTH)
    whole = gather_rows(small_mine, in_plane)
    turned = orthogonal_rows(big_mine, big_gram, jnp.bool_(False), small_mine)
    turned, whole = lax.optimization_barrier((turned, whole))
    returned = from_planes(turned.reshape(slots.shape))
    turned = orthogonal_rows(small_mine, dot_tn(whole, whole), plane == 1, small_mine)
    turned, returned = lax.optimization_barrier((turned, returned))
    small_returned = from_planes(turned.reshape(small_slots.shape))
    ortho = (
        small_returned[0],
        small_returned[1][:, :KV_WIDTH],
        small_returned[1][:, KV_WIDTH:],
        small_returned[2],
        *returned[:3],
    )
    new_weights = tuple(
        master * (1.0 - LR_MUON * DECAY_MUON)
        - LR_MUON * math.sqrt(side) * (rows_now.T if turn else rows_now).astype(F32)
        for master, rows_now, turn, side in zip(masters, ortho, sideways, full_sides)
    )

    first_new = BETA_ONE * gain_first + (1.0 - BETA_ONE) * gain_grad
    second_new = BETA_TWO * gain_second + (1.0 - BETA_TWO) * gain_grad * gain_grad
    corr_one = 1.0 - BETA_ONE**ADAM_STEP
    corr_two = 1.0 - BETA_TWO**ADAM_STEP
    gains_new = norm_gains - LR_GAIN * (first_new / corr_one) / (
        jnp.sqrt(second_new / corr_two) + EPS_ADAM
    )
    return (
        block_out,
        input_grad,
        *(grad for grad, _, _ in small + big),
        *(moment for _, moment, _ in small + big),
        *new_weights,
        first_new,
        second_new,
        gains_new,
    )


def solution(mesh):
    dp_size, fsdp_size = mesh.devices.shape
    fine_mesh = Mesh(
        mesh.devices.reshape(PLANES, dp_size // (PLANES * CORES), CORES, fsdp_size),
        ("z", "y", "core", "fsdp"),
    )
    dp = ("z", "y", "core")
    tokens = P(dp, "fsdp", None)
    by_row = P(EVERYWHERE, None)
    by_col = P(None, EVERYWHERE)
    matrices = (by_col, by_row, by_row, by_row, by_col, by_col, by_row)
    return jax.shard_map(
        per_device,
        mesh=fine_mesh,
        in_specs=(tokens, tokens, P(dp, None), *matrices, *matrices, P(), P(), P()),
        out_specs=(tokens, tokens, *matrices, *matrices, *matrices, P(), P(), P()),
        check_vma=False,
    )
```

```python
import functools
import math

import jax
import jax.numpy as jnp
from jax import lax
from jax.experimental import pallas as pl
from jax.experimental.pallas import tpu as pltpu
from jax.sharding import Mesh
from jax.sharding import PartitionSpec as P

MODEL_WIDTH = 2048
QUERY_HEADS = 16
KEY_VALUE_HEADS = 8
HEAD_SIZE = 128
FF = 6144
ADAM_STEP = 10

EPS_NORM = 1e-06
THETA = 1000000.0
NEG_FILL = -1e30
MOMENTUM = 0.95
NS_A = 3.4445
NS_B = -4.775
NS_C = 2.0315
NS_EPS = 1e-07
LR_MUON = 0.2
DECAY_MUON = 0.01
LR_GAIN = 0.5
BETA_ONE = 0.9
BETA_TWO = 0.95
EPS_ADAM = 1e-08

CORES = 2
PLANES = 4
KV_WIDTH = KEY_VALUE_HEADS * HEAD_SIZE
BF16 = jnp.bfloat16
F32 = jnp.float32
SHARDS = ("z", "y", "fsdp")
PLANE_ROWS = ("z", "y")
EVERYWHERE = ("z", "y", "core", "fsdp")


def rms_scale(values, gain):
    return values * lax.rsqrt(jnp.mean(values * values, axis=-1, keepdims=True) + EPS_NORM) * gain


def rope_tables(positions, head_width):
    half_width = head_width // 2
    freq = jnp.exp(
        -(2.0 * jnp.arange(half_width, dtype=jnp.float32) / head_width) * math.log(THETA)
    )
    angle = positions.astype(jnp.float32)[..., None] * freq
    cosine = jnp.cos(angle)
    sine = jnp.sin(angle)
    return jnp.concatenate([cosine, cosine], -1), jnp.concatenate([-sine, sine], -1)


def dot_nn(left, right):
    return lax.dot_general(left, right, (((1,), (0,)), ((), ())), preferred_element_type=F32)


def dot_nt(left, right):
    return lax.dot_general(left, right, (((1,), (1,)), ((), ())), preferred_element_type=F32)


def dot_tn(left, right):
    return lax.dot_general(left, right, (((0,), (0,)), ((), ())), preferred_element_type=F32)


def head_chain(head, gain, cosine, sine):
    scaled = head * lax.rsqrt(jnp.mean(head * head, axis=-1, keepdims=True) + EPS_NORM) * gain
    return scaled * cosine + pltpu.roll(scaled, HEAD_SIZE // 2, 1) * sine


def head_chain_back(head, gain, cosine, sine, grad):
    grad = grad * cosine + pltpu.roll(grad * sine, HEAD_SIZE // 2, 1)
    scale = lax.rsqrt(jnp.mean(head * head, axis=-1, keepdims=True) + EPS_NORM)
    unit = head * scale
    d_gain = jnp.sum(grad * unit, axis=0, keepdims=True)
    grad = grad * gain
    return scale * (grad - unit * jnp.mean(grad * unit, axis=-1, keepdims=True)), d_gain


def key_value_kernel(near_ref, far_ref, gain_ref, cos_ref, sin_ref, proj_ref, low_ref):
    proj = near_ref[...] + far_ref[...].astype(F32)
    proj_ref[...] = proj
    is_key = pl.program_id(0) < KEY_VALUE_HEADS

    @pl.when(is_key)
    def _():
        low_ref[...] = head_chain(proj, gain_ref[...], cos_ref[...], sin_ref[...]).astype(BF16)

    @pl.when(jnp.logical_not(is_key))
    def _():
        low_ref[...] = proj.astype(BF16)


def key_value_back_kernel(grad_ref, proj_ref, gain_ref, cos_ref, sin_ref, low_ref, d_gain_ref):
    head = pl.program_id(0)

    @pl.when(head == 0)
    def _():
        d_gain_ref[...] = jnp.zeros_like(d_gain_ref)

    @pl.when(head < KEY_VALUE_HEADS)
    def _():
        d_proj, d_gain = head_chain_back(
            proj_ref[...], gain_ref[...], cos_ref[...], sin_ref[...], grad_ref[0]
        )
        low_ref[...] = d_proj.astype(BF16)
        d_gain_ref[...] += d_gain

    @pl.when(head >= KEY_VALUE_HEADS)
    def _():
        low_ref[...] = grad_ref[0].astype(BF16)


def attention_weights(q_ref, k_ref, mask_ref, gain_ref, cos_ref, sin_ref):
    query = head_chain(q_ref[...], gain_ref[...], cos_ref[0], sin_ref[0]).astype(BF16)
    scores = dot_nt(k_ref[0], query)
    weights = jnp.exp2(scores * (HEAD_SIZE ** (-0.5) * math.log2(math.e)))
    return query, weights * mask_ref[0].astype(F32)


def attention_kernel(
    q_ref, k_ref, v_ref, mask_ref, gain_ref, cos_ref, sin_ref, out_ref, out_turned_ref
):
    _, weights = attention_weights(q_ref, k_ref, mask_ref, gain_ref, cos_ref, sin_ref)
    total = jnp.sum(weights, axis=0, keepdims=True)
    out = dot_tn(v_ref[0], weights.astype(BF16)) * (1.0 / total)
    out_turned_ref[...] = out.astype(BF16)
    out_ref[...] = out.T.astype(BF16)


def attention_back_kernel(
    q_ref, k_ref, v_ref, mask_ref, gain_ref, cos_ref, sin_ref, grad_ref,
    *refs,
):
    q_low_ref, q_low_turned_ref, d_kv_ref, d_gain_ref = refs[-4:]

    @pl.when(pl.program_id(0) == 0)
    def _():
        d_gain_ref[...] = jnp.zeros_like(d_gain_ref)

    query, weights = attention_weights(q_ref, k_ref, mask_ref, gain_ref, cos_ref, sin_ref)
    grad = grad_ref[...]
    probs = weights * (1.0 / jnp.sum(weights, axis=0, keepdims=True))
    d_probs = dot_nt(v_ref[0], grad)
    delta = jnp.sum(probs * d_probs, axis=0, keepdims=True)
    d_scores = (probs * (d_probs - delta)).astype(BF16)
    d_value = dot_nn(probs.astype(BF16), grad).astype(BF16)
    d_key = (dot_nn(d_scores, query) * HEAD_SIZE ** (-0.5)).astype(BF16)

    d_kv_ref[0] = d_key
    d_kv_ref[1] = d_value
    d_query = dot_tn(k_ref[0], d_scores).T * HEAD_SIZE ** (-0.5)
    d_proj, d_gain = head_chain_back(
        q_ref[...], gain_ref[...], cos_ref[0], sin_ref[0], d_query
    )
    q_low_ref[...] = d_proj.astype(BF16)
    q_low_turned_ref[...] = d_proj.T.astype(BF16)
    d_gain_ref[...] += d_gain


def swiglu_kernel(two_ref, cot_ref, gate_ref, up_ref, down_ref, *out_refs):
    width = two_ref.shape[1]
    two = two_ref[...]
    gate = dot_nt(two, gate_ref[...].reshape(-1, width))
    up = dot_nt(two, up_ref[...].reshape(-1, width))
    d_hidden = dot_nt(cot_ref[...], down_ref[...].reshape(-1, width))
    sig = 1.0 / (1.0 + jnp.exp(-gate))
    silu = gate * sig
    results = (silu * up, d_hidden * up * sig * (1.0 + gate * (1.0 - sig)), d_hidden * silu)
    for result, out_ref, turned_ref in zip(results, out_refs[:3], out_refs[3:]):
        low = result.astype(BF16)
        out_ref[...] = low
        turned_ref[...] = low.T


def back_to_width_kernel(count, *refs):
    lefts, rights, out_ref = refs[:count], refs[count : 2 * count], refs[-1]
    width = out_ref.shape[1]
    total = 0.0
    for left, right in zip(lefts, rights):
        if split_by_y(right.shape[2]):
            half = left.shape[1] // CORES
            for y in range(CORES):
                rows = right[:, y].reshape(-1, width)
                total = total + dot_nn(left[:, y * half : (y + 1) * half], rows)
        else:
            total = total + dot_nn(left[...], right[...].reshape(-1, width))
    out_ref[...] = total.astype(BF16)


def weight_grad_kernel(place_ref, left_ref, right_ref, out_ref):
    out_ref[...] = dot_nn(left_ref[...], right_ref[...]).astype(BF16)


def chain_kernel(start_ref, gram_ref, bend_ref, out_ref, first_ref, product_ref, one_ref, two_ref):
    width = start_ref.shape[1]
    tile = 512

    def columns(body):
        @pl.loop(0, width // tile)
        def _(step):
            body(pl.ds(pl.multiple_of(step * tile, tile), tile))

    def times_p(rows_ref, cols):
        return NS_A * rows_ref[:, cols].astype(F32) + dot_nn(rows_ref[...], bend_ref[:, cols])

    def to_first(cols):
        first_ref[:, cols] = times_p(start_ref, cols).astype(BF16)

    def bent_first(cols):
        one_ref[:, cols] = times_p(first_ref, cols).astype(BF16)

    def by_gram(cols):
        two_ref[:, cols] = dot_nn(one_ref[...], gram_ref[:, cols]).astype(BF16)

    def to_product(cols):
        product_ref[:, cols] = times_p(two_ref, cols).astype(BF16)

    def bent_product(cols):
        one_ref[:, cols] = times_p(product_ref, cols).astype(BF16)

    def finish(cols):
        again = times_p(two_ref, cols)
        out_ref[:, cols] = (
            NS_A * first_ref[:, cols].astype(F32)
            + NS_B * product_ref[:, cols].astype(F32)
            + NS_C * again
        ).astype(BF16)

    for body in (to_first, bent_first, by_gram, to_product, bent_product, by_gram, finish):
        columns(body)


def shaped(shape, dtype):
    return jax.ShapeDtypeStruct(shape, dtype)


SMALL = pl.CostEstimate(flops=1, bytes_accessed=1, transcendentals=0)


def limits(mebibytes):
    return pltpu.CompilerParams(vmem_limit_bytes=mebibytes * 1024 * 1024)


def key_value_chain(near, far, gain, cosine, sine):
    rows = near.shape[0]
    block = pl.BlockSpec((rows, HEAD_SIZE), lambda head: (0, head))
    fixed = pl.BlockSpec((rows, HEAD_SIZE), lambda head: (0, 0))
    one = pl.BlockSpec((1, HEAD_SIZE), lambda head: (0, 0))
    return pl.pallas_call(
        key_value_kernel,
        grid=(2 * KEY_VALUE_HEADS,),
        in_specs=[block, block, one, fixed, fixed],
        out_specs=[block, block],
        out_shape=[shaped(near.shape, F32), shaped(near.shape, BF16)],
        compiler_params=limits(16),
        cost_estimate=SMALL,
        name="key_value_chain",
    )(near, far, gain, cosine, sine)


def key_value_back(grad, proj, gain, cosine, sine):
    rows = proj.shape[0]
    heads = KEY_VALUE_HEADS
    block = pl.BlockSpec((rows, HEAD_SIZE), lambda head: (0, head))
    split = pl.BlockSpec((1, rows, HEAD_SIZE), lambda head: (head // heads, 0, head % heads))
    fixed = pl.BlockSpec((rows, HEAD_SIZE), lambda head: (0, 0))
    one = pl.BlockSpec((1, HEAD_SIZE), lambda head: (0, 0))
    return pl.pallas_call(
        key_value_back_kernel,
        grid=(2 * heads,),
        in_specs=[split, block, one, fixed, fixed],
        out_specs=[block, one],
        out_shape=[shaped(proj.shape, BF16), shaped((1, HEAD_SIZE), F32)],
        compiler_params=limits(16),
        cost_estimate=SMALL,
        name="key_value_back",
    )(grad, proj, gain, cosine, sine)


def attention_specs(rows, keys, heads):
    return [
        pl.BlockSpec((rows, HEAD_SIZE), lambda seq, head: (seq, head)),
        pl.BlockSpec((1, keys, HEAD_SIZE), lambda seq, head: (seq, 0, head)),
        pl.BlockSpec((1, keys, HEAD_SIZE), lambda seq, head: (seq, 0, heads + head)),
        pl.BlockSpec((1, keys, rows), lambda seq, head: (seq, 0, 0)),
        pl.BlockSpec((1, HEAD_SIZE), lambda seq, head: (0, 0)),
        pl.BlockSpec((1, rows, HEAD_SIZE), lambda seq, head: (seq, 0, 0)),
        pl.BlockSpec((1, rows, HEAD_SIZE), lambda seq, head: (seq, 0, 0)),
    ]


def attention(q_proj, kv, mask, gain, cosine, sine):
    sequences, keys, rows = mask.shape
    heads = q_proj.shape[1] // HEAD_SIZE
    specs = attention_specs(rows, keys, heads)
    return pl.pallas_call(
        attention_kernel,
        grid=(sequences, heads),
        in_specs=specs,
        out_specs=[specs[0], pl.BlockSpec((HEAD_SIZE, rows), lambda seq, head: (head, seq))],
        out_shape=[shaped(q_proj.shape, BF16), shaped(q_proj.shape[::-1], BF16)],
        compiler_params=limits(40),
        cost_estimate=SMALL,
        name="attention",
    )(q_proj, kv, kv, mask, gain, cosine, sine)


def attention_back(q_proj, kv, mask, gain, cosine, sine, grad, seq, others):
    _, keys, rows = mask.shape
    heads = q_proj.shape[1] // HEAD_SIZE
    specs = [
        pl.BlockSpec((rows, HEAD_SIZE), lambda head: (seq, head)),
        pl.BlockSpec((1, keys, HEAD_SIZE), lambda head: (seq, 0, head)),
        pl.BlockSpec((1, keys, HEAD_SIZE), lambda head: (seq, 0, heads + head)),
        pl.BlockSpec((1, keys, rows), lambda head: (seq, 0, 0)),
        pl.BlockSpec((1, HEAD_SIZE), lambda head: (0, 0)),
        pl.BlockSpec((1, rows, HEAD_SIZE), lambda head: (seq, 0, 0)),
        pl.BlockSpec((1, rows, HEAD_SIZE), lambda head: (seq, 0, 0)),
    ]
    return pl.pallas_call(
        attention_back_kernel,
        grid=(heads,),
        in_specs=[*specs, specs[0]] + [pl.BlockSpec(memory_space=pl.ANY)] * len(others),
        out_specs=[
            specs[0],
            pl.BlockSpec((HEAD_SIZE, rows), lambda head: (head, seq)),
            pl.BlockSpec((2, keys, HEAD_SIZE), lambda head: (0, 0, head)),
            specs[4],
        ],
        out_shape=[
            shaped(q_proj.shape, BF16),
            shaped(q_proj.shape[::-1], BF16),
            shaped((2, keys, heads * HEAD_SIZE), BF16),
            shaped((1, HEAD_SIZE), F32),
        ],
        input_output_aliases={8 + place: place for place in range(len(others))},
        compiler_params=limits(48),
        cost_estimate=SMALL,
        name="attention_back",
    )(q_proj, kv, kv, mask, gain, cosine, sine, grad, *others)


def split_by_y(block_rows):
    return (PLANES * block_rows) % 128 == 0


def swiglu_both_ways(two, cot, ff):
    tokens, width = two.shape
    _, _, block_rows, _ = ff[0].shape
    ys = 1 if split_by_y(block_rows) else CORES
    tile = min(512, tokens)
    ff_tile = PLANES * ys * block_rows
    row_block = pl.BlockSpec((tile, width), lambda col, row: (row, 0))
    out_block = pl.BlockSpec((tile, ff_tile), lambda col, row: (row, col))
    turned_block = pl.BlockSpec((ff_tile, tile), lambda col, row: (col, row))
    weights = pl.BlockSpec((PLANES, ys, block_rows, width), lambda col, row: (0, col, 0, 0))
    columns = PLANES * CORES * block_rows
    return pl.pallas_call(
        swiglu_kernel,
        grid=(CORES // ys, tokens // tile),
        in_specs=[row_block, row_block] + [weights] * 3,
        out_specs=[out_block] * 3 + [turned_block] * 3,
        out_shape=[shaped((tokens, columns), BF16)] * 3 + [shaped((columns, tokens), BF16)] * 3,
        compiler_params=limits(60),
        cost_estimate=SMALL,
        name="swiglu_both_ways",
    )(two, cot, *ff)


def back_to_width(lefts, ff, first_row, rows):
    _, _, block_rows, width = ff[0].shape
    columns = PLANES * CORES * block_rows
    tile = min(256, rows)
    first = first_row // tile
    left_block = pl.BlockSpec((tile, columns), lambda row: (first + row, 0))
    weights = pl.BlockSpec(ff[0].shape, lambda row: (0, 0, 0, 0))
    return pl.pallas_call(
        functools.partial(back_to_width_kernel, len(lefts)),
        grid=(rows // tile,),
        in_specs=[left_block] * len(lefts) + [weights] * len(lefts),
        out_specs=pl.BlockSpec((tile, width), lambda row: (row, 0)),
        out_shape=shaped((rows, width), BF16),
        compiler_params=limits(56),
        cost_estimate=SMALL,
        name="back_to_width",
    )(*lefts, *ff)


def weight_grad(left_turned, right, place, parts):
    rows = left_turned.shape[0] // parts
    tokens, width = right.shape
    tile = min(512, width)
    return pl.pallas_call(
        weight_grad_kernel,
        grid_spec=pltpu.PrefetchScalarGridSpec(
            num_scalar_prefetch=1,
            grid=(width // tile,),
            in_specs=[
                pl.BlockSpec((rows, tokens), lambda col, place_ref: (place_ref[0], 0)),
                pl.BlockSpec((tokens, tile), lambda col, place_ref: (0, col)),
            ],
            out_specs=pl.BlockSpec((rows, tile), lambda col, place_ref: (0, col)),
        ),
        out_shape=shaped((rows, width), BF16),
        compiler_params=limits(40),
        cost_estimate=SMALL,
        name="weight_grad",
    )(jnp.asarray(place, jnp.int32).reshape(1), left_turned, right)


def times_columns_kernel(left_ref, right_ref, out_ref):
    out_ref[...] = dot_nn(left_ref[...], right_ref[...]).astype(BF16)


def times_columns(left, right, first_column, width):
    rows, depth = left.shape
    tile = min(512, width)
    first = first_column // tile
    return pl.pallas_call(
        times_columns_kernel,
        grid=(width // tile,),
        in_specs=[
            pl.BlockSpec((rows, depth), lambda col: (0, 0)),
            pl.BlockSpec((depth, tile), lambda col: (0, first + col)),
        ],
        out_specs=pl.BlockSpec((rows, tile), lambda col: (0, col)),
        out_shape=shaped((rows, width), BF16),
        compiler_params=limits(40),
        cost_estimate=SMALL,
        name="times_columns",
    )(left, right)


def bend_kernel(gram_ref, tile_ref, out_ref):
    square = dot_nn(gram_ref[...], tile_ref[...])
    out_ref[...] = (NS_B * tile_ref[...].astype(F32) + NS_C * square).astype(BF16)


def bend_of(gram):
    width = gram.shape[0]
    tile = 512
    return pl.pallas_call(
        bend_kernel,
        grid=(width // tile,),
        in_specs=[
            pl.BlockSpec((width, width), lambda col: (0, 0)),
            pl.BlockSpec((width, tile), lambda col: (0, col)),
        ],
        out_specs=pl.BlockSpec((width, tile), lambda col: (0, col)),
        out_shape=shaped(gram.shape, BF16),
        compiler_params=limits(48),
        cost_estimate=SMALL,
        name="bend_of",
    )(gram, gram)


def times_rows_kernel(left_ref, right_ref, out_ref):
    out_ref[...] = dot_nt(left_ref[...], right_ref[...]).astype(BF16)


def times_rows(left, right, place):
    rows, depth = left.shape
    columns = right.shape[0]
    tile = min(256, columns)
    return pl.pallas_call(
        times_rows_kernel,
        grid=(columns // tile,),
        in_specs=[
            pl.BlockSpec((rows, depth), lambda col: (0, 0)),
            pl.BlockSpec((tile, depth), lambda col: (col, place)),
        ],
        out_specs=pl.BlockSpec((rows, tile), lambda col: (0, col)),
        out_shape=shaped((rows, columns), BF16),
        compiler_params=limits(40),
        cost_estimate=SMALL,
        name="times_rows",
    )(left, right)


def chain(start, gram, bend):
    rows, width = start.shape
    whole = pl.BlockSpec((width, width), lambda: (0, 0), pipeline_mode=pl.Buffered(1))
    block = pl.BlockSpec((rows, width), lambda: (0, 0), pipeline_mode=pl.Buffered(1))
    return pl.pallas_call(
        chain_kernel,
        grid=(),
        in_specs=[block, whole, whole],
        out_specs=pl.BlockSpec((rows, width), lambda: (0, 0)),
        out_shape=shaped(start.shape, BF16),
        scratch_shapes=[pltpu.VMEM(start.shape, BF16)] * 4,
        compiler_params=limits(56),
        cost_estimate=SMALL,
        name="chain",
    )(start, gram, bend)


def after(value, *earlier):
    return lax.optimization_barrier((value, earlier))[0]


def shifted(step, count):
    return [(src, (src + step) % count) for src in range(count)]


def swap(value, axis_name="core"):
    return lax.ppermute(value, axis_name, shifted(1, CORES))


def with_partner(value):
    return jnp.concatenate([value, swap(value)], axis=0)


def ring_blocks(value, axis_name, count):
    return [value] + [
        lax.ppermute(value, axis_name, shifted(step, count)) for step in range(1, count)
    ]


def ring_send(blocks, axis_name, count):
    return [
        lax.ppermute(blocks[step].astype(BF16), axis_name, shifted(-step, count))
        for step in range(1, count)
    ]


def add_all(own, arrived):
    for term in arrived:
        own = own + term.astype(F32)
    return own


def pick(blocks, index, axis=0):
    return lax.dynamic_index_in_dim(blocks, index, axis, keepdims=False)


def gather_rows(shard, axes):
    return lax.all_gather(shard, axes, axis=0, tiled=True)


def scatter_blocks(blocks, axis_name):
    count = blocks.shape[0]
    here = lax.axis_index(axis_name)
    arrived = [
        lax.ppermute(pick(blocks, (here + step) % count), axis_name, shifted(step, count))
        for step in range(1, count)
    ]
    return pick(blocks, here), arrived


def ff_grad_half(left_turned, right, block_rows, y):
    shape = (PLANES, block_rows, right.shape[1])
    if split_by_y(block_rows):
        return weight_grad(left_turned, right, y, CORES).reshape(shape)
    full = weight_grad(left_turned, right, 0, 1)
    return pick(full.reshape(PLANES, CORES, block_rows, -1), y, 1)


def halves_over_y(partials):
    here = lax.axis_index("y")
    split = [value.reshape(PLANES, CORES, -1, value.shape[-1]) for value in partials]
    sent = jnp.concatenate([pick(value, 1 - here, 1) for value in split], axis=-1)
    kept = [pick(value, here, 1) for value in split]
    return kept, swap(sent, "y"), sent


def chunks_over_z(kept, arrived):
    here = lax.axis_index("z")

    def chunk(step):
        plane = (here + step) % PLANES
        near = jnp.concatenate([pick(value, plane) for value in kept], axis=-1)
        return near.astype(F32) + pick(arrived, plane).astype(F32)

    own = chunk(0)
    sent = [chunk(step).astype(BF16) for step in range(1, PLANES)]
    return own, [
        lax.ppermute(value, "z", shifted(step + 1, PLANES)) for step, value in enumerate(sent)
    ], sent


def sum_everywhere(value):
    return jnp.sum(lax.all_gather(value, EVERYWHERE, axis=0, tiled=False), axis=0)


def to_planes(chunks):
    here = lax.axis_index("z")
    arrived = [pick(chunks, here)]
    for step in range(1, PLANES):
        arrived.append(
            lax.ppermute(pick(chunks, (here + step) % PLANES), "z", shifted(step, PLANES))
        )
    return jnp.stack(arrived)


def from_planes(arrived):
    here = lax.axis_index("z")
    back = [arrived[0]]
    for step in range(1, PLANES):
        back.append(lax.ppermute(arrived[step], "z", shifted(-step, PLANES)))
    back = jnp.stack(back)
    return [pick(back, (chunk - here) % PLANES) for chunk in range(PLANES)]


def normalized(update, update_gram, halves):
    width = update.shape[1]
    block = 128
    index = jnp.arange(block)
    diagonal = jnp.stack(
        [
            update_gram[at : at + block, at : at + block].astype(F32)
            for at in range(0, width, block)
        ]
    )
    diagonal = jnp.sum(
        jnp.where(index[:, None] == index[None, :], diagonal, 0.0), axis=(1, 2)
    )
    low_half = jnp.sum(diagonal[: width // block // 2])
    high_half = jnp.sum(diagonal[width // block // 2 :])
    both = low_half + high_half
    squares = jnp.stack([jnp.where(halves, low_half, both), jnp.where(halves, high_half, both)])
    inverse = jnp.repeat(1.0 / (jnp.sqrt(squares) + NS_EPS), width // 2)
    side = jnp.arange(width) < width // 2
    kept = jnp.logical_not(halves) | (side[:, None] == side[None, :])
    start = (update.astype(F32) * inverse).astype(BF16)
    gram = update_gram.astype(F32) * inverse[:, None] * inverse[None, :]
    return start, jnp.where(kept, gram, 0.0).astype(BF16)


def per_device(
    inputs,
    cotangent,
    segments,
    w_query,
    key_weight_master,
    value_weight_master,
    w_output,
    w_gate,
    w_up,
    w_down,
    moment_query,
    moment_key,
    moment_value,
    moment_output,
    moment_gate,
    moment_up,
    moment_down,
    norm_gains,
    gain_first,
    gain_second,
):
    rows = inputs.shape[1]
    complete_rows = segments.shape[1]
    ring = lax.axis_size("fsdp")
    place = lax.axis_index("fsdp")
    core = lax.axis_index("core")
    gain_attn = norm_gains[:MODEL_WIDTH]
    gain_mlp = norm_gains[MODEL_WIDTH : 2 * MODEL_WIDTH]
    gain_query = norm_gains[2 * MODEL_WIDTH : 2 * MODEL_WIDTH + HEAD_SIZE]
    gain_key = norm_gains[2 * MODEL_WIDTH + HEAD_SIZE :]

    attention_rows = gather_rows(
        jnp.concatenate(
            [
                key_weight_master.astype(BF16),
                value_weight_master.astype(BF16),
                w_query.astype(BF16).T,
                w_output.astype(BF16),
            ],
            axis=1,
        ),
        SHARDS,
    )
    key_value_rows = attention_rows[:, :MODEL_WIDTH]
    query_rows = attention_rows[:, MODEL_WIDTH : 2 * MODEL_WIDTH]
    output_rows = attention_rows[:, 2 * MODEL_WIDTH :]
    gate_ff, up_ff, down_ff = (
        gather_rows(shard[None], PLANE_ROWS).reshape(PLANES, CORES, *shard.shape)
        for shard in (w_gate.astype(BF16).T, w_up.astype(BF16).T, w_down.astype(BF16))
    )

    masters = (w_query, key_weight_master, value_weight_master, w_output, w_gate, w_up, w_down)
    moments = (
        moment_query,
        moment_key,
        moment_value,
        moment_output,
        moment_gate,
        moment_up,
        moment_down,
    )
    full_sides = (MODEL_WIDTH,) * 4 + (FF,) * 3
    sideways = (True, False, False, False, True, True, False)

    def updated(shard, idx):
        grad = shard.T if sideways[idx] else shard
        moment = MOMENTUM * moments[idx] + grad
        update = grad + MOMENTUM * moment
        return grad, moment, (update.T if sideways[idx] else update).astype(BF16)

    both_segments = with_partner(segments)
    row_idx = jnp.arange(complete_rows, dtype=jnp.int32)
    boundary = jnp.concatenate(
        [
            jnp.ones((CORES, 1), dtype=bool),
            both_segments[:, 1:] != both_segments[:, :-1],
        ],
        axis=1,
    )
    doc_start = lax.cummax(jnp.where(boundary, row_idx[None, :], 0), axis=1)
    first_row = place * rows
    positions = lax.dynamic_slice_in_dim(row_idx[None, :] - doc_start, first_row, rows, 1)
    cosine_table, sine_table = rope_tables(positions, HEAD_SIZE)
    query_segments = lax.dynamic_slice_in_dim(both_segments, first_row, rows, 1)
    query_pos = first_row + jnp.arange(rows, dtype=jnp.int32)
    key_starts = [((place - step) % ring) * rows for step in range(ring)]
    key_pos = jnp.concatenate([at + jnp.arange(rows, dtype=jnp.int32) for at in key_starts])
    key_segments = jnp.concatenate(
        [lax.dynamic_slice_in_dim(both_segments, at, rows, 1) for at in key_starts], axis=1
    )
    mask = (
        (key_pos[None, :, None] <= query_pos[None, None, :])
        & (key_segments[:, :, None] == query_segments[:, None, :])
    ).astype(BF16)

    residual = inputs.astype(F32).reshape(rows, MODEL_WIDTH)
    normed = rms_scale(residual, gain_attn).astype(BF16)
    both_normed = with_partner(normed)
    cotangent_rows = cotangent.reshape(rows, MODEL_WIDTH)
    pair_rows = CORES * rows

    def own_columns(values):
        split = values.reshape(values.shape[0], -1, CORES, HEAD_SIZE)
        return pick(split, core, 2).reshape(values.shape[0], MODEL_WIDTH // CORES)

    own_normed = own_columns(both_normed)
    kv_sent = dot_nn(own_normed[rows:], key_value_rows).astype(BF16)
    kv_near = dot_nn(own_normed[:rows], key_value_rows)
    q_proj = dot_nt(both_normed, query_rows)
    kv_proj, kv_low = key_value_chain(
        kv_near, swap(kv_sent), gain_key[None], cosine_table[0], sine_table[0]
    )
    own_kv = after(jnp.concatenate(ring_blocks(kv_low, "fsdp", ring), axis=0), q_proj)
    both_kv = with_partner(own_kv).reshape(CORES, complete_rows, 2 * KV_WIDTH)
    attention_inputs = (q_proj, both_kv, mask, gain_query[None], cosine_table, sine_table)
    att_low, att_turned = attention(*attention_inputs)
    team_cotangent = with_partner(
        jnp.concatenate(ring_blocks(after(cotangent_rows, own_kv), "fsdp", ring), axis=0)
    )
    out_sent = dot_nn(att_low[rows:], output_rows).astype(BF16)
    out_near = dot_nn(att_low[:rows], output_rows)
    middle = residual + out_near + swap(out_sent).astype(F32)

    normed_two = rms_scale(middle, gain_mlp).astype(BF16)
    team_two = with_partner(jnp.concatenate(ring_blocks(normed_two, "fsdp", ring), axis=0))
    hidden, d_gate, d_up, hidden_turned, d_gate_turned, d_up_turned = swiglu_both_ways(
        team_two, team_cotangent, (gate_ff, up_ff, down_ff)
    )
    block_rows = gate_ff.shape[2]
    own_rows = ring * rows
    other_y = 1 - lax.axis_index("y")
    own_y = lax.axis_index("y")
    down_sent = ff_grad_half(hidden_turned, team_cotangent, block_rows, other_y)
    down_passed = swap(down_sent, "y")
    down_kept = ff_grad_half(
        after(hidden_turned, down_sent), team_cotangent, block_rows, own_y
    )
    back_grads = after((d_gate, d_up), down_kept)
    back_far = back_to_width(back_grads, (gate_ff, up_ff), own_rows, own_rows)
    back_near = back_to_width(after(back_grads, back_far), (gate_ff, up_ff), 0, own_rows)
    gate_turned = after(d_gate_turned, back_near)
    gate_sent = ff_grad_half(gate_turned, team_two, block_rows, other_y)
    gate_passed = swap(gate_sent, "y")
    down_own, down_chunks, down_chunks_sent = chunks_over_z(
        [down_kept], after(down_passed, gate_sent)
    )
    back_half = back_near.astype(F32) + swap(after(back_far, down_chunks_sent)).astype(F32)
    back_half = back_half.reshape(ring, rows, MODEL_WIDTH)
    back_arrived = ring_send([back_half[step] for step in range(ring)], "fsdp", ring)
    gate_kept = ff_grad_half(after(gate_turned, back_half), team_two, block_rows, own_y)
    up_turned = after(d_up_turned, gate_kept)
    up_sent = ff_grad_half(up_turned, team_two, block_rows, other_y)
    up_passed = swap(up_sent, "y")
    up_kept = ff_grad_half(after(up_turned, up_sent), team_two, block_rows, own_y)
    back_arrived, down_chunks, gate_passed = after(
        (back_arrived, down_chunks, gate_passed), up_kept
    )
    gate_own, gate_chunks, gate_chunks_sent = chunks_over_z([gate_kept], gate_passed)
    d_normed_two = add_all(after(back_half[0], gate_chunks_sent), back_arrived)
    second_back = jax.vjp(rms_scale, middle, gain_mlp)[1]
    d_mid_norm, d_gain_mlp = second_back(d_normed_two)
    d_middle = cotangent_rows.astype(F32) + d_mid_norm

    both_mid = with_partner(d_middle.astype(BF16))
    d_head = times_rows(both_mid, attention_rows, 2)
    output_grad = weight_grad(att_turned, after(both_mid, d_head), 0, 1)
    output_blocks = jnp.moveaxis(output_grad.reshape(PLANES * CORES, ring, -1, MODEL_WIDTH), 1, 0)
    output_own, output_arrived = scatter_blocks(output_blocks, "fsdp")
    d_head = after(d_head, output_grad)
    *far_parts, d_kv_far, far_gain = attention_back(*attention_inputs, d_head, 1, ())
    q_low, q_low_turned, d_kv_near, near_gain = attention_back(
        *attention_inputs, d_head, 0, far_parts
    )
    d_gain_query = (far_gain + near_gain)[0]
    query_grad = weight_grad(q_low_turned, both_normed, 0, 1)
    from_query = times_columns(after(q_low, query_grad), attention_rows, MODEL_WIDTH, MODEL_WIDTH)
    query_blocks = jnp.moveaxis(query_grad.reshape(PLANES * CORES, ring, -1, MODEL_WIDTH), 1, 0)
    query_own, query_arrived = scatter_blocks(query_blocks, "fsdp")
    up_passed, gate_chunks, output_arrived = after(
        (up_passed, gate_chunks, output_arrived), from_query
    )
    up_own, up_chunks, up_chunks_sent = chunks_over_z([up_kept], up_passed)
    d_kv_half = d_kv_near.astype(F32) + swap(after(d_kv_far, up_chunks_sent)).astype(F32)
    d_kv_half = d_kv_half.reshape(2, ring, rows, KV_WIDTH)
    d_kv_arrived = ring_send([d_kv_half[:, step] for step in range(ring)], "fsdp", ring)
    hidden = after(hidden, d_kv_half)
    down_far = back_to_width((hidden,), (down_ff,), own_rows, own_rows)
    down_near = back_to_width((after(hidden, down_far),), (down_ff,), 0, own_rows)
    gate_new = updated(add_all(gate_own, gate_chunks), 4)
    down_new = updated(add_all(down_own, down_chunks), 6)
    up_chunks, d_kv_arrived, query_arrived = after(
        (up_chunks, d_kv_arrived, query_arrived), down_near
    )
    big = [gate_new, updated(add_all(up_own, up_chunks), 5), down_new]
    slots = jnp.stack([new[2] for new in big] + [jnp.zeros_like(down_new[2])])
    big_mine = to_planes(slots).reshape(-1, MODEL_WIDTH)
    first_kept, first_passed, first_sent = halves_over_y(
        [
            add_all(output_own.astype(F32), output_arrived).astype(BF16),
            add_all(query_own.astype(F32), query_arrived).astype(BF16),
        ]
    )
    d_kv_total = add_all(d_kv_half[:, 0], d_kv_arrived)
    kv_low_grad, d_gain_key = key_value_back(
        d_kv_total, kv_proj, gain_key[None], cosine_table[0], sine_table[0]
    )
    d_gain_key = d_gain_key[0]
    both_kv_low = with_partner(kv_low_grad)
    key_value_grad = dot_tn(own_normed, both_kv_low).astype(BF16)
    key_value_blocks = jnp.moveaxis(
        key_value_grad.reshape(PLANES * CORES, ring, -1, MODEL_WIDTH), 1, 0
    )
    key_value_own, key_value_arrived = scatter_blocks(key_value_blocks, "fsdp")
    plane = lax.axis_index("z")
    in_plane = ("y", "core", "fsdp")
    big_mine, key_value_arrived, first_passed = lax.optimization_barrier(
        (big_mine, key_value_arrived, first_passed)
    )
    first_own, first_chunks, first_chunks_sent = chunks_over_z(first_kept, first_passed)
    kept, arrived, attention_passed = halves_over_y(
        [add_all(key_value_own.astype(F32), key_value_arrived).astype(BF16)]
    )
    big_gram = dot_tn(after(big_mine, attention_passed, first_chunks_sent), big_mine).astype(BF16)
    from_kv = times_rows(after(both_kv_low, big_gram), attention_rows, 0)
    big_gram = lax.psum(big_gram, in_plane)
    arrived, first_chunks = after((arrived, first_chunks), from_kv)
    last_own, last_chunks, last_chunks_sent = chunks_over_z(kept, arrived)
    from_kv = after(from_kv, last_chunks_sent)

    from_query = from_query[:rows].astype(F32) + swap(from_query[rows:]).astype(F32)
    kv_here = from_kv[:rows].reshape(rows, -1, HEAD_SIZE)
    kv_there = swap(from_kv[rows:]).reshape(rows, -1, HEAD_SIZE)
    from_kv_full = jnp.stack(
        [jnp.where(core == 0, kv_here, kv_there), jnp.where(core == 0, kv_there, kv_here)], axis=2
    ).reshape(rows, MODEL_WIDTH)
    d_normed = from_query + from_kv_full.astype(F32)
    first_back = jax.vjp(rms_scale, residual, gain_attn)[1]
    d_residual, d_gain_attn = first_back(d_normed)
    input_grad = (d_middle + d_residual).reshape(inputs.shape)
    down_half = (down_near.astype(F32) + swap(after(down_far, d_normed)).astype(F32)).reshape(
        ring, rows, MODEL_WIDTH
    )
    down_arrived = ring_send([down_half[step] for step in range(ring)], "fsdp", ring)
    gain_grad = jnp.concatenate([d_gain_attn, d_gain_mlp, d_gain_query, d_gain_key])

    last_chunks = after(last_chunks, input_grad)
    first_total = add_all(first_own, first_chunks)
    output_shard = first_total[:, :MODEL_WIDTH]
    query_shard = first_total[:, MODEL_WIDTH:]
    key_value_shard = add_all(last_own, last_chunks)
    small = [
        updated(query_shard, 0),
        updated(key_value_shard[:, :KV_WIDTH], 1),
        updated(key_value_shard[:, KV_WIDTH:], 2),
        updated(output_shard, 3),
    ]
    small_slots = jnp.stack(
        [
            small[0][2],
            jnp.concatenate([small[1][2], small[2][2]], axis=1),
            small[3][2],
            jnp.zeros_like(small[3][2]),
        ]
    )
    small_mine = to_planes(small_slots).reshape(-1, MODEL_WIDTH)
    whole = gather_rows(small_mine, in_plane)
    start, gram = normalized(big_mine, big_gram, jnp.bool_(False))
    turned = chain(start, after(gram, small_mine), bend_of(gram))
    turned, whole = lax.optimization_barrier((turned, whole))
    returned = from_planes(turned.reshape(PLANES, -1, MODEL_WIDTH))
    small_gram = dot_tn(whole, whole).astype(BF16)
    start, gram = normalized(small_mine, small_gram, plane == 1)
    turned, returned, down_arrived, gain_grad = lax.optimization_barrier(
        (chain(start, gram, bend_of(gram)), returned, down_arrived, sum_everywhere(gain_grad))
    )
    small_returned = from_planes(turned.reshape(small_slots.shape))
    block_out = (middle + add_all(down_half[0], down_arrived)).astype(BF16).reshape(inputs.shape)
    ortho = (
        small_returned[0],
        small_returned[1][:, :KV_WIDTH],
        small_returned[1][:, KV_WIDTH:],
        small_returned[2],
        *returned[:3],
    )
    new_weights = tuple(
        master * (1.0 - LR_MUON * DECAY_MUON)
        - LR_MUON * math.sqrt(side) * (rows_now.T if turn else rows_now).astype(F32)
        for master, rows_now, turn, side in zip(masters, ortho, sideways, full_sides)
    )

    first_new = BETA_ONE * gain_first + (1.0 - BETA_ONE) * gain_grad
    second_new = BETA_TWO * gain_second + (1.0 - BETA_TWO) * gain_grad * gain_grad
    corr_one = 1.0 - BETA_ONE**ADAM_STEP
    corr_two = 1.0 - BETA_TWO**ADAM_STEP
    gains_new = norm_gains - LR_GAIN * (first_new / corr_one) / (
        jnp.sqrt(second_new / corr_two) + EPS_ADAM
    )
    return (
        block_out,
        input_grad,
        *(grad for grad, _, _ in small + big),
        *(moment for _, moment, _ in small + big),
        *new_weights,
        first_new,
        second_new,
        gains_new,
    )


def solution(mesh):
    dp_size, fsdp_size = mesh.devices.shape
    fine_mesh = Mesh(
        mesh.devices.reshape(PLANES, dp_size // (PLANES * CORES), CORES, fsdp_size),
        ("z", "y", "core", "fsdp"),
    )
    dp = ("z", "y", "core")
    tokens = P(dp, "fsdp", None)
    by_row = P(EVERYWHERE, None)
    by_col = P(None, EVERYWHERE)
    matrices = (by_col, by_row, by_row, by_row, by_col, by_col, by_row)
    return jax.shard_map(
        per_device,
        mesh=fine_mesh,
        in_specs=(tokens, tokens, P(dp, None), *matrices, *matrices, P(), P(), P()),
        out_specs=(tokens, tokens, *matrices, *matrices, *matrices, P(), P(), P()),
        check_vma=False,
    )
```

```python
import functools
import math

import jax
import jax.numpy as jnp
from jax import lax
from jax.experimental import pallas as pl
from jax.experimental.pallas import tpu as pltpu
from jax.sharding import Mesh
from jax.sharding import PartitionSpec as P

MODEL_WIDTH = 2048
QUERY_HEADS = 16
KEY_VALUE_HEADS = 8
HEAD_SIZE = 128
FF = 6144
ADAM_STEP = 10

EPS_NORM = 1e-06
THETA = 1000000.0
NEG_FILL = -1e30
MOMENTUM = 0.95
NS_A = 3.4445
NS_B = -4.775
NS_C = 2.0315
NS_EPS = 1e-07
LR_MUON = 0.2
DECAY_MUON = 0.01
LR_GAIN = 0.5
BETA_ONE = 0.9
BETA_TWO = 0.95
EPS_ADAM = 1e-08

CORES = 2
PLANES = 4
GRAM_TILE = 512
KV_WIDTH = KEY_VALUE_HEADS * HEAD_SIZE
BF16 = jnp.bfloat16
F32 = jnp.float32
SHARDS = ("z", "y", "fsdp")
EVERYWHERE = ("z", "y", "core", "fsdp")


def rms_scale(values, gain):
    return values * lax.rsqrt(jnp.mean(values * values, axis=-1, keepdims=True) + EPS_NORM) * gain


def rope_tables(positions, head_width):
    half_width = head_width // 2
    freq = jnp.exp(
        -(2.0 * jnp.arange(half_width, dtype=jnp.float32) / head_width) * math.log(THETA)
    )
    angle = positions.astype(jnp.float32)[..., None] * freq
    cosine = jnp.cos(angle)
    sine = jnp.sin(angle)
    return jnp.concatenate([cosine, cosine], -1), jnp.concatenate([-sine, sine], -1)


def dot_nn(left, right):
    return lax.dot_general(left, right, (((1,), (0,)), ((), ())), preferred_element_type=F32)


def dot_nt(left, right):
    return lax.dot_general(left, right, (((1,), (1,)), ((), ())), preferred_element_type=F32)


def dot_tn(left, right):
    return lax.dot_general(left, right, (((0,), (0,)), ((), ())), preferred_element_type=F32)


def gram_pairs(width):
    count = width // GRAM_TILE
    return [(i, j) for i in range(count) for j in range(i, count)]


def head_chain(head, gain, cosine, sine):
    scaled = head * lax.rsqrt(jnp.mean(head * head, axis=-1, keepdims=True) + EPS_NORM) * gain
    return scaled * cosine + pltpu.roll(scaled, HEAD_SIZE // 2, 1) * sine


def head_chain_back(head, gain, cosine, sine, grad):
    grad = grad * cosine + pltpu.roll(grad * sine, HEAD_SIZE // 2, 1)
    scale = lax.rsqrt(jnp.mean(head * head, axis=-1, keepdims=True) + EPS_NORM)
    unit = head * scale
    d_gain = jnp.sum(grad * unit, axis=0, keepdims=True)
    grad = grad * gain
    return scale * (grad - unit * jnp.mean(grad * unit, axis=-1, keepdims=True)), d_gain


def key_value_kernel(near_ref, far_ref, gain_ref, cos_ref, sin_ref, proj_ref, low_ref):
    proj = near_ref[...] + far_ref[...].astype(F32)
    proj_ref[...] = proj
    is_key = pl.program_id(0) < KEY_VALUE_HEADS

    @pl.when(is_key)
    def _():
        low_ref[...] = head_chain(proj, gain_ref[...], cos_ref[...], sin_ref[...]).astype(BF16)

    @pl.when(jnp.logical_not(is_key))
    def _():
        low_ref[...] = proj.astype(BF16)


def key_value_back_kernel(grad_ref, proj_ref, gain_ref, cos_ref, sin_ref, low_ref, d_gain_ref):
    head = pl.program_id(0)

    @pl.when(head == 0)
    def _():
        d_gain_ref[...] = jnp.zeros_like(d_gain_ref)

    @pl.when(head < KEY_VALUE_HEADS)
    def _():
        d_proj, d_gain = head_chain_back(
            proj_ref[...], gain_ref[...], cos_ref[...], sin_ref[...], grad_ref[0]
        )
        low_ref[...] = d_proj.astype(BF16)
        d_gain_ref[...] += d_gain

    @pl.when(head >= KEY_VALUE_HEADS)
    def _():
        low_ref[...] = grad_ref[0].astype(BF16)


def attention_weights(q_ref, k_ref, mask_ref, gain_ref, cos_ref, sin_ref):
    query = head_chain(q_ref[...], gain_ref[...], cos_ref[0], sin_ref[0]).astype(BF16)
    scores = dot_nt(k_ref[0], query)
    weights = jnp.exp2(scores * (HEAD_SIZE ** (-0.5) * math.log2(math.e)))
    return query, weights * mask_ref[0].astype(F32)


def attention_kernel(
    q_ref, k_ref, v_ref, mask_ref, gain_ref, cos_ref, sin_ref, out_ref, out_turned_ref
):
    _, weights = attention_weights(q_ref, k_ref, mask_ref, gain_ref, cos_ref, sin_ref)
    total = jnp.sum(weights, axis=0, keepdims=True)
    out = dot_tn(v_ref[0], weights.astype(BF16)) * (1.0 / total)
    out_turned_ref[...] = out.astype(BF16)
    out_ref[...] = out.T.astype(BF16)


def attention_back_kernel(
    q_ref, k_ref, v_ref, mask_ref, gain_ref, cos_ref, sin_ref, grad_ref,
    *refs,
):
    q_low_ref, q_low_turned_ref, d_kv_ref, d_gain_ref = refs[-4:]

    @pl.when(pl.program_id(0) == 0)
    def _():
        d_gain_ref[...] = jnp.zeros_like(d_gain_ref)

    query, weights = attention_weights(q_ref, k_ref, mask_ref, gain_ref, cos_ref, sin_ref)
    grad = grad_ref[...]
    probs = weights * (1.0 / jnp.sum(weights, axis=0, keepdims=True))
    d_probs = dot_nt(v_ref[0], grad)
    delta = jnp.sum(probs * d_probs, axis=0, keepdims=True)
    d_scores = (probs * (d_probs - delta)).astype(BF16)
    d_value = dot_nn(probs.astype(BF16), grad).astype(BF16)
    d_key = (dot_nn(d_scores, query) * HEAD_SIZE ** (-0.5)).astype(BF16)

    d_kv_ref[0] = d_key
    d_kv_ref[1] = d_value
    d_query = dot_tn(k_ref[0], d_scores).T * HEAD_SIZE ** (-0.5)
    d_proj, d_gain = head_chain_back(
        q_ref[...], gain_ref[...], cos_ref[0], sin_ref[0], d_query
    )
    q_low_ref[...] = d_proj.astype(BF16)
    q_low_turned_ref[...] = d_proj.T.astype(BF16)
    d_gain_ref[...] += d_gain


def swiglu_kernel(two_ref, cot_ref, gate_ref, up_ref, down_ref, *out_refs):
    two = two_ref[...]
    gate = dot_nt(two, gate_ref[...])
    up = dot_nt(two, up_ref[...])
    d_hidden = dot_nt(cot_ref[...], down_ref[...])
    sig = 1.0 / (1.0 + jnp.exp(-gate))
    silu = gate * sig
    results = (silu * up, d_hidden * up * sig * (1.0 + gate * (1.0 - sig)), d_hidden * silu)
    for result, out_ref, turned_ref in zip(results, out_refs[:3], out_refs[3:]):
        low = result.astype(BF16)
        out_ref[...] = low
        turned_ref[...] = low.T


def back_to_width_kernel(count, *refs):
    lefts, rights, out_ref = refs[:count], refs[count : 2 * count], refs[-1]
    total = 0.0
    for left, right in zip(lefts, rights):
        total = total + dot_nn(left[...], right[...])
    out_ref[...] = total.astype(BF16)


def weight_grad_kernel(left_ref, right_ref, out_ref):
    out_ref[...] = dot_nn(left_ref[...], right_ref[...]).astype(BF16)


def gram_kernel(first_ref, second_ref, left_ref, right_ref, out_ref):
    out_ref[0] = dot_tn(left_ref[...], right_ref[...]).astype(BF16)


def muon_kernel(
    halves_ref, update_ref, packed_ref, row_ref, col_ref, out_ref,
    start_ref, gram_ref, bend_ref, first_ref, product_ref, one_ref, two_ref,
):
    width = update_ref.shape[1]
    tile = GRAM_TILE
    count = width // tile
    start_ref[...] = (update_ref[...].astype(F32) * row_ref[...]).astype(BF16)
    one_matrix = (1 - halves_ref[0]).astype(F32)

    def put(ref, i, j, value):
        ref[i * tile : (i + 1) * tile, j * tile : (j + 1) * tile] = value
        if i != j:
            ref[j * tile : (j + 1) * tile, i * tile : (i + 1) * tile] = value.T

    for place, (i, j) in enumerate(gram_pairs(width)):
        block = packed_ref[place].astype(F32) * col_ref[i * tile : (i + 1) * tile, :]
        block = block * row_ref[:, j * tile : (j + 1) * tile]
        if 2 * i < count <= 2 * j:
            block = block * one_matrix
        put(gram_ref, i, j, block.astype(BF16))
    for i, j in gram_pairs(width):
        rows, cols = slice(i * tile, (i + 1) * tile), slice(j * tile, (j + 1) * tile)
        square = dot_nn(gram_ref[rows, :], gram_ref[:, cols])
        put(bend_ref, i, j, (NS_B * gram_ref[rows, cols].astype(F32) + NS_C * square).astype(BF16))

    def columns(body):
        @pl.loop(0, count)
        def _(step):
            body(pl.ds(pl.multiple_of(step * tile, tile), tile))

    def times_p(rows_ref, cols):
        return NS_A * rows_ref[:, cols].astype(F32) + dot_nn(rows_ref[...], bend_ref[:, cols])

    def to_first(cols):
        first_ref[:, cols] = times_p(start_ref, cols).astype(BF16)

    def bent_first(cols):
        one_ref[:, cols] = times_p(first_ref, cols).astype(BF16)

    def by_gram(cols):
        two_ref[:, cols] = dot_nn(one_ref[...], gram_ref[:, cols]).astype(BF16)

    def to_product(cols):
        product_ref[:, cols] = times_p(two_ref, cols).astype(BF16)

    def bent_product(cols):
        one_ref[:, cols] = times_p(product_ref, cols).astype(BF16)

    def finish(cols):
        again = times_p(two_ref, cols)
        out_ref[:, cols] = (
            NS_A * first_ref[:, cols].astype(F32)
            + NS_B * product_ref[:, cols].astype(F32)
            + NS_C * again
        ).astype(BF16)

    for body in (to_first, bent_first, by_gram, to_product, bent_product, by_gram, finish):
        columns(body)


def shaped(shape, dtype):
    return jax.ShapeDtypeStruct(shape, dtype)


SMALL = pl.CostEstimate(flops=1, bytes_accessed=1, transcendentals=0)


def limits(mebibytes):
    return pltpu.CompilerParams(vmem_limit_bytes=mebibytes * 1024 * 1024)


def key_value_chain(near, far, gain, cosine, sine):
    rows = near.shape[0]
    block = pl.BlockSpec((rows, HEAD_SIZE), lambda head: (0, head))
    fixed = pl.BlockSpec((rows, HEAD_SIZE), lambda head: (0, 0))
    one = pl.BlockSpec((1, HEAD_SIZE), lambda head: (0, 0))
    return pl.pallas_call(
        key_value_kernel,
        grid=(2 * KEY_VALUE_HEADS,),
        in_specs=[block, block, one, fixed, fixed],
        out_specs=[block, block],
        out_shape=[shaped(near.shape, F32), shaped(near.shape, BF16)],
        compiler_params=limits(16),
        cost_estimate=SMALL,
        name="key_value_chain",
    )(near, far, gain, cosine, sine)


def key_value_back(grad, proj, gain, cosine, sine):
    rows = proj.shape[0]
    heads = KEY_VALUE_HEADS
    block = pl.BlockSpec((rows, HEAD_SIZE), lambda head: (0, head))
    split = pl.BlockSpec((1, rows, HEAD_SIZE), lambda head: (head // heads, 0, head % heads))
    fixed = pl.BlockSpec((rows, HEAD_SIZE), lambda head: (0, 0))
    one = pl.BlockSpec((1, HEAD_SIZE), lambda head: (0, 0))
    return pl.pallas_call(
        key_value_back_kernel,
        grid=(2 * heads,),
        in_specs=[split, block, one, fixed, fixed],
        out_specs=[block, one],
        out_shape=[shaped(proj.shape, BF16), shaped((1, HEAD_SIZE), F32)],
        compiler_params=limits(16),
        cost_estimate=SMALL,
        name="key_value_back",
    )(grad, proj, gain, cosine, sine)


def attention_specs(rows, keys, heads):
    return [
        pl.BlockSpec((rows, HEAD_SIZE), lambda seq, head: (seq, head)),
        pl.BlockSpec((1, keys, HEAD_SIZE), lambda seq, head: (seq, 0, head)),
        pl.BlockSpec((1, keys, HEAD_SIZE), lambda seq, head: (seq, 0, heads + head)),
        pl.BlockSpec((1, keys, rows), lambda seq, head: (seq, 0, 0)),
        pl.BlockSpec((1, HEAD_SIZE), lambda seq, head: (0, 0)),
        pl.BlockSpec((1, rows, HEAD_SIZE), lambda seq, head: (seq, 0, 0)),
        pl.BlockSpec((1, rows, HEAD_SIZE), lambda seq, head: (seq, 0, 0)),
    ]


def attention(q_proj, kv, mask, gain, cosine, sine):
    sequences, keys, rows = mask.shape
    heads = q_proj.shape[1] // HEAD_SIZE
    specs = attention_specs(rows, keys, heads)
    return pl.pallas_call(
        attention_kernel,
        grid=(sequences, heads),
        in_specs=specs,
        out_specs=[specs[0], pl.BlockSpec((HEAD_SIZE, rows), lambda seq, head: (head, seq))],
        out_shape=[shaped(q_proj.shape, BF16), shaped(q_proj.shape[::-1], BF16)],
        compiler_params=limits(40),
        cost_estimate=SMALL,
        name="attention",
    )(q_proj, kv, kv, mask, gain, cosine, sine)


def attention_back(q_proj, kv, mask, gain, cosine, sine, grad, seq, others):
    _, keys, rows = mask.shape
    heads = q_proj.shape[1] // HEAD_SIZE
    specs = [
        pl.BlockSpec((rows, HEAD_SIZE), lambda head: (seq, head)),
        pl.BlockSpec((1, keys, HEAD_SIZE), lambda head: (seq, 0, head)),
        pl.BlockSpec((1, keys, HEAD_SIZE), lambda head: (seq, 0, heads + head)),
        pl.BlockSpec((1, keys, rows), lambda head: (seq, 0, 0)),
        pl.BlockSpec((1, HEAD_SIZE), lambda head: (0, 0)),
        pl.BlockSpec((1, rows, HEAD_SIZE), lambda head: (seq, 0, 0)),
        pl.BlockSpec((1, rows, HEAD_SIZE), lambda head: (seq, 0, 0)),
    ]
    return pl.pallas_call(
        attention_back_kernel,
        grid=(heads,),
        in_specs=[*specs, specs[0]] + [pl.BlockSpec(memory_space=pl.ANY)] * len(others),
        out_specs=[
            specs[0],
            pl.BlockSpec((HEAD_SIZE, rows), lambda head: (head, seq)),
            pl.BlockSpec((2, keys, HEAD_SIZE), lambda head: (0, 0, head)),
            specs[4],
        ],
        out_shape=[
            shaped(q_proj.shape, BF16),
            shaped(q_proj.shape[::-1], BF16),
            shaped((2, keys, heads * HEAD_SIZE), BF16),
            shaped((1, HEAD_SIZE), F32),
        ],
        input_output_aliases={8 + place: place for place in range(len(others))},
        compiler_params=limits(48),
        cost_estimate=SMALL,
        name="attention_back",
    )(q_proj, kv, kv, mask, gain, cosine, sine, grad, *others)


def swiglu_both_ways(two, cot, gate, up, down):
    tokens, width = two.shape
    columns = gate.shape[0]
    tile = min(512, tokens)
    row_block = pl.BlockSpec((tile, width), lambda row: (row, 0))
    weights = pl.BlockSpec((columns, width), lambda row: (0, 0))
    return pl.pallas_call(
        swiglu_kernel,
        grid=(tokens // tile,),
        in_specs=[row_block, row_block] + [weights] * 3,
        out_specs=[pl.BlockSpec((tile, columns), lambda row: (row, 0))] * 3
        + [pl.BlockSpec((columns, tile), lambda row: (0, row))] * 3,
        out_shape=[shaped((tokens, columns), BF16)] * 3 + [shaped((columns, tokens), BF16)] * 3,
        compiler_params=limits(60),
        cost_estimate=SMALL,
        name="swiglu_both_ways",
    )(two, cot, gate, up, down)


def back_to_width(lefts, rights, first_row, rows):
    width = rights[0].shape[1]
    tile = min(256, rows)
    first = first_row // tile
    return pl.pallas_call(
        functools.partial(back_to_width_kernel, len(lefts)),
        grid=(rows // tile,),
        in_specs=[
            pl.BlockSpec((tile, left.shape[1]), lambda row: (first + row, 0)) for left in lefts
        ]
        + [pl.BlockSpec(right.shape, lambda row: (0, 0)) for right in rights],
        out_specs=pl.BlockSpec((tile, width), lambda row: (row, 0)),
        out_shape=shaped((rows, width), BF16),
        compiler_params=limits(56),
        cost_estimate=SMALL,
        name="back_to_width",
    )(*lefts, *rights)


def weight_grad(left_turned, right):
    rows, tokens = left_turned.shape
    width = right.shape[1]
    tile = min(512, width)
    return pl.pallas_call(
        weight_grad_kernel,
        grid=(width // tile,),
        in_specs=[
            pl.BlockSpec((rows, tokens), lambda col: (0, 0)),
            pl.BlockSpec((tokens, tile), lambda col: (0, col)),
        ],
        out_specs=pl.BlockSpec((rows, tile), lambda col: (0, col)),
        out_shape=shaped((rows, width), BF16),
        compiler_params=limits(40),
        cost_estimate=SMALL,
        name="weight_grad",
    )(left_turned, right)


def times_columns_kernel(left_ref, right_ref, out_ref):
    out_ref[...] = dot_nn(left_ref[...], right_ref[...]).astype(BF16)


def times_columns(left, right, first_column, width):
    rows, depth = left.shape
    tile = min(512, width)
    first = first_column // tile
    return pl.pallas_call(
        times_columns_kernel,
        grid=(width // tile,),
        in_specs=[
            pl.BlockSpec((rows, depth), lambda col: (0, 0)),
            pl.BlockSpec((depth, tile), lambda col: (0, first + col)),
        ],
        out_specs=pl.BlockSpec((rows, tile), lambda col: (0, col)),
        out_shape=shaped((rows, width), BF16),
        compiler_params=limits(40),
        cost_estimate=SMALL,
        name="times_columns",
    )(left, right)


def times_rows_kernel(left_ref, right_ref, out_ref):
    out_ref[...] = dot_nt(left_ref[...], right_ref[...]).astype(BF16)


def times_rows(left, right, place):
    rows, depth = left.shape
    columns = right.shape[0]
    tile = min(256, columns)
    return pl.pallas_call(
        times_rows_kernel,
        grid=(columns // tile,),
        in_specs=[
            pl.BlockSpec((rows, depth), lambda col: (0, 0)),
            pl.BlockSpec((tile, depth), lambda col: (col, place)),
        ],
        out_specs=pl.BlockSpec((rows, tile), lambda col: (0, col)),
        out_shape=shaped((rows, columns), BF16),
        compiler_params=limits(40),
        cost_estimate=SMALL,
        name="times_rows",
    )(left, right)


def gram_blocks(rows):
    depth, width = rows.shape
    pairs = gram_pairs(width)
    first = jnp.asarray([i for i, _ in pairs], jnp.int32)
    second = jnp.asarray([j for _, j in pairs], jnp.int32)
    shape = (len(pairs), GRAM_TILE, GRAM_TILE)
    return pl.pallas_call(
        gram_kernel,
        grid_spec=pltpu.PrefetchScalarGridSpec(
            num_scalar_prefetch=2,
            grid=(len(pairs),),
            in_specs=[
                pl.BlockSpec((depth, GRAM_TILE), lambda step, one, two: (0, one[step])),
                pl.BlockSpec((depth, GRAM_TILE), lambda step, one, two: (0, two[step])),
            ],
            out_specs=pl.BlockSpec((1, *shape[1:]), lambda step, one, two: (step, 0, 0)),
        ),
        out_shape=shaped(shape, BF16),
        compiler_params=limits(40),
        cost_estimate=SMALL,
        name="gram_blocks",
    )(first, second, rows, rows)


def muon(update, packed, halves):
    rows, width = update.shape
    index = jnp.arange(GRAM_TILE)
    pairs = gram_pairs(width)
    squares = jnp.stack(
        [
            jnp.sum(jnp.where(index[:, None] == index[None, :], packed[at].astype(F32), 0.0))
            for at, (i, j) in enumerate(pairs)
            if i == j
        ]
    )
    count = squares.shape[0]
    low_half, high_half = jnp.sum(squares[: count // 2]), jnp.sum(squares[count // 2 :])
    both = low_half + high_half
    squares = jnp.stack([jnp.where(halves, low_half, both), jnp.where(halves, high_half, both)])
    inverse = jnp.repeat(1.0 / (jnp.sqrt(squares) + NS_EPS), width // 2)
    once = dict(pipeline_mode=pl.Buffered(1))
    return pl.pallas_call(
        muon_kernel,
        grid=(),
        in_specs=[
            pl.BlockSpec(memory_space=pltpu.SMEM),
            pl.BlockSpec(update.shape, lambda: (0, 0), **once),
            pl.BlockSpec(packed.shape, lambda: (0, 0, 0), **once),
            pl.BlockSpec((1, width), lambda: (0, 0)),
            pl.BlockSpec((width, 1), lambda: (0, 0)),
        ],
        out_specs=pl.BlockSpec(update.shape, lambda: (0, 0)),
        out_shape=shaped(update.shape, BF16),
        scratch_shapes=[pltpu.VMEM(update.shape, BF16)]
        + [pltpu.VMEM((width, width), BF16)] * 2
        + [pltpu.VMEM(update.shape, BF16)] * 4,
        compiler_params=limits(58),
        cost_estimate=SMALL,
        name="muon",
    )(
        jnp.asarray(halves, jnp.int32).reshape(1),
        update,
        packed,
        inverse[None],
        inverse[:, None],
    )


def after(value, *earlier):
    return lax.optimization_barrier((value, earlier))[0]


def shifted(step, count):
    return [(src, (src + step) % count) for src in range(count)]


def swap(value, axis_name="core"):
    return lax.ppermute(value, axis_name, shifted(1, CORES))


def with_partner(value):
    return jnp.concatenate([value, swap(value)], axis=0)


def ring_blocks(value, axis_name, count):
    return [value] + [
        lax.ppermute(value, axis_name, shifted(step, count)) for step in range(1, count)
    ]


def ring_send(blocks, axis_name, count):
    return [
        lax.ppermute(blocks[step].astype(BF16), axis_name, shifted(-step, count))
        for step in range(1, count)
    ]


def add_all(own, arrived):
    for term in arrived:
        own = own + term.astype(F32)
    return own


def pick(blocks, index, axis=0):
    return lax.dynamic_index_in_dim(blocks, index, axis, keepdims=False)


def gather_rows(shard, axes):
    return lax.all_gather(shard, axes, axis=0, tiled=True)


def scatter_blocks(blocks, axis_name):
    count = blocks.shape[0]
    here = lax.axis_index(axis_name)
    arrived = [
        lax.ppermute(pick(blocks, (here + step) % count), axis_name, shifted(step, count))
        for step in range(1, count)
    ]
    return pick(blocks, here), arrived


def ff_grad(left_turned, right):
    return weight_grad(left_turned, right).reshape(PLANES, -1, right.shape[1])


def halves_over_y(partials):
    here = lax.axis_index("y")
    split = [value.reshape(PLANES, CORES, -1, value.shape[-1]) for value in partials]
    sent = jnp.concatenate([pick(value, 1 - here, 1) for value in split], axis=-1)
    kept = [pick(value, here, 1) for value in split]
    return kept, swap(sent, "y"), sent


def chunks_over_z(kept, arrived):
    here = lax.axis_index("z")

    def chunk(step):
        plane = (here + step) % PLANES
        near = jnp.concatenate([pick(value, plane) for value in kept], axis=-1)
        return near.astype(F32) + pick(arrived, plane).astype(F32)

    own = chunk(0)
    sent = [chunk(step).astype(BF16) for step in range(1, PLANES)]
    return own, [
        lax.ppermute(value, "z", shifted(step + 1, PLANES)) for step, value in enumerate(sent)
    ], sent


def butterfly(value, axis_name):
    count = lax.axis_size(axis_name)
    step = 1
    while step < count:
        value = value + lax.ppermute(value, axis_name, [(src, src ^ step) for src in range(count)])
        step *= 2
    return value


def sum_in_order(value, arrived):
    here = lax.axis_index("z")
    values = jnp.stack([value, *arrived])
    total = pick(values, here)
    for plane in range(1, PLANES):
        total = total + pick(values, (here - plane) % PLANES)
    return total


def to_planes(chunks):
    here = lax.axis_index("z")
    arrived = [pick(chunks, here)]
    for step in range(1, PLANES):
        arrived.append(
            lax.ppermute(pick(chunks, (here + step) % PLANES), "z", shifted(step, PLANES))
        )
    return jnp.stack(arrived)


def from_planes(arrived):
    here = lax.axis_index("z")
    back = [arrived[0]]
    for step in range(1, PLANES):
        back.append(lax.ppermute(arrived[step], "z", shifted(-step, PLANES)))
    back = jnp.stack(back)
    return [pick(back, (chunk - here) % PLANES) for chunk in range(PLANES)]


def per_device(
    inputs,
    cotangent,
    segments,
    w_query,
    key_weight_master,
    value_weight_master,
    w_output,
    w_gate,
    w_up,
    w_down,
    moment_query,
    moment_key,
    moment_value,
    moment_output,
    moment_gate,
    moment_up,
    moment_down,
    norm_gains,
    gain_first,
    gain_second,
):
    rows = inputs.shape[1]
    complete_rows = segments.shape[1]
    ring = lax.axis_size("fsdp")
    place = lax.axis_index("fsdp")
    core = lax.axis_index("core")
    gain_attn = norm_gains[:MODEL_WIDTH]
    gain_mlp = norm_gains[MODEL_WIDTH : 2 * MODEL_WIDTH]
    gain_query = norm_gains[2 * MODEL_WIDTH : 2 * MODEL_WIDTH + HEAD_SIZE]
    gain_key = norm_gains[2 * MODEL_WIDTH + HEAD_SIZE :]

    attention_rows = gather_rows(
        jnp.concatenate(
            [
                key_weight_master.astype(BF16),
                value_weight_master.astype(BF16),
                w_query.astype(BF16).T,
                w_output.astype(BF16),
            ],
            axis=1,
        ),
        SHARDS,
    )
    key_value_rows = attention_rows[:, :MODEL_WIDTH]
    query_rows = attention_rows[:, MODEL_WIDTH : 2 * MODEL_WIDTH]
    output_rows = attention_rows[:, 2 * MODEL_WIDTH :]
    gate_own, up_own_rows, down_own_rows = (
        gather_rows(shard, ("z",))
        for shard in (w_gate.astype(BF16).T, w_up.astype(BF16).T, w_down.astype(BF16))
    )

    masters = (w_query, key_weight_master, value_weight_master, w_output, w_gate, w_up, w_down)
    moments = (
        moment_query,
        moment_key,
        moment_value,
        moment_output,
        moment_gate,
        moment_up,
        moment_down,
    )
    full_sides = (MODEL_WIDTH,) * 4 + (FF,) * 3
    sideways = (True, False, False, False, True, True, False)

    def updated(shard, idx):
        grad = shard.T if sideways[idx] else shard
        moment = MOMENTUM * moments[idx] + grad
        update = grad + MOMENTUM * moment
        return grad, moment, (update.T if sideways[idx] else update).astype(BF16)

    both_segments = with_partner(segments)
    row_idx = jnp.arange(complete_rows, dtype=jnp.int32)
    boundary = jnp.concatenate(
        [
            jnp.ones((CORES, 1), dtype=bool),
            both_segments[:, 1:] != both_segments[:, :-1],
        ],
        axis=1,
    )
    doc_start = lax.cummax(jnp.where(boundary, row_idx[None, :], 0), axis=1)
    first_row = place * rows
    positions = lax.dynamic_slice_in_dim(row_idx[None, :] - doc_start, first_row, rows, 1)
    cosine_table, sine_table = rope_tables(positions, HEAD_SIZE)
    query_segments = lax.dynamic_slice_in_dim(both_segments, first_row, rows, 1)
    query_pos = first_row + jnp.arange(rows, dtype=jnp.int32)
    key_starts = [((place - step) % ring) * rows for step in range(ring)]
    key_pos = jnp.concatenate([at + jnp.arange(rows, dtype=jnp.int32) for at in key_starts])
    key_segments = jnp.concatenate(
        [lax.dynamic_slice_in_dim(both_segments, at, rows, 1) for at in key_starts], axis=1
    )
    mask = (
        (key_pos[None, :, None] <= query_pos[None, None, :])
        & (key_segments[:, :, None] == query_segments[:, None, :])
    ).astype(BF16)

    residual = inputs.astype(F32).reshape(rows, MODEL_WIDTH)
    normed = rms_scale(residual, gain_attn).astype(BF16)
    both_normed = with_partner(normed)
    cotangent_rows = cotangent.reshape(rows, MODEL_WIDTH)
    pair_rows = CORES * rows

    def own_columns(values):
        split = values.reshape(values.shape[0], -1, CORES, HEAD_SIZE)
        return pick(split, core, 2).reshape(values.shape[0], MODEL_WIDTH // CORES)

    own_normed = own_columns(both_normed)
    kv_sent = dot_nn(own_normed[rows:], key_value_rows).astype(BF16)
    kv_near = dot_nn(own_normed[:rows], key_value_rows)
    q_proj = dot_nt(both_normed, query_rows)
    kv_proj, kv_low = key_value_chain(
        kv_near, swap(kv_sent), gain_key[None], cosine_table[0], sine_table[0]
    )
    kv_blocks, gate_own = after((ring_blocks(kv_low, "fsdp", ring), gate_own), q_proj)
    gate_other = swap(gate_own, "y")
    own_kv = jnp.concatenate(kv_blocks, axis=0)
    both_kv = with_partner(own_kv).reshape(CORES, complete_rows, 2 * KV_WIDTH)
    attention_inputs = (q_proj, both_kv, mask, gain_query[None], cosine_table, sine_table)
    att_low, att_turned = attention(*attention_inputs)
    cotangent_blocks = ring_blocks(after(cotangent_rows, own_kv), "fsdp", ring)
    att_low, cotangent_blocks = lax.optimization_barrier((att_low, cotangent_blocks))
    team_cotangent = with_partner(jnp.concatenate(cotangent_blocks, axis=0))
    out_sent = dot_nn(att_low[rows:], output_rows).astype(BF16)
    out_near = dot_nn(att_low[:rows], output_rows)
    out_sent, out_near, gate_other, up_own_rows = lax.optimization_barrier(
        (out_sent, out_near, gate_other, up_own_rows)
    )
    up_other = swap(up_own_rows, "y")
    middle = residual + out_near + swap(out_sent).astype(F32)

    normed_two = rms_scale(middle, gain_mlp).astype(BF16)
    two_blocks, down_own_rows, up_other = after(
        (ring_blocks(normed_two, "fsdp", ring), down_own_rows, up_other), team_cotangent
    )
    down_other = swap(down_own_rows, "y")
    team_two = with_partner(jnp.concatenate(two_blocks, axis=0))
    own_rows = ring * rows
    hidden, d_gate, d_up, hidden_turned, d_gate_turned, d_up_turned = swiglu_both_ways(
        team_two, team_cotangent, gate_own, up_own_rows, down_own_rows
    )
    down_kept = ff_grad(hidden_turned, team_cotangent)
    gate_kept = ff_grad(after(d_gate_turned, down_kept), team_two)
    up_kept = ff_grad(after(d_up_turned, gate_kept), team_two)
    (
        far_hidden,
        far_d_gate,
        far_d_up,
        far_hidden_turned,
        far_d_gate_turned,
        far_d_up_turned,
    ) = swiglu_both_ways(
        team_two, team_cotangent, gate_other, up_other, after(down_other, up_kept)
    )
    down_sent = ff_grad(far_hidden_turned, team_cotangent)
    down_passed = swap(down_sent, "y")
    gate_sent = ff_grad(after(far_d_gate_turned, down_sent), team_two)
    gate_passed = swap(gate_sent, "y")
    back_lefts = after((d_gate, d_up, far_d_gate, far_d_up), gate_sent)
    back_rights = (gate_own, up_own_rows, gate_other, up_other)
    back_far = back_to_width(back_lefts, back_rights, own_rows, own_rows)
    back_near = back_to_width(after(back_lefts, back_far), back_rights, 0, own_rows)
    down_own, down_chunks, down_chunks_sent = chunks_over_z(
        [down_kept], after(down_passed, back_near)
    )
    back_half = back_near.astype(F32) + swap(after(back_far, down_chunks_sent)).astype(F32)
    back_half = back_half.reshape(ring, rows, MODEL_WIDTH)
    back_arrived = ring_send([back_half[step] for step in range(ring)], "fsdp", ring)
    up_sent = ff_grad(after(far_d_up_turned, back_half), team_two)
    up_passed = swap(up_sent, "y")
    back_arrived, down_chunks = after((back_arrived, down_chunks), up_sent)
    d_normed_two = add_all(after(back_half[0], down_chunks), back_arrived)
    second_back = jax.vjp(rms_scale, middle, gain_mlp)[1]
    d_mid_norm, d_gain_mlp = second_back(d_normed_two)
    d_middle = cotangent_rows.astype(F32) + d_mid_norm
    d_middle, gate_passed = lax.optimization_barrier((d_middle, gate_passed))

    both_mid = with_partner(d_middle.astype(BF16))
    gate_own, gate_chunks, gate_chunks_sent = chunks_over_z([gate_kept], gate_passed)
    output_grad = weight_grad(att_turned, after(both_mid, gate_chunks_sent))
    output_blocks = jnp.moveaxis(output_grad.reshape(PLANES * CORES, ring, -1, MODEL_WIDTH), 1, 0)
    output_own, output_arrived = scatter_blocks(output_blocks, "fsdp")
    d_head = times_rows(after(both_mid, output_grad), attention_rows, 2)
    *far_parts, d_kv_far, far_gain = attention_back(*attention_inputs, d_head, 1, ())
    q_low, q_low_turned, d_kv_near, near_gain = attention_back(
        *attention_inputs, d_head, 0, far_parts
    )
    d_gain_query = (far_gain + near_gain)[0]
    query_grad = weight_grad(q_low_turned, both_normed)
    from_query = times_columns(after(q_low, query_grad), attention_rows, MODEL_WIDTH, MODEL_WIDTH)
    query_blocks = jnp.moveaxis(query_grad.reshape(PLANES * CORES, ring, -1, MODEL_WIDTH), 1, 0)
    query_own, query_arrived = scatter_blocks(query_blocks, "fsdp")
    up_passed, gate_chunks, output_arrived = after(
        (up_passed, gate_chunks, output_arrived), from_query
    )
    up_own, up_chunks, up_chunks_sent = chunks_over_z([up_kept], up_passed)
    d_kv_half = d_kv_near.astype(F32) + swap(after(d_kv_far, up_chunks_sent)).astype(F32)
    d_kv_half = d_kv_half.reshape(2, ring, rows, KV_WIDTH)
    d_kv_arrived = ring_send([d_kv_half[:, step] for step in range(ring)], "fsdp", ring)
    hiddens = after((hidden, far_hidden), d_kv_half)
    down_rights = (down_own_rows, down_other)
    down_far = back_to_width(hiddens, down_rights, own_rows, own_rows)
    down_near = back_to_width(after(hiddens, down_far), down_rights, 0, own_rows)
    gate_new = updated(add_all(gate_own, gate_chunks), 4)
    down_new = updated(add_all(down_own, down_chunks), 6)
    up_chunks, d_kv_arrived, query_arrived = after(
        (up_chunks, d_kv_arrived, query_arrived), down_near
    )
    big = [gate_new, updated(add_all(up_own, up_chunks), 5), down_new]
    slots = jnp.stack([new[2] for new in big] + [jnp.zeros_like(down_new[2])])
    big_mine = to_planes(slots).reshape(-1, MODEL_WIDTH)
    first_kept, first_passed, first_sent = halves_over_y(
        [
            add_all(output_own.astype(F32), output_arrived).astype(BF16),
            add_all(query_own.astype(F32), query_arrived).astype(BF16),
        ]
    )
    d_kv_total = add_all(d_kv_half[:, 0], d_kv_arrived)
    kv_low_grad, d_gain_key = key_value_back(
        d_kv_total, kv_proj, gain_key[None], cosine_table[0], sine_table[0]
    )
    d_gain_key = d_gain_key[0]
    both_kv_low = with_partner(kv_low_grad)
    key_value_grad = dot_tn(own_normed, both_kv_low).astype(BF16)
    key_value_blocks = jnp.moveaxis(
        key_value_grad.reshape(PLANES * CORES, ring, -1, MODEL_WIDTH), 1, 0
    )
    key_value_own, key_value_arrived = scatter_blocks(key_value_blocks, "fsdp")
    plane = lax.axis_index("z")
    in_plane = ("y", "core", "fsdp")
    big_mine, first_passed, key_value_grad = lax.optimization_barrier(
        (big_mine, first_passed, key_value_grad)
    )
    big_gram = gram_blocks(big_mine)
    from_query, down_far = after((from_query, down_far), big_gram)
    down_half = (down_near.astype(F32) + swap(down_far).astype(F32)).reshape(
        ring, rows, MODEL_WIDTH
    )
    first_own, first_chunks, first_chunks_sent = chunks_over_z(
        first_kept, after(first_passed, big_gram)
    )
    from_kv = times_rows(
        after(both_kv_low, key_value_grad, first_chunks_sent), attention_rows, 0
    )
    big_gram = lax.psum(big_gram, in_plane)

    from_query = from_query[:rows].astype(F32) + swap(from_query[rows:]).astype(F32)
    kv_here = from_kv[:rows].reshape(rows, -1, HEAD_SIZE)
    kv_there = swap(from_kv[rows:]).reshape(rows, -1, HEAD_SIZE)
    from_kv_full = jnp.stack(
        [jnp.where(core == 0, kv_here, kv_there), jnp.where(core == 0, kv_there, kv_here)], axis=2
    ).reshape(rows, MODEL_WIDTH)
    d_normed = from_query + from_kv_full.astype(F32)
    first_back = jax.vjp(rms_scale, residual, gain_attn)[1]
    d_residual, d_gain_attn = first_back(d_normed)
    input_grad = (d_middle + d_residual).reshape(inputs.shape)
    gain_grad = jnp.concatenate([d_gain_attn, d_gain_mlp, d_gain_query, d_gain_key])

    key_value_arrived, first_chunks = after((key_value_arrived, first_chunks), input_grad)
    kept, arrived, _ = halves_over_y(
        [add_all(key_value_own.astype(F32), key_value_arrived).astype(BF16)]
    )
    last_own, last_chunks, _ = chunks_over_z(kept, arrived)
    last_chunks, big_gram, gain_grad, down_half = lax.optimization_barrier(
        (last_chunks, big_gram, butterfly(butterfly(gain_grad, "core"), "fsdp"), down_half)
    )
    first_total = add_all(first_own, first_chunks)
    output_shard = first_total[:, :MODEL_WIDTH]
    query_shard = first_total[:, MODEL_WIDTH:]
    key_value_shard = add_all(last_own, last_chunks)
    small = [
        updated(query_shard, 0),
        updated(key_value_shard[:, :KV_WIDTH], 1),
        updated(key_value_shard[:, KV_WIDTH:], 2),
        updated(output_shard, 3),
    ]
    small_slots = jnp.stack(
        [
            small[0][2],
            jnp.concatenate([small[1][2], small[2][2]], axis=1),
            small[3][2],
            jnp.zeros_like(small[3][2]),
        ]
    )
    small_mine = to_planes(small_slots).reshape(-1, MODEL_WIDTH)
    small_mine, gain_grad = lax.optimization_barrier((small_mine, butterfly(gain_grad, "y")))
    whole = gather_rows(small_mine, in_plane)
    turned = muon(after(big_mine, small_mine), big_gram, jnp.bool_(False))
    turned, whole, gain_arrived = lax.optimization_barrier(
        (turned, whole, ring_blocks(gain_grad, "z", PLANES)[1:])
    )
    gain_grad = sum_in_order(gain_grad, gain_arrived)
    returned = from_planes(turned.reshape(PLANES, -1, MODEL_WIDTH))
    small_gram = gram_blocks(whole)
    down_arrived = ring_send(
        [after(down_half, small_gram)[step] for step in range(ring)], "fsdp", ring
    )
    turned, returned, down_arrived = lax.optimization_barrier(
        (muon(small_mine, small_gram, plane == 1), returned, down_arrived)
    )
    small_returned = from_planes(turned.reshape(small_slots.shape))
    block_out = (middle + add_all(down_half[0], down_arrived)).astype(BF16).reshape(inputs.shape)
    ortho = (
        small_returned[0],
        small_returned[1][:, :KV_WIDTH],
        small_returned[1][:, KV_WIDTH:],
        small_returned[2],
        *returned[:3],
    )
    new_weights = tuple(
        master * (1.0 - LR_MUON * DECAY_MUON)
        - LR_MUON * math.sqrt(side) * (rows_now.T if turn else rows_now).astype(F32)
        for master, rows_now, turn, side in zip(masters, ortho, sideways, full_sides)
    )

    first_new = BETA_ONE * gain_first + (1.0 - BETA_ONE) * gain_grad
    second_new = BETA_TWO * gain_second + (1.0 - BETA_TWO) * gain_grad * gain_grad
    corr_one = 1.0 - BETA_ONE**ADAM_STEP
    corr_two = 1.0 - BETA_TWO**ADAM_STEP
    gains_new = norm_gains - LR_GAIN * (first_new / corr_one) / (
        jnp.sqrt(second_new / corr_two) + EPS_ADAM
    )
    return (
        block_out,
        input_grad,
        *(grad for grad, _, _ in small + big),
        *(moment for _, moment, _ in small + big),
        *new_weights,
        first_new,
        second_new,
        gains_new,
    )


def solution(mesh):
    dp_size, fsdp_size = mesh.devices.shape
    fine_mesh = Mesh(
        mesh.devices.reshape(PLANES, dp_size // (PLANES * CORES), CORES, fsdp_size),
        ("z", "y", "core", "fsdp"),
    )
    dp = ("z", "y", "core")
    tokens = P(dp, "fsdp", None)
    by_row = P(EVERYWHERE, None)
    by_col = P(None, EVERYWHERE)
    matrices = (by_col, by_row, by_row, by_row, by_col, by_col, by_row)
    return jax.shard_map(
        per_device,
        mesh=fine_mesh,
        in_specs=(tokens, tokens, P(dp, None), *matrices, *matrices, P(), P(), P()),
        out_specs=(tokens, tokens, *matrices, *matrices, *matrices, P(), P(), P()),
        check_vma=False,
    )
```

```python
import functools
import math

import jax
import jax.numpy as jnp
from jax import lax
from jax.experimental import pallas as pl
from jax.experimental.pallas import tpu as pltpu
from jax.sharding import Mesh
from jax.sharding import PartitionSpec as P

MODEL_WIDTH = 2048
QUERY_HEADS = 16
KEY_VALUE_HEADS = 8
HEAD_SIZE = 128
FF = 6144
ADAM_STEP = 10

EPS_NORM = 1e-06
THETA = 1000000.0
NEG_FILL = -1e30
MOMENTUM = 0.95
NS_A = 3.4445
NS_B = -4.775
NS_C = 2.0315
NS_EPS = 1e-07
LR_MUON = 0.2
DECAY_MUON = 0.01
LR_GAIN = 0.5
BETA_ONE = 0.9
BETA_TWO = 0.95
EPS_ADAM = 1e-08

CORES = 2
PLANES = 4
GRAM_TILE = 512
KV_WIDTH = KEY_VALUE_HEADS * HEAD_SIZE
BF16 = jnp.bfloat16
F32 = jnp.float32
SHARDS = ("z", "y", "fsdp")
EVERYWHERE = ("z", "y", "core", "fsdp")


def rms_scale(values, gain):
    return values * lax.rsqrt(jnp.mean(values * values, axis=-1, keepdims=True) + EPS_NORM) * gain


def rope_tables(positions, head_width):
    half_width = head_width // 2
    freq = jnp.exp(
        -(2.0 * jnp.arange(half_width, dtype=jnp.float32) / head_width) * math.log(THETA)
    )
    angle = positions.astype(jnp.float32)[..., None] * freq
    cosine = jnp.cos(angle)
    sine = jnp.sin(angle)
    return jnp.concatenate([cosine, cosine], -1), jnp.concatenate([-sine, sine], -1)


def dot_nn(left, right):
    return lax.dot_general(left, right, (((1,), (0,)), ((), ())), preferred_element_type=F32)


def dot_nt(left, right):
    return lax.dot_general(left, right, (((1,), (1,)), ((), ())), preferred_element_type=F32)


def dot_tn(left, right):
    return lax.dot_general(left, right, (((0,), (0,)), ((), ())), preferred_element_type=F32)


def gram_pairs(width):
    count = width // GRAM_TILE
    return [(i, j) for i in range(count) for j in range(i, count)]


def head_chain(head, gain, cosine, sine):
    scaled = head * lax.rsqrt(jnp.mean(head * head, axis=-1, keepdims=True) + EPS_NORM) * gain
    return scaled * cosine + pltpu.roll(scaled, HEAD_SIZE // 2, 1) * sine


def head_chain_back(head, gain, cosine, sine, grad):
    grad = grad * cosine + pltpu.roll(grad * sine, HEAD_SIZE // 2, 1)
    scale = lax.rsqrt(jnp.mean(head * head, axis=-1, keepdims=True) + EPS_NORM)
    unit = head * scale
    d_gain = jnp.sum(grad * unit, axis=0, keepdims=True)
    grad = grad * gain
    return scale * (grad - unit * jnp.mean(grad * unit, axis=-1, keepdims=True)), d_gain


def key_value_kernel(near_ref, far_ref, gain_ref, cos_ref, sin_ref, proj_ref, low_ref):
    proj = near_ref[...] + far_ref[...].astype(F32)
    proj_ref[...] = proj
    is_key = pl.program_id(0) < KEY_VALUE_HEADS

    @pl.when(is_key)
    def _():
        low_ref[...] = head_chain(proj, gain_ref[...], cos_ref[...], sin_ref[...]).astype(BF16)

    @pl.when(jnp.logical_not(is_key))
    def _():
        low_ref[...] = proj.astype(BF16)


def key_value_back_kernel(grad_ref, proj_ref, gain_ref, cos_ref, sin_ref, low_ref, d_gain_ref):
    head = pl.program_id(0)

    @pl.when(head == 0)
    def _():
        d_gain_ref[...] = jnp.zeros_like(d_gain_ref)

    @pl.when(head < KEY_VALUE_HEADS)
    def _():
        d_proj, d_gain = head_chain_back(
            proj_ref[...], gain_ref[...], cos_ref[...], sin_ref[...], grad_ref[0]
        )
        low_ref[...] = d_proj.astype(BF16)
        d_gain_ref[...] += d_gain

    @pl.when(head >= KEY_VALUE_HEADS)
    def _():
        low_ref[...] = grad_ref[0].astype(BF16)


def attention_weights(q_ref, k_ref, mask_ref, gain_ref, cos_ref, sin_ref):
    query = head_chain(q_ref[...], gain_ref[...], cos_ref[0], sin_ref[0]).astype(BF16)
    scores = dot_nt(k_ref[0], query)
    weights = jnp.exp2(scores * (HEAD_SIZE ** (-0.5) * math.log2(math.e)))
    return query, weights * mask_ref[0].astype(F32)


def attention_kernel(
    q_ref, k_ref, v_ref, mask_ref, gain_ref, cos_ref, sin_ref, out_ref, out_turned_ref
):
    _, weights = attention_weights(q_ref, k_ref, mask_ref, gain_ref, cos_ref, sin_ref)
    total = jnp.sum(weights, axis=0, keepdims=True)
    out = dot_tn(v_ref[0], weights.astype(BF16)) * (1.0 / total)
    out_turned_ref[...] = out.astype(BF16)
    out_ref[...] = out.T.astype(BF16)


def attention_back_kernel(
    q_ref, k_ref, v_ref, mask_ref, gain_ref, cos_ref, sin_ref, grad_ref,
    *refs,
):
    q_low_ref, q_low_turned_ref, d_kv_ref, d_gain_ref = refs[-4:]

    @pl.when(pl.program_id(0) == 0)
    def _():
        d_gain_ref[...] = jnp.zeros_like(d_gain_ref)

    query, weights = attention_weights(q_ref, k_ref, mask_ref, gain_ref, cos_ref, sin_ref)
    grad = grad_ref[...]
    probs = weights * (1.0 / jnp.sum(weights, axis=0, keepdims=True))
    d_probs = dot_nt(v_ref[0], grad)
    delta = jnp.sum(probs * d_probs, axis=0, keepdims=True)
    d_scores = (probs * (d_probs - delta)).astype(BF16)
    d_value = dot_nn(probs.astype(BF16), grad).astype(BF16)
    d_key = (dot_nn(d_scores, query) * HEAD_SIZE ** (-0.5)).astype(BF16)

    d_kv_ref[0] = d_key
    d_kv_ref[1] = d_value
    d_query = dot_tn(k_ref[0], d_scores).T * HEAD_SIZE ** (-0.5)
    d_proj, d_gain = head_chain_back(
        q_ref[...], gain_ref[...], cos_ref[0], sin_ref[0], d_query
    )
    q_low_ref[...] = d_proj.astype(BF16)
    q_low_turned_ref[...] = d_proj.T.astype(BF16)
    d_gain_ref[...] += d_gain


def swiglu_kernel(two_ref, cot_ref, gate_ref, up_ref, down_ref, *out_refs):
    two = two_ref[...]
    gate = dot_nt(two, gate_ref[...])
    up = dot_nt(two, up_ref[...])
    d_hidden = dot_nt(cot_ref[...], down_ref[...])
    sig = 1.0 / (1.0 + jnp.exp(-gate))
    silu = gate * sig
    results = (silu * up, d_hidden * up * sig * (1.0 + gate * (1.0 - sig)), d_hidden * silu)
    for result, out_ref, turned_ref in zip(results, out_refs[:3], out_refs[3:]):
        low = result.astype(BF16)
        out_ref[...] = low
        turned_ref[...] = low.T


def back_to_width_kernel(count, *refs):
    lefts, rights, out_ref = refs[:count], refs[count : 2 * count], refs[-1]
    total = 0.0
    for left, right in zip(lefts, rights):
        total = total + dot_nn(left[...], right[...])
    out_ref[...] = total.astype(BF16)


def weight_grad_kernel(left_ref, right_ref, out_ref):
    out_ref[...] = dot_nn(left_ref[...], right_ref[...]).astype(BF16)


def gram_kernel(first_ref, second_ref, left_ref, right_ref, out_ref):
    out_ref[0] = dot_tn(left_ref[...], right_ref[...]).astype(BF16)


def muon_kernel(
    halves_ref, update_ref, packed_ref, out_ref,
    start_ref, gram_ref, bend_ref, first_ref, product_ref, one_ref, two_ref,
):
    width = update_ref.shape[1]
    tile = GRAM_TILE
    count = width // tile
    one_matrix = (1 - halves_ref[0]).astype(F32)
    index = lax.broadcasted_iota(jnp.int32, (tile, tile), 0)
    on_diagonal = index == lax.broadcasted_iota(jnp.int32, (tile, tile), 1)
    traces = [0.0, 0.0]
    for place, (i, j) in enumerate(gram_pairs(width)):
        if i == j:
            block = jnp.where(on_diagonal, packed_ref[place].astype(F32), 0.0)
            block = jnp.sum(jnp.sum(block, axis=0, keepdims=True), axis=1, keepdims=True)
            traces[2 * i // count] = traces[2 * i // count] + block
    inverse = [
        1.0 / (jnp.sqrt(traces[half] + one_matrix * traces[1 - half]) + NS_EPS) for half in range(2)
    ]
    middle = width // 2
    start_ref[:, :middle] = (update_ref[:, :middle].astype(F32) * inverse[0]).astype(BF16)
    start_ref[:, middle:] = (update_ref[:, middle:].astype(F32) * inverse[1]).astype(BF16)

    def put(ref, i, j, value):
        ref[i * tile : (i + 1) * tile, j * tile : (j + 1) * tile] = value
        if i != j:
            ref[j * tile : (j + 1) * tile, i * tile : (i + 1) * tile] = value.T

    for place, (i, j) in enumerate(gram_pairs(width)):
        block = packed_ref[place].astype(F32) * inverse[2 * i // count] * inverse[2 * j // count]
        if 2 * i < count <= 2 * j:
            block = block * one_matrix
        put(gram_ref, i, j, block.astype(BF16))
    for i, j in gram_pairs(width):
        rows, cols = slice(i * tile, (i + 1) * tile), slice(j * tile, (j + 1) * tile)
        square = dot_nn(gram_ref[rows, :], gram_ref[:, cols])
        put(bend_ref, i, j, (NS_B * gram_ref[rows, cols].astype(F32) + NS_C * square).astype(BF16))

    def columns(body):
        @pl.loop(0, count)
        def _(step):
            body(pl.ds(pl.multiple_of(step * tile, tile), tile))

    def times_p(rows_ref, cols):
        return NS_A * rows_ref[:, cols].astype(F32) + dot_nn(rows_ref[...], bend_ref[:, cols])

    def to_first(cols):
        first_ref[:, cols] = times_p(start_ref, cols).astype(BF16)

    def bent_first(cols):
        one_ref[:, cols] = times_p(first_ref, cols).astype(BF16)

    def by_gram(cols):
        two_ref[:, cols] = dot_nn(one_ref[...], gram_ref[:, cols]).astype(BF16)

    def to_product(cols):
        product_ref[:, cols] = times_p(two_ref, cols).astype(BF16)

    def bent_product(cols):
        one_ref[:, cols] = times_p(product_ref, cols).astype(BF16)

    def finish(cols):
        again = times_p(two_ref, cols)
        out_ref[:, cols] = (
            NS_A * first_ref[:, cols].astype(F32)
            + NS_B * product_ref[:, cols].astype(F32)
            + NS_C * again
        ).astype(BF16)

    for body in (to_first, bent_first, by_gram, to_product, bent_product, by_gram, finish):
        columns(body)


def shaped(shape, dtype):
    return jax.ShapeDtypeStruct(shape, dtype)


SMALL = pl.CostEstimate(flops=1, bytes_accessed=1, transcendentals=0)


def limits(mebibytes):
    return pltpu.CompilerParams(vmem_limit_bytes=mebibytes * 1024 * 1024)


def key_value_chain(near, far, gain, cosine, sine):
    rows = near.shape[0]
    block = pl.BlockSpec((rows, HEAD_SIZE), lambda head: (0, head))
    fixed = pl.BlockSpec((rows, HEAD_SIZE), lambda head: (0, 0))
    one = pl.BlockSpec((1, HEAD_SIZE), lambda head: (0, 0))
    return pl.pallas_call(
        key_value_kernel,
        grid=(2 * KEY_VALUE_HEADS,),
        in_specs=[block, block, one, fixed, fixed],
        out_specs=[block, block],
        out_shape=[shaped(near.shape, F32), shaped(near.shape, BF16)],
        compiler_params=limits(16),
        cost_estimate=SMALL,
        name="key_value_chain",
    )(near, far, gain, cosine, sine)


def key_value_back(grad, proj, gain, cosine, sine):
    rows = proj.shape[0]
    heads = KEY_VALUE_HEADS
    block = pl.BlockSpec((rows, HEAD_SIZE), lambda head: (0, head))
    split = pl.BlockSpec((1, rows, HEAD_SIZE), lambda head: (head // heads, 0, head % heads))
    fixed = pl.BlockSpec((rows, HEAD_SIZE), lambda head: (0, 0))
    one = pl.BlockSpec((1, HEAD_SIZE), lambda head: (0, 0))
    return pl.pallas_call(
        key_value_back_kernel,
        grid=(2 * heads,),
        in_specs=[split, block, one, fixed, fixed],
        out_specs=[block, one],
        out_shape=[shaped(proj.shape, BF16), shaped((1, HEAD_SIZE), F32)],
        compiler_params=limits(16),
        cost_estimate=SMALL,
        name="key_value_back",
    )(grad, proj, gain, cosine, sine)


def attention_specs(rows, keys, heads):
    return [
        pl.BlockSpec((rows, HEAD_SIZE), lambda seq, head: (seq, head)),
        pl.BlockSpec((1, keys, HEAD_SIZE), lambda seq, head: (seq, 0, head)),
        pl.BlockSpec((1, keys, HEAD_SIZE), lambda seq, head: (seq, 0, heads + head)),
        pl.BlockSpec((1, keys, rows), lambda seq, head: (seq, 0, 0)),
        pl.BlockSpec((1, HEAD_SIZE), lambda seq, head: (0, 0)),
        pl.BlockSpec((1, rows, HEAD_SIZE), lambda seq, head: (seq, 0, 0)),
        pl.BlockSpec((1, rows, HEAD_SIZE), lambda seq, head: (seq, 0, 0)),
    ]


def attention(q_proj, kv, mask, gain, cosine, sine):
    sequences, keys, rows = mask.shape
    heads = q_proj.shape[1] // HEAD_SIZE
    specs = attention_specs(rows, keys, heads)
    return pl.pallas_call(
        attention_kernel,
        grid=(sequences, heads),
        in_specs=specs,
        out_specs=[specs[0], pl.BlockSpec((HEAD_SIZE, rows), lambda seq, head: (head, seq))],
        out_shape=[shaped(q_proj.shape, BF16), shaped(q_proj.shape[::-1], BF16)],
        compiler_params=limits(40),
        cost_estimate=SMALL,
        name="attention",
    )(q_proj, kv, kv, mask, gain, cosine, sine)


def attention_back(q_proj, kv, mask, gain, cosine, sine, grad, seq, others):
    _, keys, rows = mask.shape
    heads = q_proj.shape[1] // HEAD_SIZE
    specs = [
        pl.BlockSpec((rows, HEAD_SIZE), lambda head: (seq, head)),
        pl.BlockSpec((1, keys, HEAD_SIZE), lambda head: (seq, 0, head)),
        pl.BlockSpec((1, keys, HEAD_SIZE), lambda head: (seq, 0, heads + head)),
        pl.BlockSpec((1, keys, rows), lambda head: (seq, 0, 0)),
        pl.BlockSpec((1, HEAD_SIZE), lambda head: (0, 0)),
        pl.BlockSpec((1, rows, HEAD_SIZE), lambda head: (seq, 0, 0)),
        pl.BlockSpec((1, rows, HEAD_SIZE), lambda head: (seq, 0, 0)),
    ]
    return pl.pallas_call(
        attention_back_kernel,
        grid=(heads,),
        in_specs=[*specs, specs[0]] + [pl.BlockSpec(memory_space=pl.ANY)] * len(others),
        out_specs=[
            specs[0],
            pl.BlockSpec((HEAD_SIZE, rows), lambda head: (head, seq)),
            pl.BlockSpec((2, keys, HEAD_SIZE), lambda head: (0, 0, head)),
            specs[4],
        ],
        out_shape=[
            shaped(q_proj.shape, BF16),
            shaped(q_proj.shape[::-1], BF16),
            shaped((2, keys, heads * HEAD_SIZE), BF16),
            shaped((1, HEAD_SIZE), F32),
        ],
        input_output_aliases={8 + place: place for place in range(len(others))},
        compiler_params=limits(48),
        cost_estimate=SMALL,
        name="attention_back",
    )(q_proj, kv, kv, mask, gain, cosine, sine, grad, *others)


def swiglu_both_ways(two, cot, gate, up, down):
    tokens, width = two.shape
    columns = gate.shape[0]
    tile = min(512, tokens)
    row_block = pl.BlockSpec((tile, width), lambda row: (row, 0))
    weights = pl.BlockSpec((columns, width), lambda row: (0, 0))
    return pl.pallas_call(
        swiglu_kernel,
        grid=(tokens // tile,),
        in_specs=[row_block, row_block] + [weights] * 3,
        out_specs=[pl.BlockSpec((tile, columns), lambda row: (row, 0))] * 3
        + [pl.BlockSpec((columns, tile), lambda row: (0, row))] * 3,
        out_shape=[shaped((tokens, columns), BF16)] * 3 + [shaped((columns, tokens), BF16)] * 3,
        compiler_params=limits(60),
        cost_estimate=SMALL,
        name="swiglu_both_ways",
    )(two, cot, gate, up, down)


def back_to_width(lefts, rights, first_row, rows):
    width = rights[0].shape[1]
    tile = min(256, rows)
    first = first_row // tile
    return pl.pallas_call(
        functools.partial(back_to_width_kernel, len(lefts)),
        grid=(rows // tile,),
        in_specs=[
            pl.BlockSpec((tile, left.shape[1]), lambda row: (first + row, 0)) for left in lefts
        ]
        + [pl.BlockSpec(right.shape, lambda row: (0, 0)) for right in rights],
        out_specs=pl.BlockSpec((tile, width), lambda row: (row, 0)),
        out_shape=shaped((rows, width), BF16),
        compiler_params=limits(56),
        cost_estimate=SMALL,
        name="back_to_width",
    )(*lefts, *rights)


def weight_grad(left_turned, right):
    rows, tokens = left_turned.shape
    width = right.shape[1]
    tile = min(512, width)
    return pl.pallas_call(
        weight_grad_kernel,
        grid=(width // tile,),
        in_specs=[
            pl.BlockSpec((rows, tokens), lambda col: (0, 0)),
            pl.BlockSpec((tokens, tile), lambda col: (0, col)),
        ],
        out_specs=pl.BlockSpec((rows, tile), lambda col: (0, col)),
        out_shape=shaped((rows, width), BF16),
        compiler_params=limits(40),
        cost_estimate=SMALL,
        name="weight_grad",
    )(left_turned, right)


def times_columns_kernel(left_ref, right_ref, out_ref):
    out_ref[...] = dot_nn(left_ref[...], right_ref[...]).astype(BF16)


def times_columns(left, right, first_column, width):
    rows, depth = left.shape
    tile = min(512, width)
    first = first_column // tile
    return pl.pallas_call(
        times_columns_kernel,
        grid=(width // tile,),
        in_specs=[
            pl.BlockSpec((rows, depth), lambda col: (0, 0)),
            pl.BlockSpec((depth, tile), lambda col: (0, first + col)),
        ],
        out_specs=pl.BlockSpec((rows, tile), lambda col: (0, col)),
        out_shape=shaped((rows, width), BF16),
        compiler_params=limits(40),
        cost_estimate=SMALL,
        name="times_columns",
    )(left, right)


def times_rows_kernel(left_ref, right_ref, out_ref):
    out_ref[...] = dot_nt(left_ref[...], right_ref[...]).astype(BF16)


def times_rows(left, right, place):
    rows, depth = left.shape
    columns = right.shape[0]
    tile = min(256, columns)
    return pl.pallas_call(
        times_rows_kernel,
        grid=(columns // tile,),
        in_specs=[
            pl.BlockSpec((rows, depth), lambda col: (0, 0)),
            pl.BlockSpec((tile, depth), lambda col: (col, place)),
        ],
        out_specs=pl.BlockSpec((rows, tile), lambda col: (0, col)),
        out_shape=shaped((rows, columns), BF16),
        compiler_params=limits(40),
        cost_estimate=SMALL,
        name="times_rows",
    )(left, right)


def gram_blocks(rows):
    depth, width = rows.shape
    pairs = gram_pairs(width)
    first = jnp.asarray([i for i, _ in pairs], jnp.int32)
    second = jnp.asarray([j for _, j in pairs], jnp.int32)
    shape = (len(pairs), GRAM_TILE, GRAM_TILE)
    return pl.pallas_call(
        gram_kernel,
        grid_spec=pltpu.PrefetchScalarGridSpec(
            num_scalar_prefetch=2,
            grid=(len(pairs),),
            in_specs=[
                pl.BlockSpec((depth, GRAM_TILE), lambda step, one, two: (0, one[step])),
                pl.BlockSpec((depth, GRAM_TILE), lambda step, one, two: (0, two[step])),
            ],
            out_specs=pl.BlockSpec((1, *shape[1:]), lambda step, one, two: (step, 0, 0)),
        ),
        out_shape=shaped(shape, BF16),
        compiler_params=limits(40),
        cost_estimate=SMALL,
        name="gram_blocks",
    )(first, second, rows, rows)


def muon(update, packed, halves):
    width = update.shape[1]
    once = dict(pipeline_mode=pl.Buffered(1))
    return pl.pallas_call(
        muon_kernel,
        grid=(),
        in_specs=[
            pl.BlockSpec(memory_space=pltpu.SMEM),
            pl.BlockSpec(update.shape, lambda: (0, 0), **once),
            pl.BlockSpec(packed.shape, lambda: (0, 0, 0), **once),
        ],
        out_specs=pl.BlockSpec(update.shape, lambda: (0, 0)),
        out_shape=shaped(update.shape, BF16),
        scratch_shapes=[pltpu.VMEM(update.shape, BF16)]
        + [pltpu.VMEM((width, width), BF16)] * 2
        + [pltpu.VMEM(update.shape, BF16)] * 4,
        compiler_params=limits(58),
        cost_estimate=SMALL,
        name="muon",
    )(jnp.asarray(halves, jnp.int32).reshape(1), update, packed)


def after(value, *earlier):
    return lax.optimization_barrier((value, earlier))[0]


def shifted(step, count):
    return [(src, (src + step) % count) for src in range(count)]


def swap(value, axis_name="core"):
    return lax.ppermute(value, axis_name, shifted(1, CORES))


def with_partner(value):
    return jnp.concatenate([value, swap(value)], axis=0)


def ring_blocks(value, axis_name, count):
    return [value] + [
        lax.ppermute(value, axis_name, shifted(step, count)) for step in range(1, count)
    ]


def ring_send(blocks, axis_name, count):
    return [
        lax.ppermute(blocks[step].astype(BF16), axis_name, shifted(-step, count))
        for step in range(1, count)
    ]


def add_all(own, arrived):
    for term in arrived:
        own = own + term.astype(F32)
    return own


def pick(blocks, index, axis=0):
    return lax.dynamic_index_in_dim(blocks, index, axis, keepdims=False)


def gather_rows(shard, axes):
    return lax.all_gather(shard, axes, axis=0, tiled=True)


def scatter_blocks(blocks, axis_name):
    count = blocks.shape[0]
    here = lax.axis_index(axis_name)
    arrived = [
        lax.ppermute(pick(blocks, (here + step) % count), axis_name, shifted(step, count))
        for step in range(1, count)
    ]
    return pick(blocks, here), arrived


def ff_grad(left_turned, right):
    return weight_grad(left_turned, right).reshape(PLANES, -1, right.shape[1])


def halves_over_y(partials):
    here = lax.axis_index("y")
    split = [value.reshape(PLANES, CORES, -1, value.shape[-1]) for value in partials]
    sent = jnp.concatenate([pick(value, 1 - here, 1) for value in split], axis=-1)
    kept = [pick(value, here, 1) for value in split]
    return kept, swap(sent, "y"), sent


def chunks_over_z(kept, arrived):
    here = lax.axis_index("z")

    def chunk(step):
        plane = (here + step) % PLANES
        near = jnp.concatenate([pick(value, plane) for value in kept], axis=-1)
        return near.astype(F32) + pick(arrived, plane).astype(F32)

    own = chunk(0)
    sent = [chunk(step).astype(BF16) for step in range(1, PLANES)]
    return own, [
        lax.ppermute(value, "z", shifted(step + 1, PLANES)) for step, value in enumerate(sent)
    ], sent


def butterfly(value, axis_name):
    count = lax.axis_size(axis_name)
    step = 1
    while step < count:
        value = value + lax.ppermute(value, axis_name, [(src, src ^ step) for src in range(count)])
        step *= 2
    return value


def sum_in_order(value, arrived):
    here = lax.axis_index("z")
    values = jnp.stack([value, *arrived])
    total = pick(values, here)
    for plane in range(1, PLANES):
        total = total + pick(values, (here - plane) % PLANES)
    return total


def to_planes(chunks):
    here = lax.axis_index("z")
    arrived = [pick(chunks, here)]
    for step in range(1, PLANES):
        arrived.append(
            lax.ppermute(pick(chunks, (here + step) % PLANES), "z", shifted(step, PLANES))
        )
    return jnp.stack(arrived)


def from_planes(arrived):
    here = lax.axis_index("z")
    back = [arrived[0]]
    for step in range(1, PLANES):
        back.append(lax.ppermute(arrived[step], "z", shifted(-step, PLANES)))
    back = jnp.stack(back)
    return [pick(back, (chunk - here) % PLANES) for chunk in range(PLANES)]


def per_device(
    inputs,
    cotangent,
    segments,
    w_query,
    key_weight_master,
    value_weight_master,
    w_output,
    w_gate,
    w_up,
    w_down,
    moment_query,
    moment_key,
    moment_value,
    moment_output,
    moment_gate,
    moment_up,
    moment_down,
    norm_gains,
    gain_first,
    gain_second,
):
    rows = inputs.shape[1]
    complete_rows = segments.shape[1]
    ring = lax.axis_size("fsdp")
    place = lax.axis_index("fsdp")
    core = lax.axis_index("core")
    gain_attn = norm_gains[:MODEL_WIDTH]
    gain_mlp = norm_gains[MODEL_WIDTH : 2 * MODEL_WIDTH]
    gain_query = norm_gains[2 * MODEL_WIDTH : 2 * MODEL_WIDTH + HEAD_SIZE]
    gain_key = norm_gains[2 * MODEL_WIDTH + HEAD_SIZE :]

    attention_rows = gather_rows(
        jnp.concatenate(
            [
                key_weight_master.astype(BF16),
                value_weight_master.astype(BF16),
                w_query.astype(BF16).T,
                w_output.astype(BF16),
            ],
            axis=1,
        ),
        SHARDS,
    )
    key_value_rows = attention_rows[:, :MODEL_WIDTH]
    query_rows = attention_rows[:, MODEL_WIDTH : 2 * MODEL_WIDTH]
    output_rows = attention_rows[:, 2 * MODEL_WIDTH :]
    gate_own, up_own_rows, down_own_rows = (
        gather_rows(shard, ("z",))
        for shard in (w_gate.astype(BF16).T, w_up.astype(BF16).T, w_down.astype(BF16))
    )

    masters = (w_query, key_weight_master, value_weight_master, w_output, w_gate, w_up, w_down)
    moments = (
        moment_query,
        moment_key,
        moment_value,
        moment_output,
        moment_gate,
        moment_up,
        moment_down,
    )
    full_sides = (MODEL_WIDTH,) * 4 + (FF,) * 3
    sideways = (True, False, False, False, True, True, False)

    def updated(shard, idx):
        grad = shard.T if sideways[idx] else shard
        moment = MOMENTUM * moments[idx] + grad
        update = grad + MOMENTUM * moment
        return grad, moment, (update.T if sideways[idx] else update).astype(BF16)

    both_segments = with_partner(segments)
    row_idx = jnp.arange(complete_rows, dtype=jnp.int32)
    boundary = jnp.concatenate(
        [
            jnp.ones((CORES, 1), dtype=bool),
            both_segments[:, 1:] != both_segments[:, :-1],
        ],
        axis=1,
    )
    doc_start = lax.cummax(jnp.where(boundary, row_idx[None, :], 0), axis=1)
    first_row = place * rows
    positions = lax.dynamic_slice_in_dim(row_idx[None, :] - doc_start, first_row, rows, 1)
    cosine_table, sine_table = rope_tables(positions, HEAD_SIZE)
    query_segments = lax.dynamic_slice_in_dim(both_segments, first_row, rows, 1)
    query_pos = first_row + jnp.arange(rows, dtype=jnp.int32)
    key_starts = [((place - step) % ring) * rows for step in range(ring)]
    key_pos = jnp.concatenate([at + jnp.arange(rows, dtype=jnp.int32) for at in key_starts])
    key_segments = jnp.concatenate(
        [lax.dynamic_slice_in_dim(both_segments, at, rows, 1) for at in key_starts], axis=1
    )
    mask = (
        (key_pos[None, :, None] <= query_pos[None, None, :])
        & (key_segments[:, :, None] == query_segments[:, None, :])
    ).astype(BF16)

    residual = inputs.astype(F32).reshape(rows, MODEL_WIDTH)
    normed = rms_scale(residual, gain_attn).astype(BF16)
    both_normed = with_partner(normed)
    cotangent_rows = cotangent.reshape(rows, MODEL_WIDTH)
    pair_rows = CORES * rows

    def own_columns(values):
        split = values.reshape(values.shape[0], -1, CORES, HEAD_SIZE)
        return pick(split, core, 2).reshape(values.shape[0], MODEL_WIDTH // CORES)

    own_normed = own_columns(both_normed)
    kv_sent = dot_nn(own_normed[rows:], key_value_rows).astype(BF16)
    kv_near = dot_nn(own_normed[:rows], key_value_rows)
    q_proj = dot_nt(both_normed, query_rows)
    kv_proj, kv_low = key_value_chain(
        kv_near, swap(kv_sent), gain_key[None], cosine_table[0], sine_table[0]
    )
    kv_blocks, gate_own = after((ring_blocks(kv_low, "fsdp", ring), gate_own), q_proj)
    gate_other = swap(gate_own, "y")
    own_kv = jnp.concatenate(kv_blocks, axis=0)
    both_kv = with_partner(own_kv).reshape(CORES, complete_rows, 2 * KV_WIDTH)
    attention_inputs = (q_proj, both_kv, mask, gain_query[None], cosine_table, sine_table)
    att_low, att_turned = attention(*attention_inputs)
    cotangent_blocks = ring_blocks(after(cotangent_rows, own_kv), "fsdp", ring)
    att_low, cotangent_blocks = lax.optimization_barrier((att_low, cotangent_blocks))
    team_cotangent = with_partner(jnp.concatenate(cotangent_blocks, axis=0))
    out_sent = dot_nn(att_low[rows:], output_rows).astype(BF16)
    out_near = dot_nn(att_low[:rows], output_rows)
    out_sent, out_near, gate_other, up_own_rows = lax.optimization_barrier(
        (out_sent, out_near, gate_other, up_own_rows)
    )
    up_other = swap(up_own_rows, "y")
    middle = residual + out_near + swap(out_sent).astype(F32)

    normed_two = rms_scale(middle, gain_mlp).astype(BF16)
    two_blocks, down_own_rows, up_other = after(
        (ring_blocks(normed_two, "fsdp", ring), down_own_rows, up_other), team_cotangent
    )
    down_other = swap(down_own_rows, "y")
    team_two = with_partner(jnp.concatenate(two_blocks, axis=0))
    own_rows = ring * rows
    hidden, d_gate, d_up, hidden_turned, d_gate_turned, d_up_turned = swiglu_both_ways(
        team_two, team_cotangent, gate_own, up_own_rows, down_own_rows
    )
    down_kept = ff_grad(hidden_turned, team_cotangent)
    gate_kept = ff_grad(after(d_gate_turned, down_kept), team_two)
    up_kept = ff_grad(after(d_up_turned, gate_kept), team_two)
    (
        far_hidden,
        far_d_gate,
        far_d_up,
        far_hidden_turned,
        far_d_gate_turned,
        far_d_up_turned,
    ) = swiglu_both_ways(
        team_two, team_cotangent, gate_other, up_other, after(down_other, up_kept)
    )
    down_sent = ff_grad(far_hidden_turned, team_cotangent)
    down_passed = swap(down_sent, "y")
    gate_sent = ff_grad(after(far_d_gate_turned, down_sent), team_two)
    gate_passed = swap(gate_sent, "y")
    back_lefts = after((d_gate, d_up, far_d_gate, far_d_up), gate_sent)
    back_rights = (gate_own, up_own_rows, gate_other, up_other)
    back_far = back_to_width(back_lefts, back_rights, own_rows, own_rows)
    back_near = back_to_width(after(back_lefts, back_far), back_rights, 0, own_rows)
    down_own, down_chunks, down_chunks_sent = chunks_over_z(
        [down_kept], after(down_passed, back_near)
    )
    back_half = back_near.astype(F32) + swap(after(back_far, down_chunks_sent)).astype(F32)
    back_half = back_half.reshape(ring, rows, MODEL_WIDTH)
    back_arrived = ring_send([back_half[step] for step in range(ring)], "fsdp", ring)
    up_sent = ff_grad(after(far_d_up_turned, back_half), team_two)
    up_passed = swap(up_sent, "y")
    back_arrived, down_chunks = after((back_arrived, down_chunks), up_sent)
    d_normed_two = add_all(after(back_half[0], down_chunks), back_arrived)
    second_back = jax.vjp(rms_scale, middle, gain_mlp)[1]
    d_mid_norm, d_gain_mlp = second_back(d_normed_two)
    d_middle = cotangent_rows.astype(F32) + d_mid_norm
    d_middle, gate_passed = lax.optimization_barrier((d_middle, gate_passed))

    both_mid = with_partner(d_middle.astype(BF16))
    gate_own, gate_chunks, gate_chunks_sent = chunks_over_z([gate_kept], gate_passed)
    output_grad = weight_grad(att_turned, after(both_mid, gate_chunks_sent))
    output_blocks = jnp.moveaxis(output_grad.reshape(PLANES * CORES, ring, -1, MODEL_WIDTH), 1, 0)
    output_own, output_arrived = scatter_blocks(output_blocks, "fsdp")
    d_head = times_rows(after(both_mid, output_grad), attention_rows, 2)
    *far_parts, d_kv_far, far_gain = attention_back(*attention_inputs, d_head, 1, ())
    q_low, q_low_turned, d_kv_near, near_gain = attention_back(
        *attention_inputs, d_head, 0, far_parts
    )
    d_gain_query = (far_gain + near_gain)[0]
    query_grad = weight_grad(q_low_turned, both_normed)
    from_query = times_columns(after(q_low, query_grad), attention_rows, MODEL_WIDTH, MODEL_WIDTH)
    query_blocks = jnp.moveaxis(query_grad.reshape(PLANES * CORES, ring, -1, MODEL_WIDTH), 1, 0)
    query_own, query_arrived = scatter_blocks(query_blocks, "fsdp")
    up_passed, gate_chunks, output_arrived = after(
        (up_passed, gate_chunks, output_arrived), from_query
    )
    up_own, up_chunks, up_chunks_sent = chunks_over_z([up_kept], up_passed)
    d_kv_half = d_kv_near.astype(F32) + swap(after(d_kv_far, up_chunks_sent)).astype(F32)
    d_kv_half = d_kv_half.reshape(2, ring, rows, KV_WIDTH)
    d_kv_arrived = ring_send([d_kv_half[:, step] for step in range(ring)], "fsdp", ring)
    hiddens = after((hidden, far_hidden), d_kv_half)
    down_rights = (down_own_rows, down_other)
    down_far = back_to_width(hiddens, down_rights, own_rows, own_rows)
    down_near = back_to_width(after(hiddens, down_far), down_rights, 0, own_rows)
    gate_new = updated(add_all(gate_own, gate_chunks), 4)
    down_new = updated(add_all(down_own, down_chunks), 6)
    up_chunks, d_kv_arrived, query_arrived = after(
        (up_chunks, d_kv_arrived, query_arrived), down_near
    )
    big = [gate_new, updated(add_all(up_own, up_chunks), 5), down_new]
    slots = jnp.stack([new[2] for new in big] + [jnp.zeros_like(down_new[2])])
    big_mine = to_planes(slots).reshape(-1, MODEL_WIDTH)
    first_kept, first_passed, first_sent = halves_over_y(
        [
            add_all(output_own.astype(F32), output_arrived).astype(BF16),
            add_all(query_own.astype(F32), query_arrived).astype(BF16),
        ]
    )
    d_kv_total = add_all(d_kv_half[:, 0], d_kv_arrived)
    kv_low_grad, d_gain_key = key_value_back(
        d_kv_total, kv_proj, gain_key[None], cosine_table[0], sine_table[0]
    )
    d_gain_key = d_gain_key[0]
    both_kv_low = with_partner(kv_low_grad)
    key_value_grad = dot_tn(own_normed, both_kv_low).astype(BF16)
    key_value_blocks = jnp.moveaxis(
        key_value_grad.reshape(PLANES * CORES, ring, -1, MODEL_WIDTH), 1, 0
    )
    key_value_own, key_value_arrived = scatter_blocks(key_value_blocks, "fsdp")
    plane = lax.axis_index("z")
    in_plane = ("y", "core", "fsdp")
    big_mine, key_value_arrived, first_passed = lax.optimization_barrier(
        (big_mine, key_value_arrived, first_passed)
    )
    big_gram = gram_blocks(big_mine)
    from_query, down_far, first_passed, key_value_arrived = after(
        (from_query, down_far, first_passed, key_value_arrived), big_gram
    )
    down_half = (down_near.astype(F32) + swap(down_far).astype(F32)).reshape(
        ring, rows, MODEL_WIDTH
    )
    kept, arrived, attention_passed = halves_over_y(
        [add_all(key_value_own.astype(F32), key_value_arrived).astype(BF16)]
    )
    first_own, first_chunks, first_chunks_sent = chunks_over_z(first_kept, first_passed)
    from_kv = times_rows(
        after(both_kv_low, attention_passed, first_chunks_sent), attention_rows, 0
    )
    big_gram = lax.psum(big_gram, in_plane)
    arrived, first_chunks = after((arrived, first_chunks), from_kv)
    last_own, last_chunks, last_chunks_sent = chunks_over_z(kept, arrived)
    from_kv = after(from_kv, last_chunks_sent)

    from_query = from_query[:rows].astype(F32) + swap(from_query[rows:]).astype(F32)
    kv_here = from_kv[:rows].reshape(rows, -1, HEAD_SIZE)
    kv_there = swap(from_kv[rows:]).reshape(rows, -1, HEAD_SIZE)
    from_kv_full = jnp.stack(
        [jnp.where(core == 0, kv_here, kv_there), jnp.where(core == 0, kv_there, kv_here)], axis=2
    ).reshape(rows, MODEL_WIDTH)
    d_normed = from_query + from_kv_full.astype(F32)
    first_back = jax.vjp(rms_scale, residual, gain_attn)[1]
    d_residual, d_gain_attn = first_back(d_normed)
    input_grad = (d_middle + d_residual).reshape(inputs.shape)
    gain_grad = jnp.concatenate([d_gain_attn, d_gain_mlp, d_gain_query, d_gain_key])

    first_total = add_all(first_own, first_chunks)
    output_new = updated(first_total[:, :MODEL_WIDTH], 3)
    query_new = updated(first_total[:, MODEL_WIDTH:], 0)
    last_chunks, big_gram, gain_grad, down_half, output_new, query_new = after(
        (
            last_chunks,
            big_gram,
            butterfly(butterfly(gain_grad, "core"), "fsdp"),
            down_half,
            output_new,
            query_new,
        ),
        input_grad,
    )
    key_value_shard = add_all(last_own, last_chunks)
    small = [
        query_new,
        updated(key_value_shard[:, :KV_WIDTH], 1),
        updated(key_value_shard[:, KV_WIDTH:], 2),
        output_new,
    ]
    small_slots = jnp.stack(
        [
            small[0][2],
            jnp.concatenate([small[1][2], small[2][2]], axis=1),
            small[3][2],
            jnp.zeros_like(small[3][2]),
        ]
    )
    small_mine = to_planes(small_slots).reshape(-1, MODEL_WIDTH)
    small_mine, gain_grad = lax.optimization_barrier((small_mine, butterfly(gain_grad, "y")))
    whole = gather_rows(small_mine, in_plane)
    turned = muon(after(big_mine, small_mine), big_gram, jnp.bool_(False))
    turned, whole, gain_arrived = lax.optimization_barrier(
        (turned, whole, ring_blocks(gain_grad, "z", PLANES)[1:])
    )
    gain_grad = sum_in_order(gain_grad, gain_arrived)
    returned = from_planes(turned.reshape(PLANES, -1, MODEL_WIDTH))
    small_gram = gram_blocks(whole)
    down_arrived = ring_send(
        [after(down_half, turned)[step] for step in range(ring)], "fsdp", ring
    )
    turned, returned, down_arrived = lax.optimization_barrier(
        (muon(small_mine, small_gram, plane == 1), returned, down_arrived)
    )
    small_returned = from_planes(turned.reshape(small_slots.shape))
    block_out = (middle + add_all(down_half[0], down_arrived)).astype(BF16).reshape(inputs.shape)
    ortho = (
        small_returned[0],
        small_returned[1][:, :KV_WIDTH],
        small_returned[1][:, KV_WIDTH:],
        small_returned[2],
        *returned[:3],
    )
    new_weights = tuple(
        master * (1.0 - LR_MUON * DECAY_MUON)
        - LR_MUON * math.sqrt(side) * (rows_now.T if turn else rows_now).astype(F32)
        for master, rows_now, turn, side in zip(masters, ortho, sideways, full_sides)
    )

    first_new = BETA_ONE * gain_first + (1.0 - BETA_ONE) * gain_grad
    second_new = BETA_TWO * gain_second + (1.0 - BETA_TWO) * gain_grad * gain_grad
    corr_one = 1.0 - BETA_ONE**ADAM_STEP
    corr_two = 1.0 - BETA_TWO**ADAM_STEP
    gains_new = norm_gains - LR_GAIN * (first_new / corr_one) / (
        jnp.sqrt(second_new / corr_two) + EPS_ADAM
    )
    return (
        block_out,
        input_grad,
        *(grad for grad, _, _ in small + big),
        *(moment for _, moment, _ in small + big),
        *new_weights,
        first_new,
        second_new,
        gains_new,
    )


def solution(mesh):
    dp_size, fsdp_size = mesh.devices.shape
    fine_mesh = Mesh(
        mesh.devices.reshape(PLANES, dp_size // (PLANES * CORES), CORES, fsdp_size),
        ("z", "y", "core", "fsdp"),
    )
    dp = ("z", "y", "core")
    tokens = P(dp, "fsdp", None)
    by_row = P(EVERYWHERE, None)
    by_col = P(None, EVERYWHERE)
    matrices = (by_col, by_row, by_row, by_row, by_col, by_col, by_row)
    return jax.shard_map(
        per_device,
        mesh=fine_mesh,
        in_specs=(tokens, tokens, P(dp, None), *matrices, *matrices, P(), P(), P()),
        out_specs=(tokens, tokens, *matrices, *matrices, *matrices, P(), P(), P()),
        check_vma=False,
    )
```

```python
import functools
import math

import jax
import jax.numpy as jnp
from jax import lax
from jax.experimental import pallas as pl
from jax.experimental.pallas import tpu as pltpu
from jax.sharding import Mesh
from jax.sharding import PartitionSpec as P

MODEL_WIDTH = 2048
QUERY_HEADS = 16
KEY_VALUE_HEADS = 8
HEAD_SIZE = 128
FF = 6144
ADAM_STEP = 10

EPS_NORM = 1e-06
THETA = 1000000.0
NEG_FILL = -1e30
MOMENTUM = 0.95
NS_A = 3.4445
NS_B = -4.775
NS_C = 2.0315
NS_EPS = 1e-07
LR_MUON = 0.2
DECAY_MUON = 0.01
LR_GAIN = 0.5
BETA_ONE = 0.9
BETA_TWO = 0.95
EPS_ADAM = 1e-08

CORES = 2
PLANES = 4
GRAM_TILE = 512
KV_WIDTH = KEY_VALUE_HEADS * HEAD_SIZE
BF16 = jnp.bfloat16
F32 = jnp.float32
SHARDS = ("z", "y", "fsdp")
EVERYWHERE = ("z", "y", "core", "fsdp")


def rms_scale(values, gain):
    return values * lax.rsqrt(jnp.mean(values * values, axis=-1, keepdims=True) + EPS_NORM) * gain


def rope_tables(positions, head_width):
    half_width = head_width // 2
    freq = jnp.exp(
        -(2.0 * jnp.arange(half_width, dtype=jnp.float32) / head_width) * math.log(THETA)
    )
    angle = positions.astype(jnp.float32)[..., None] * freq
    cosine = jnp.cos(angle)
    sine = jnp.sin(angle)
    return jnp.concatenate([cosine, cosine], -1), jnp.concatenate([-sine, sine], -1)


def dot_nn(left, right):
    return lax.dot_general(left, right, (((1,), (0,)), ((), ())), preferred_element_type=F32)


def dot_nt(left, right):
    return lax.dot_general(left, right, (((1,), (1,)), ((), ())), preferred_element_type=F32)


def dot_tn(left, right):
    return lax.dot_general(left, right, (((0,), (0,)), ((), ())), preferred_element_type=F32)


def gram_pairs(width):
    count = width // GRAM_TILE
    return [(i, j) for i in range(count) for j in range(i, count)]


def head_chain(head, gain, cosine, sine):
    scaled = head * lax.rsqrt(jnp.mean(head * head, axis=-1, keepdims=True) + EPS_NORM) * gain
    return scaled * cosine + pltpu.roll(scaled, HEAD_SIZE // 2, 1) * sine


def head_chain_back(head, gain, cosine, sine, grad):
    grad = grad * cosine + pltpu.roll(grad * sine, HEAD_SIZE // 2, 1)
    scale = lax.rsqrt(jnp.mean(head * head, axis=-1, keepdims=True) + EPS_NORM)
    unit = head * scale
    d_gain = jnp.sum(grad * unit, axis=0, keepdims=True)
    grad = grad * gain
    return scale * (grad - unit * jnp.mean(grad * unit, axis=-1, keepdims=True)), d_gain


def key_value_kernel(near_ref, far_ref, gain_ref, cos_ref, sin_ref, proj_ref, low_ref):
    proj = near_ref[...] + far_ref[...].astype(F32)
    proj_ref[...] = proj
    is_key = pl.program_id(0) < KEY_VALUE_HEADS

    @pl.when(is_key)
    def _():
        low_ref[...] = head_chain(proj, gain_ref[...], cos_ref[...], sin_ref[...]).astype(BF16)

    @pl.when(jnp.logical_not(is_key))
    def _():
        low_ref[...] = proj.astype(BF16)


def key_value_back_kernel(grad_ref, proj_ref, gain_ref, cos_ref, sin_ref, low_ref, d_gain_ref):
    head = pl.program_id(0)

    @pl.when(head == 0)
    def _():
        d_gain_ref[...] = jnp.zeros_like(d_gain_ref)

    @pl.when(head < KEY_VALUE_HEADS)
    def _():
        d_proj, d_gain = head_chain_back(
            proj_ref[...], gain_ref[...], cos_ref[...], sin_ref[...], grad_ref[0]
        )
        low_ref[...] = d_proj.astype(BF16)
        d_gain_ref[...] += d_gain

    @pl.when(head >= KEY_VALUE_HEADS)
    def _():
        low_ref[...] = grad_ref[0].astype(BF16)


def attention_weights(q_ref, k_ref, mask_ref, gain_ref, cos_ref, sin_ref):
    query = head_chain(q_ref[...], gain_ref[...], cos_ref[0], sin_ref[0]).astype(BF16)
    scores = dot_nt(k_ref[0], query)
    weights = jnp.exp2(scores * (HEAD_SIZE ** (-0.5) * math.log2(math.e)))
    return query, weights * mask_ref[0].astype(F32)


def attention_kernel(
    q_ref, k_ref, v_ref, mask_ref, gain_ref, cos_ref, sin_ref, out_ref, out_turned_ref
):
    _, weights = attention_weights(q_ref, k_ref, mask_ref, gain_ref, cos_ref, sin_ref)
    total = jnp.sum(weights, axis=0, keepdims=True)
    out = dot_tn(v_ref[0], weights.astype(BF16)) * (1.0 / total)
    out_turned_ref[...] = out.astype(BF16)
    out_ref[...] = out.T.astype(BF16)


def attention_back_kernel(
    q_ref, k_ref, v_ref, mask_ref, gain_ref, cos_ref, sin_ref, grad_ref,
    *refs,
):
    q_low_ref, q_low_turned_ref, d_kv_ref, d_gain_ref = refs[-4:]

    @pl.when(pl.program_id(0) == 0)
    def _():
        d_gain_ref[...] = jnp.zeros_like(d_gain_ref)

    query, weights = attention_weights(q_ref, k_ref, mask_ref, gain_ref, cos_ref, sin_ref)
    grad = grad_ref[...]
    probs = weights * (1.0 / jnp.sum(weights, axis=0, keepdims=True))
    d_probs = dot_nt(v_ref[0], grad)
    delta = jnp.sum(probs * d_probs, axis=0, keepdims=True)
    d_scores = (probs * (d_probs - delta)).astype(BF16)
    d_value = dot_nn(probs.astype(BF16), grad).astype(BF16)
    d_key = (dot_nn(d_scores, query) * HEAD_SIZE ** (-0.5)).astype(BF16)

    d_kv_ref[0] = d_key
    d_kv_ref[1] = d_value
    d_query = dot_tn(k_ref[0], d_scores).T * HEAD_SIZE ** (-0.5)
    d_proj, d_gain = head_chain_back(
        q_ref[...], gain_ref[...], cos_ref[0], sin_ref[0], d_query
    )
    q_low_ref[...] = d_proj.astype(BF16)
    q_low_turned_ref[...] = d_proj.T.astype(BF16)
    d_gain_ref[...] += d_gain


def swiglu_kernel(two_ref, cot_ref, gate_ref, up_ref, down_ref, *out_refs):
    two = two_ref[...]
    gate = dot_nt(two, gate_ref[...])
    up = dot_nt(two, up_ref[...])
    d_hidden = dot_nt(cot_ref[...], down_ref[...])
    sig = 1.0 / (1.0 + jnp.exp(-gate))
    silu = gate * sig
    results = (silu * up, d_hidden * up * sig * (1.0 + gate * (1.0 - sig)), d_hidden * silu)
    for result, out_ref, turned_ref in zip(results, out_refs[:3], out_refs[3:]):
        low = result.astype(BF16)
        out_ref[...] = low
        turned_ref[...] = low.T


def back_to_width_kernel(count, *refs):
    lefts, rights, out_ref = refs[:count], refs[count : 2 * count], refs[-1]
    total = 0.0
    for left, right in zip(lefts, rights):
        total = total + dot_nn(left[...], right[...])
    out_ref[...] = total.astype(BF16)


def weight_grad_kernel(left_ref, right_ref, out_ref):
    out_ref[...] = dot_nn(left_ref[...], right_ref[...]).astype(BF16)


def gram_kernel(first_ref, second_ref, left_ref, right_ref, out_ref):
    out_ref[0] = dot_tn(left_ref[...], right_ref[...]).astype(BF16)


def muon_kernel(
    halves_ref, update_ref, packed_ref, out_ref,
    start_ref, gram_ref, bend_ref, first_ref, product_ref, one_ref, two_ref,
):
    width = update_ref.shape[1]
    tile = GRAM_TILE
    count = width // tile
    one_matrix = (1 - halves_ref[0]).astype(F32)
    index = lax.broadcasted_iota(jnp.int32, (tile, tile), 0)
    on_diagonal = index == lax.broadcasted_iota(jnp.int32, (tile, tile), 1)
    traces = [0.0, 0.0]
    for place, (i, j) in enumerate(gram_pairs(width)):
        if i == j:
            block = jnp.where(on_diagonal, packed_ref[place].astype(F32), 0.0)
            block = jnp.sum(jnp.sum(block, axis=0, keepdims=True), axis=1, keepdims=True)
            traces[2 * i // count] = traces[2 * i // count] + block
    inverse = [
        1.0 / (jnp.sqrt(traces[half] + one_matrix * traces[1 - half]) + NS_EPS) for half in range(2)
    ]
    middle = width // 2
    start_ref[:, :middle] = (update_ref[:, :middle].astype(F32) * inverse[0]).astype(BF16)
    start_ref[:, middle:] = (update_ref[:, middle:].astype(F32) * inverse[1]).astype(BF16)

    def put(ref, i, j, value):
        ref[i * tile : (i + 1) * tile, j * tile : (j + 1) * tile] = value
        if i != j:
            ref[j * tile : (j + 1) * tile, i * tile : (i + 1) * tile] = value.T

    for place, (i, j) in enumerate(gram_pairs(width)):
        block = packed_ref[place].astype(F32) * inverse[2 * i // count] * inverse[2 * j // count]
        if 2 * i < count <= 2 * j:
            block = block * one_matrix
        put(gram_ref, i, j, block.astype(BF16))
    for i, j in gram_pairs(width):
        rows, cols = slice(i * tile, (i + 1) * tile), slice(j * tile, (j + 1) * tile)
        square = dot_nn(gram_ref[rows, :], gram_ref[:, cols])
        put(bend_ref, i, j, (NS_B * gram_ref[rows, cols].astype(F32) + NS_C * square).astype(BF16))

    def columns(body):
        @pl.loop(0, count)
        def _(step):
            body(pl.ds(pl.multiple_of(step * tile, tile), tile))

    def times_p(rows_ref, cols):
        return NS_A * rows_ref[:, cols].astype(F32) + dot_nn(rows_ref[...], bend_ref[:, cols])

    def to_first(cols):
        first_ref[:, cols] = times_p(start_ref, cols).astype(BF16)

    def bent_first(cols):
        one_ref[:, cols] = times_p(first_ref, cols).astype(BF16)

    def by_gram(cols):
        two_ref[:, cols] = dot_nn(one_ref[...], gram_ref[:, cols]).astype(BF16)

    def to_product(cols):
        product_ref[:, cols] = times_p(two_ref, cols).astype(BF16)

    def bent_product(cols):
        one_ref[:, cols] = times_p(product_ref, cols).astype(BF16)

    def finish(cols):
        again = times_p(two_ref, cols)
        out_ref[:, cols] = (
            NS_A * first_ref[:, cols].astype(F32)
            + NS_B * product_ref[:, cols].astype(F32)
            + NS_C * again
        ).astype(BF16)

    for body in (to_first, bent_first, by_gram, to_product, bent_product, by_gram, finish):
        columns(body)


def shaped(shape, dtype):
    return jax.ShapeDtypeStruct(shape, dtype)


SMALL = pl.CostEstimate(flops=1, bytes_accessed=1, transcendentals=0)


def limits(mebibytes):
    return pltpu.CompilerParams(vmem_limit_bytes=mebibytes * 1024 * 1024)


def key_value_chain(near, far, gain, cosine, sine):
    rows = near.shape[0]
    block = pl.BlockSpec((rows, HEAD_SIZE), lambda head: (0, head))
    fixed = pl.BlockSpec((rows, HEAD_SIZE), lambda head: (0, 0))
    one = pl.BlockSpec((1, HEAD_SIZE), lambda head: (0, 0))
    return pl.pallas_call(
        key_value_kernel,
        grid=(2 * KEY_VALUE_HEADS,),
        in_specs=[block, block, one, fixed, fixed],
        out_specs=[block, block],
        out_shape=[shaped(near.shape, F32), shaped(near.shape, BF16)],
        compiler_params=limits(16),
        cost_estimate=SMALL,
        name="key_value_chain",
    )(near, far, gain, cosine, sine)


def key_value_back(grad, proj, gain, cosine, sine):
    rows = proj.shape[0]
    heads = KEY_VALUE_HEADS
    block = pl.BlockSpec((rows, HEAD_SIZE), lambda head: (0, head))
    split = pl.BlockSpec((1, rows, HEAD_SIZE), lambda head: (head // heads, 0, head % heads))
    fixed = pl.BlockSpec((rows, HEAD_SIZE), lambda head: (0, 0))
    one = pl.BlockSpec((1, HEAD_SIZE), lambda head: (0, 0))
    return pl.pallas_call(
        key_value_back_kernel,
        grid=(2 * heads,),
        in_specs=[split, block, one, fixed, fixed],
        out_specs=[block, one],
        out_shape=[shaped(proj.shape, BF16), shaped((1, HEAD_SIZE), F32)],
        compiler_params=limits(16),
        cost_estimate=SMALL,
        name="key_value_back",
    )(grad, proj, gain, cosine, sine)


def attention_specs(rows, keys, heads):
    return [
        pl.BlockSpec((rows, HEAD_SIZE), lambda seq, head: (seq, head)),
        pl.BlockSpec((1, keys, HEAD_SIZE), lambda seq, head: (seq, 0, head)),
        pl.BlockSpec((1, keys, HEAD_SIZE), lambda seq, head: (seq, 0, heads + head)),
        pl.BlockSpec((1, keys, rows), lambda seq, head: (seq, 0, 0)),
        pl.BlockSpec((1, HEAD_SIZE), lambda seq, head: (0, 0)),
        pl.BlockSpec((1, rows, HEAD_SIZE), lambda seq, head: (seq, 0, 0)),
        pl.BlockSpec((1, rows, HEAD_SIZE), lambda seq, head: (seq, 0, 0)),
    ]


def attention(q_proj, kv, mask, gain, cosine, sine):
    sequences, keys, rows = mask.shape
    heads = q_proj.shape[1] // HEAD_SIZE
    specs = attention_specs(rows, keys, heads)
    return pl.pallas_call(
        attention_kernel,
        grid=(sequences, heads),
        in_specs=specs,
        out_specs=[specs[0], pl.BlockSpec((HEAD_SIZE, rows), lambda seq, head: (head, seq))],
        out_shape=[shaped(q_proj.shape, BF16), shaped(q_proj.shape[::-1], BF16)],
        compiler_params=limits(40),
        cost_estimate=SMALL,
        name="attention",
    )(q_proj, kv, kv, mask, gain, cosine, sine)


def attention_back(q_proj, kv, mask, gain, cosine, sine, grad, seq, others):
    _, keys, rows = mask.shape
    heads = q_proj.shape[1] // HEAD_SIZE
    specs = [
        pl.BlockSpec((rows, HEAD_SIZE), lambda head: (seq, head)),
        pl.BlockSpec((1, keys, HEAD_SIZE), lambda head: (seq, 0, head)),
        pl.BlockSpec((1, keys, HEAD_SIZE), lambda head: (seq, 0, heads + head)),
        pl.BlockSpec((1, keys, rows), lambda head: (seq, 0, 0)),
        pl.BlockSpec((1, HEAD_SIZE), lambda head: (0, 0)),
        pl.BlockSpec((1, rows, HEAD_SIZE), lambda head: (seq, 0, 0)),
        pl.BlockSpec((1, rows, HEAD_SIZE), lambda head: (seq, 0, 0)),
    ]
    return pl.pallas_call(
        attention_back_kernel,
        grid=(heads,),
        in_specs=[*specs, specs[0]] + [pl.BlockSpec(memory_space=pl.ANY)] * len(others),
        out_specs=[
            specs[0],
            pl.BlockSpec((HEAD_SIZE, rows), lambda head: (head, seq)),
            pl.BlockSpec((2, keys, HEAD_SIZE), lambda head: (0, 0, head)),
            specs[4],
        ],
        out_shape=[
            shaped(q_proj.shape, BF16),
            shaped(q_proj.shape[::-1], BF16),
            shaped((2, keys, heads * HEAD_SIZE), BF16),
            shaped((1, HEAD_SIZE), F32),
        ],
        input_output_aliases={8 + place: place for place in range(len(others))},
        compiler_params=limits(48),
        cost_estimate=SMALL,
        name="attention_back",
    )(q_proj, kv, kv, mask, gain, cosine, sine, grad, *others)


def swiglu_both_ways(two, cot, gate, up, down):
    tokens, width = two.shape
    columns = gate.shape[0]
    tile = min(512, tokens)
    row_block = pl.BlockSpec((tile, width), lambda row: (row, 0))
    weights = pl.BlockSpec((columns, width), lambda row: (0, 0))
    return pl.pallas_call(
        swiglu_kernel,
        grid=(tokens // tile,),
        in_specs=[row_block, row_block] + [weights] * 3,
        out_specs=[pl.BlockSpec((tile, columns), lambda row: (row, 0))] * 3
        + [pl.BlockSpec((columns, tile), lambda row: (0, row))] * 3,
        out_shape=[shaped((tokens, columns), BF16)] * 3 + [shaped((columns, tokens), BF16)] * 3,
        compiler_params=limits(60),
        cost_estimate=SMALL,
        name="swiglu_both_ways",
    )(two, cot, gate, up, down)


def back_to_width(lefts, rights, first_row, rows):
    width = rights[0].shape[1]
    tile = min(256, rows)
    first = first_row // tile
    return pl.pallas_call(
        functools.partial(back_to_width_kernel, len(lefts)),
        grid=(rows // tile,),
        in_specs=[
            pl.BlockSpec((tile, left.shape[1]), lambda row: (first + row, 0)) for left in lefts
        ]
        + [pl.BlockSpec(right.shape, lambda row: (0, 0)) for right in rights],
        out_specs=pl.BlockSpec((tile, width), lambda row: (row, 0)),
        out_shape=shaped((rows, width), BF16),
        compiler_params=limits(56),
        cost_estimate=SMALL,
        name="back_to_width",
    )(*lefts, *rights)


def weight_grad(left_turned, right):
    rows, tokens = left_turned.shape
    width = right.shape[1]
    tile = min(512, width)
    return pl.pallas_call(
        weight_grad_kernel,
        grid=(width // tile,),
        in_specs=[
            pl.BlockSpec((rows, tokens), lambda col: (0, 0)),
            pl.BlockSpec((tokens, tile), lambda col: (0, col)),
        ],
        out_specs=pl.BlockSpec((rows, tile), lambda col: (0, col)),
        out_shape=shaped((rows, width), BF16),
        compiler_params=limits(40),
        cost_estimate=SMALL,
        name="weight_grad",
    )(left_turned, right)


def times_columns_kernel(left_ref, right_ref, out_ref):
    out_ref[...] = dot_nn(left_ref[...], right_ref[...]).astype(BF16)


def times_columns(left, right, first_column, width):
    rows, depth = left.shape
    tile = min(512, width)
    first = first_column // tile
    return pl.pallas_call(
        times_columns_kernel,
        grid=(width // tile,),
        in_specs=[
            pl.BlockSpec((rows, depth), lambda col: (0, 0)),
            pl.BlockSpec((depth, tile), lambda col: (0, first + col)),
        ],
        out_specs=pl.BlockSpec((rows, tile), lambda col: (0, col)),
        out_shape=shaped((rows, width), BF16),
        compiler_params=limits(40),
        cost_estimate=SMALL,
        name="times_columns",
    )(left, right)


def times_rows_kernel(left_ref, right_ref, out_ref):
    out_ref[...] = dot_nt(left_ref[...], right_ref[...]).astype(BF16)


def times_rows(left, right, place):
    rows, depth = left.shape
    columns = right.shape[0]
    tile = min(256, columns)
    return pl.pallas_call(
        times_rows_kernel,
        grid=(columns // tile,),
        in_specs=[
            pl.BlockSpec((rows, depth), lambda col: (0, 0)),
            pl.BlockSpec((tile, depth), lambda col: (col, place)),
        ],
        out_specs=pl.BlockSpec((rows, tile), lambda col: (0, col)),
        out_shape=shaped((rows, columns), BF16),
        compiler_params=limits(40),
        cost_estimate=SMALL,
        name="times_rows",
    )(left, right)


def gram_blocks(rows):
    depth, width = rows.shape
    pairs = gram_pairs(width)
    first = jnp.asarray([i for i, _ in pairs], jnp.int32)
    second = jnp.asarray([j for _, j in pairs], jnp.int32)
    shape = (len(pairs), GRAM_TILE, GRAM_TILE)
    return pl.pallas_call(
        gram_kernel,
        grid_spec=pltpu.PrefetchScalarGridSpec(
            num_scalar_prefetch=2,
            grid=(len(pairs),),
            in_specs=[
                pl.BlockSpec((depth, GRAM_TILE), lambda step, one, two: (0, one[step])),
                pl.BlockSpec((depth, GRAM_TILE), lambda step, one, two: (0, two[step])),
            ],
            out_specs=pl.BlockSpec((1, *shape[1:]), lambda step, one, two: (step, 0, 0)),
        ),
        out_shape=shaped(shape, BF16),
        compiler_params=limits(40),
        cost_estimate=SMALL,
        name="gram_blocks",
    )(first, second, rows, rows)


def muon(update, packed, halves):
    width = update.shape[1]
    once = dict(pipeline_mode=pl.Buffered(1))
    return pl.pallas_call(
        muon_kernel,
        grid=(),
        in_specs=[
            pl.BlockSpec(memory_space=pltpu.SMEM),
            pl.BlockSpec(update.shape, lambda: (0, 0), **once),
            pl.BlockSpec(packed.shape, lambda: (0, 0, 0), **once),
        ],
        out_specs=pl.BlockSpec(update.shape, lambda: (0, 0)),
        out_shape=shaped(update.shape, BF16),
        scratch_shapes=[pltpu.VMEM(update.shape, BF16)]
        + [pltpu.VMEM((width, width), BF16)] * 2
        + [pltpu.VMEM(update.shape, BF16)] * 4,
        compiler_params=limits(58),
        cost_estimate=SMALL,
        name="muon",
    )(jnp.asarray(halves, jnp.int32).reshape(1), update, packed)


def after(value, *earlier):
    return lax.optimization_barrier((value, earlier))[0]


def shifted(step, count):
    return [(src, (src + step) % count) for src in range(count)]


def swap(value, axis_name="core"):
    return lax.ppermute(value, axis_name, shifted(1, CORES))


def with_partner(value):
    return jnp.concatenate([value, swap(value)], axis=0)


def ring_blocks(value, axis_name, count):
    return [value] + [
        lax.ppermute(value, axis_name, shifted(step, count)) for step in range(1, count)
    ]


def ring_send(blocks, axis_name, count):
    return [
        lax.ppermute(blocks[step].astype(BF16), axis_name, shifted(-step, count))
        for step in range(1, count)
    ]


def add_all(own, arrived):
    for term in arrived:
        own = own + term.astype(F32)
    return own


def pick(blocks, index, axis=0):
    return lax.dynamic_index_in_dim(blocks, index, axis, keepdims=False)


def gather_rows(shard, axes):
    return lax.all_gather(shard, axes, axis=0, tiled=True)


def scatter_blocks(blocks, axis_name):
    count = blocks.shape[0]
    here = lax.axis_index(axis_name)
    arrived = [
        lax.ppermute(pick(blocks, (here + step) % count), axis_name, shifted(step, count))
        for step in range(1, count)
    ]
    return pick(blocks, here), arrived


def ff_grad(left_turned, right):
    return weight_grad(left_turned, right).reshape(PLANES, -1, right.shape[1])


def halves_over_y(partials):
    here = lax.axis_index("y")
    split = [value.reshape(PLANES, CORES, -1, value.shape[-1]) for value in partials]
    sent = jnp.concatenate([pick(value, 1 - here, 1) for value in split], axis=-1)
    kept = [pick(value, here, 1) for value in split]
    return kept, swap(sent, "y"), sent


def chunks_over_z(kept, arrived):
    here = lax.axis_index("z")

    def chunk(step):
        plane = (here + step) % PLANES
        near = jnp.concatenate([pick(value, plane) for value in kept], axis=-1)
        return near.astype(F32) + pick(arrived, plane).astype(F32)

    own = chunk(0)
    sent = [chunk(step).astype(BF16) for step in range(1, PLANES)]
    return own, [
        lax.ppermute(value, "z", shifted(step + 1, PLANES)) for step, value in enumerate(sent)
    ], sent


def butterfly(value, axis_name):
    count = lax.axis_size(axis_name)
    step = 1
    while step < count:
        value = value + lax.ppermute(value, axis_name, [(src, src ^ step) for src in range(count)])
        step *= 2
    return value


def sum_in_order(value, arrived):
    here = lax.axis_index("z")
    values = jnp.stack([value, *arrived])
    total = pick(values, here)
    for plane in range(1, PLANES):
        total = total + pick(values, (here - plane) % PLANES)
    return total


def to_planes(chunks):
    here = lax.axis_index("z")
    arrived = [pick(chunks, here)]
    for step in range(1, PLANES):
        arrived.append(
            lax.ppermute(pick(chunks, (here + step) % PLANES), "z", shifted(step, PLANES))
        )
    return jnp.stack(arrived)


def from_planes(arrived):
    here = lax.axis_index("z")
    back = [arrived[0]]
    for step in range(1, PLANES):
        back.append(lax.ppermute(arrived[step], "z", shifted(-step, PLANES)))
    back = jnp.stack(back)
    return [pick(back, (chunk - here) % PLANES) for chunk in range(PLANES)]


def per_device(
    inputs,
    cotangent,
    segments,
    w_query,
    key_weight_master,
    value_weight_master,
    w_output,
    w_gate,
    w_up,
    w_down,
    moment_query,
    moment_key,
    moment_value,
    moment_output,
    moment_gate,
    moment_up,
    moment_down,
    norm_gains,
    gain_first,
    gain_second,
):
    rows = inputs.shape[1]
    complete_rows = segments.shape[1]
    ring = lax.axis_size("fsdp")
    place = lax.axis_index("fsdp")
    core = lax.axis_index("core")
    gain_attn = norm_gains[:MODEL_WIDTH]
    gain_mlp = norm_gains[MODEL_WIDTH : 2 * MODEL_WIDTH]
    gain_query = norm_gains[2 * MODEL_WIDTH : 2 * MODEL_WIDTH + HEAD_SIZE]
    gain_key = norm_gains[2 * MODEL_WIDTH + HEAD_SIZE :]

    attention_rows = gather_rows(
        jnp.concatenate(
            [
                key_weight_master.astype(BF16),
                value_weight_master.astype(BF16),
                w_query.astype(BF16).T,
                w_output.astype(BF16),
            ],
            axis=1,
        ),
        SHARDS,
    )
    key_value_rows = attention_rows[:, :MODEL_WIDTH]
    query_rows = attention_rows[:, MODEL_WIDTH : 2 * MODEL_WIDTH]
    output_rows = attention_rows[:, 2 * MODEL_WIDTH :]
    gate_own, up_own_rows, down_own_rows = (
        gather_rows(shard, ("z",))
        for shard in (w_gate.astype(BF16).T, w_up.astype(BF16).T, w_down.astype(BF16))
    )

    masters = (w_query, key_weight_master, value_weight_master, w_output, w_gate, w_up, w_down)
    moments = (
        moment_query,
        moment_key,
        moment_value,
        moment_output,
        moment_gate,
        moment_up,
        moment_down,
    )
    full_sides = (MODEL_WIDTH,) * 4 + (FF,) * 3
    sideways = (True, False, False, False, True, True, False)

    def updated(shard, idx):
        grad = shard.T if sideways[idx] else shard
        moment = MOMENTUM * moments[idx] + grad
        update = grad + MOMENTUM * moment
        return grad, moment, (update.T if sideways[idx] else update).astype(BF16)

    both_segments = with_partner(segments)
    row_idx = jnp.arange(complete_rows, dtype=jnp.int32)
    boundary = jnp.concatenate(
        [
            jnp.ones((CORES, 1), dtype=bool),
            both_segments[:, 1:] != both_segments[:, :-1],
        ],
        axis=1,
    )
    doc_start = lax.cummax(jnp.where(boundary, row_idx[None, :], 0), axis=1)
    first_row = place * rows
    positions = lax.dynamic_slice_in_dim(row_idx[None, :] - doc_start, first_row, rows, 1)
    cosine_table, sine_table = rope_tables(positions, HEAD_SIZE)
    query_segments = lax.dynamic_slice_in_dim(both_segments, first_row, rows, 1)
    query_pos = first_row + jnp.arange(rows, dtype=jnp.int32)
    key_starts = [((place - step) % ring) * rows for step in range(ring)]
    key_pos = jnp.concatenate([at + jnp.arange(rows, dtype=jnp.int32) for at in key_starts])
    key_segments = jnp.concatenate(
        [lax.dynamic_slice_in_dim(both_segments, at, rows, 1) for at in key_starts], axis=1
    )
    mask = (
        (key_pos[None, :, None] <= query_pos[None, None, :])
        & (key_segments[:, :, None] == query_segments[:, None, :])
    ).astype(BF16)

    residual = inputs.astype(F32).reshape(rows, MODEL_WIDTH)
    normed = rms_scale(residual, gain_attn).astype(BF16)
    both_normed = with_partner(normed)
    cotangent_rows = cotangent.reshape(rows, MODEL_WIDTH)
    pair_rows = CORES * rows

    def own_columns(values):
        split = values.reshape(values.shape[0], -1, CORES, HEAD_SIZE)
        return pick(split, core, 2).reshape(values.shape[0], MODEL_WIDTH // CORES)

    own_normed = own_columns(both_normed)
    kv_sent = dot_nn(own_normed[rows:], key_value_rows).astype(BF16)
    kv_near = dot_nn(own_normed[:rows], key_value_rows)
    q_proj = dot_nt(both_normed, query_rows)
    kv_proj, kv_low = key_value_chain(
        kv_near, swap(kv_sent), gain_key[None], cosine_table[0], sine_table[0]
    )
    kv_blocks, gate_own = after((ring_blocks(kv_low, "fsdp", ring), gate_own), q_proj)
    gate_other = swap(gate_own, "y")
    own_kv = jnp.concatenate(kv_blocks, axis=0)
    both_kv = with_partner(own_kv).reshape(CORES, complete_rows, 2 * KV_WIDTH)
    attention_inputs = (q_proj, both_kv, mask, gain_query[None], cosine_table, sine_table)
    att_low, att_turned = attention(*attention_inputs)
    cotangent_blocks = ring_blocks(after(cotangent_rows, own_kv), "fsdp", ring)
    att_low, cotangent_blocks = lax.optimization_barrier((att_low, cotangent_blocks))
    team_cotangent = with_partner(jnp.concatenate(cotangent_blocks, axis=0))
    out_sent = dot_nn(att_low[rows:], output_rows).astype(BF16)
    out_near = dot_nn(att_low[:rows], output_rows)
    out_sent, out_near, gate_other, up_own_rows = lax.optimization_barrier(
        (out_sent, out_near, gate_other, up_own_rows)
    )
    up_other = swap(up_own_rows, "y")
    middle = residual + out_near + swap(out_sent).astype(F32)

    normed_two = rms_scale(middle, gain_mlp).astype(BF16)
    two_blocks, down_own_rows, up_other = after(
        (ring_blocks(normed_two, "fsdp", ring), down_own_rows, up_other), team_cotangent
    )
    down_other = swap(down_own_rows, "y")
    team_two = with_partner(jnp.concatenate(two_blocks, axis=0))
    own_rows = ring * rows
    hidden, d_gate, d_up, hidden_turned, d_gate_turned, d_up_turned = swiglu_both_ways(
        team_two, team_cotangent, gate_own, up_own_rows, down_own_rows
    )
    down_kept = ff_grad(hidden_turned, team_cotangent)
    gate_kept = ff_grad(after(d_gate_turned, down_kept), team_two)
    up_kept = ff_grad(after(d_up_turned, gate_kept), team_two)
    (
        far_hidden,
        far_d_gate,
        far_d_up,
        far_hidden_turned,
        far_d_gate_turned,
        far_d_up_turned,
    ) = swiglu_both_ways(
        team_two, team_cotangent, gate_other, up_other, after(down_other, up_kept)
    )
    down_sent = ff_grad(far_hidden_turned, team_cotangent)
    down_passed = swap(down_sent, "y")
    gate_sent = ff_grad(after(far_d_gate_turned, down_sent), team_two)
    gate_passed = swap(gate_sent, "y")
    back_lefts = after((d_gate, d_up, far_d_gate, far_d_up), gate_sent)
    back_rights = (gate_own, up_own_rows, gate_other, up_other)
    back_far = back_to_width(back_lefts, back_rights, own_rows, own_rows)
    back_near = back_to_width(after(back_lefts, back_far), back_rights, 0, own_rows)
    down_own, down_chunks, down_chunks_sent = chunks_over_z(
        [down_kept], after(down_passed, back_near)
    )
    back_half = back_near.astype(F32) + swap(after(back_far, down_chunks_sent)).astype(F32)
    back_half = back_half.reshape(ring, rows, MODEL_WIDTH)
    back_arrived = ring_send([back_half[step] for step in range(ring)], "fsdp", ring)
    up_sent = ff_grad(after(far_d_up_turned, back_half), team_two)
    up_passed = swap(up_sent, "y")
    back_arrived, down_chunks = after((back_arrived, down_chunks), up_sent)
    d_normed_two = add_all(after(back_half[0], down_chunks), back_arrived)
    second_back = jax.vjp(rms_scale, middle, gain_mlp)[1]
    d_mid_norm, d_gain_mlp = second_back(d_normed_two)
    d_middle = cotangent_rows.astype(F32) + d_mid_norm
    d_middle, gate_passed = lax.optimization_barrier((d_middle, gate_passed))

    both_mid = with_partner(d_middle.astype(BF16))
    gate_own, gate_chunks, gate_chunks_sent = chunks_over_z([gate_kept], gate_passed)
    output_grad = weight_grad(att_turned, after(both_mid, gate_chunks_sent))
    output_blocks = jnp.moveaxis(output_grad.reshape(PLANES * CORES, ring, -1, MODEL_WIDTH), 1, 0)
    output_own, output_arrived = scatter_blocks(output_blocks, "fsdp")
    d_head = times_rows(after(both_mid, output_grad), attention_rows, 2)
    *far_parts, d_kv_far, far_gain = attention_back(*attention_inputs, d_head, 1, ())
    q_low, q_low_turned, d_kv_near, near_gain = attention_back(
        *attention_inputs, d_head, 0, far_parts
    )
    d_gain_query = (far_gain + near_gain)[0]
    query_grad = weight_grad(q_low_turned, both_normed)
    from_query = times_columns(after(q_low, query_grad), attention_rows, MODEL_WIDTH, MODEL_WIDTH)
    query_blocks = jnp.moveaxis(query_grad.reshape(PLANES * CORES, ring, -1, MODEL_WIDTH), 1, 0)
    up_passed, gate_chunks, output_arrived = after(
        (up_passed, gate_chunks, output_arrived), from_query
    )
    up_own, up_chunks, up_chunks_sent = chunks_over_z([up_kept], up_passed)
    d_kv_half = d_kv_near.astype(F32) + swap(after(d_kv_far, up_chunks_sent)).astype(F32)
    d_kv_half = d_kv_half.reshape(2, ring, rows, KV_WIDTH)
    d_kv_arrived = ring_send([d_kv_half[:, step] for step in range(ring)], "fsdp", ring)
    hiddens = after((hidden, far_hidden), d_kv_half)
    down_rights = (down_own_rows, down_other)
    down_far = back_to_width(hiddens, down_rights, own_rows, own_rows)
    down_near = back_to_width(after(hiddens, down_far), down_rights, 0, own_rows)
    gate_shard = add_all(gate_own, gate_chunks)
    down_shard = add_all(down_own, down_chunks)
    gate_form = updated(gate_shard, 4)[2]
    down_form = updated(down_shard, 6)[2]
    first_kept, first_passed, _ = halves_over_y(
        [add_all(output_own.astype(F32), output_arrived).astype(BF16)]
    )
    up_chunks, d_kv_arrived, first_passed = after((up_chunks, d_kv_arrived, first_passed), down_near)
    query_own, query_arrived = scatter_blocks(after(query_blocks, *d_kv_arrived), "fsdp")
    up_shard = add_all(up_own, up_chunks)
    slots = jnp.stack([gate_form, updated(up_shard, 5)[2], down_form, jnp.zeros_like(down_form)])
    big_mine = to_planes(slots).reshape(-1, MODEL_WIDTH)
    d_kv_total = add_all(d_kv_half[:, 0], d_kv_arrived)
    kv_low_grad, d_gain_key = key_value_back(
        d_kv_total, kv_proj, gain_key[None], cosine_table[0], sine_table[0]
    )
    d_gain_key = d_gain_key[0]
    both_kv_low = with_partner(kv_low_grad)
    key_value_grad = dot_tn(own_normed, both_kv_low).astype(BF16)
    key_value_blocks = jnp.moveaxis(
        key_value_grad.reshape(PLANES * CORES, ring, -1, MODEL_WIDTH), 1, 0
    )
    key_value_own, key_value_arrived = scatter_blocks(key_value_blocks, "fsdp")
    plane = lax.axis_index("z")
    in_plane = ("y", "core", "fsdp")
    big_mine, key_value_arrived, query_arrived = lax.optimization_barrier(
        (big_mine, key_value_arrived, query_arrived)
    )
    big_gram = gram_blocks(big_mine)
    from_query, down_far, query_arrived, key_value_arrived = after(
        (from_query, down_far, query_arrived, key_value_arrived), big_gram
    )
    down_half = (down_near.astype(F32) + swap(down_far).astype(F32)).reshape(
        ring, rows, MODEL_WIDTH
    )
    kept, arrived, attention_passed = halves_over_y(
        [
            add_all(query_own.astype(F32), query_arrived).astype(BF16),
            add_all(key_value_own.astype(F32), key_value_arrived).astype(BF16),
        ]
    )
    first_own, first_chunks, first_chunks_sent = chunks_over_z(
        first_kept, after(first_passed, attention_passed)
    )
    big_gram = lax.psum(big_gram, in_plane)
    arrived = after(arrived, first_chunks_sent)
    last_own, last_chunks, last_chunks_sent = chunks_over_z(kept, arrived)
    from_kv = dot_nt(after(both_kv_low, last_chunks_sent), key_value_rows).astype(BF16)

    from_query = from_query[:rows].astype(F32) + swap(from_query[rows:]).astype(F32)
    kv_here = from_kv[:rows].reshape(rows, -1, HEAD_SIZE)
    kv_there = swap(from_kv[rows:]).reshape(rows, -1, HEAD_SIZE)
    from_kv_full = jnp.stack(
        [jnp.where(core == 0, kv_here, kv_there), jnp.where(core == 0, kv_there, kv_here)], axis=2
    ).reshape(rows, MODEL_WIDTH)
    d_normed = from_query + from_kv_full.astype(F32)
    first_back = jax.vjp(rms_scale, residual, gain_attn)[1]
    d_residual, d_gain_attn = first_back(d_normed)
    input_grad = (d_middle + d_residual).reshape(inputs.shape)
    gain_grad = jnp.concatenate([d_gain_attn, d_gain_mlp, d_gain_query, d_gain_key])

    output_new = updated(add_all(first_own, first_chunks), 3)
    big = [
        updated(shard, idx)
        for shard, idx in zip(after((gate_shard, up_shard, down_shard), last_chunks_sent), (4, 5, 6))
    ]
    big = [(grad, moment) for grad, moment, _ in big]
    last_chunks, big_gram, gain_grad, down_half, output_new, big = after(
        (
            last_chunks,
            big_gram,
            butterfly(butterfly(gain_grad, "core"), "fsdp"),
            down_half,
            output_new,
            big,
        ),
        input_grad,
    )
    last_total = add_all(last_own, last_chunks)
    small = [
        updated(last_total[:, :MODEL_WIDTH], 0),
        updated(last_total[:, MODEL_WIDTH : MODEL_WIDTH + KV_WIDTH], 1),
        updated(last_total[:, MODEL_WIDTH + KV_WIDTH :], 2),
        output_new,
    ]
    small_slots = jnp.stack(
        [
            small[0][2],
            jnp.concatenate([small[1][2], small[2][2]], axis=1),
            small[3][2],
            jnp.zeros_like(small[3][2]),
        ]
    )
    small_mine = to_planes(small_slots).reshape(-1, MODEL_WIDTH)
    small_mine, gain_grad = lax.optimization_barrier((small_mine, butterfly(gain_grad, "y")))
    whole = gather_rows(small_mine, in_plane)
    turned = muon(after(big_mine, small_mine), big_gram, jnp.bool_(False))
    turned, whole, gain_arrived = lax.optimization_barrier(
        (turned, whole, ring_blocks(gain_grad, "z", PLANES)[1:])
    )
    gain_grad = sum_in_order(gain_grad, gain_arrived)
    returned = from_planes(turned.reshape(PLANES, -1, MODEL_WIDTH))
    small_gram = gram_blocks(whole)
    down_arrived = ring_send(
        [after(down_half, turned)[step] for step in range(ring)], "fsdp", ring
    )
    turned, returned, down_arrived = lax.optimization_barrier(
        (muon(small_mine, small_gram, plane == 1), returned, down_arrived)
    )
    small_returned = from_planes(turned.reshape(small_slots.shape))
    block_out = (middle + add_all(down_half[0], down_arrived)).astype(BF16).reshape(inputs.shape)
    ortho = (
        small_returned[0],
        small_returned[1][:, :KV_WIDTH],
        small_returned[1][:, KV_WIDTH:],
        small_returned[2],
        *returned[:3],
    )
    new_weights = tuple(
        master * (1.0 - LR_MUON * DECAY_MUON)
        - LR_MUON * math.sqrt(side) * (rows_now.T if turn else rows_now).astype(F32)
        for master, rows_now, turn, side in zip(masters, ortho, sideways, full_sides)
    )

    first_new = BETA_ONE * gain_first + (1.0 - BETA_ONE) * gain_grad
    second_new = BETA_TWO * gain_second + (1.0 - BETA_TWO) * gain_grad * gain_grad
    corr_one = 1.0 - BETA_ONE**ADAM_STEP
    corr_two = 1.0 - BETA_TWO**ADAM_STEP
    gains_new = norm_gains - LR_GAIN * (first_new / corr_one) / (
        jnp.sqrt(second_new / corr_two) + EPS_ADAM
    )
    return (
        block_out,
        input_grad,
        *(new[0] for new in small + big),
        *(new[1] for new in small + big),
        *new_weights,
        first_new,
        second_new,
        gains_new,
    )


def solution(mesh):
    dp_size, fsdp_size = mesh.devices.shape
    fine_mesh = Mesh(
        mesh.devices.reshape(PLANES, dp_size // (PLANES * CORES), CORES, fsdp_size),
        ("z", "y", "core", "fsdp"),
    )
    dp = ("z", "y", "core")
    tokens = P(dp, "fsdp", None)
    by_row = P(EVERYWHERE, None)
    by_col = P(None, EVERYWHERE)
    matrices = (by_col, by_row, by_row, by_row, by_col, by_col, by_row)
    return jax.shard_map(
        per_device,
        mesh=fine_mesh,
        in_specs=(tokens, tokens, P(dp, None), *matrices, *matrices, P(), P(), P()),
        out_specs=(tokens, tokens, *matrices, *matrices, *matrices, P(), P(), P()),
        check_vma=False,
    )
```
